128 devices in a mesh: group: 8 (over z, core), member: 16 (over x, y).
Axes of the slice: x: 4, y: 4, z: 4, core: 2. Of those that a mesh axis runs over, the one named last changes fastest.
Arguments:
- dense_in: float32 [16384, 13], P(('group', 'member')), may hold values from -6 to 6
- lookup_owner: int32 [16384, 8, 8], P(('group', 'member')), may hold values from 0 to 127, as said below
- lookup_row: int32 [16384, 8, 8], P(('group', 'member')), may hold values from 0 to 8191
- bag_length: int32 [16384, 8], P(('group', 'member')), may hold values from 1 to 8
- logit_grad: float32 [16384], P(('group', 'member')), may hold values from -6 to 6
- table: float32 [1048576, 128], P(('group', 'member')), may hold values from -1.2 to 1.2
- parity: float32 [65536, 256], P(('group', 'member')), may hold values from -3 to 3
- w_bottom0: float32 [13, 512], replicated, may hold values from -1.75 to 1.75
- w_bottom1: float32 [512, 256], replicated, may hold values from -0.25 to 0.25
- w_bottom2: float32 [256, 128], replicated, may hold values from -0.375 to 0.375
- w_top0: float32 [164, 1024], replicated, may hold values from -0.5 to 0.5
- w_top1: float32 [1024], replicated, may hold values from -0.1875 to 0.1875
Outputs:
- new_table: float32 [1048576, 128], P(('group', 'member'))
- new_parity: float32 [65536, 256], P(('group', 'member'))
- grad_bottom0: float32 [13, 512], replicated
- grad_bottom1: float32 [512, 256], replicated
- grad_bottom2: float32 [256, 128], replicated
- grad_top0: float32 [164, 1024], replicated
- grad_top1: float32 [1024], replicated
The draws below stay inside these ranges and needn't reach their ends.
Inputs may be any that keep to these rules, and one draw needn't show every extreme that they name: `lookup_owner`: among the 8192 bag slots of one device's samples at most 97 name rows of any one device, and one device is named by exactly 97 slots of every device. `bag_length`: slots at or beyond a bag's length are padding; their owner and row are still in range.
All inputs are finite; a program needn't handle non-finite values.
Results may differ from the reference program's by a relative error of at most 0.005.
Values may be sent and summed in bfloat16 or wider, within the bound.
A program may use at most 128 MiB of HBM per device.

```python
import jax
import jax.numpy as jnp
import numpy as np
from jax import lax

E = 128
DENSE = 13
BOT1 = 512
BOT2 = 256
TOPH = 1024
NT = 8
HOT = 8
B_DEV = 128
ROWS_DEV = 8192
SHARDS = 128
SAMPLES = 16384
ROWS = 1048576
CAP = 97
TOPIN = 164
N_GROUP = 8
N_MEMBER = 16


def draw_lookup_owner(key, part):
    key = jax.random.fold_in(key, 11)
    lookups = B_DEV * NT * HOT
    others = SHARDS - 1
    remain = lookups - CAP
    busy_key, tilt_key, order_key, shuffle_key = jax.random.split(key, 4)
    busiest = jax.random.randint(busy_key, (), 0, SHARDS, dtype=jnp.int32)
    tilts = jax.random.randint(tilt_key, (SHARDS,), 0, 3, dtype=jnp.int32)
    order_keys = jax.random.split(order_key, SHARDS)
    shuffle_keys = jax.random.split(shuffle_key, SHARDS)
    ranks = jnp.arange(others, dtype=jnp.int32)

    def one_source(tilt_value, order_one, shuffle_one):
        weights = others + tilt_value * ranks
        total = jnp.sum(weights)
        counts = remain * weights // total
        leftover = remain - jnp.sum(counts)
        counts = counts + (ranks < leftover).astype(jnp.int32)
        bounds = jnp.cumsum(counts).astype(jnp.int32)[:-1]
        position = jnp.arange(remain, dtype=jnp.int32)
        which = jnp.searchsorted(bounds, position, side='right').astype(jnp.int32)
        shuffled = jax.random.permutation(order_one, others).astype(jnp.int32)
        shuffled = shuffled + (shuffled >= busiest).astype(jnp.int32)
        owners = jnp.concatenate([jnp.full((CAP,), busiest, dtype=jnp.int32), shuffled[which]])
        return jax.random.permutation(shuffle_one, owners)
    drawn = jax.vmap(one_source)(tilts, order_keys, shuffle_keys)
    return drawn.reshape(SAMPLES, NT, HOT).astype(jnp.int32)


def plant(values, key, least, largest):
    index_at = [jax.random.randint(jax.random.fold_in(key, axis), (), 0, length) for axis, length in enumerate(values.shape)]
    main_axis = values.shape.index(max(values.shape))
    beside = index_at[:main_axis] + [(index_at[main_axis] + 1) % values.shape[main_axis]] + index_at[main_axis + 1:]
    return values.at[tuple(index_at)].set(least).at[tuple(beside)].set(largest)


def steps_of(key, extent, cuts, smallest, top_value):
    loudness, own = 1.0, jax.random.fold_in(key, 6)
    for axis_at, blocks in cuts:
        draws = jnp.exp(jax.random.uniform(jax.random.fold_in(own, axis_at), (blocks,), jnp.float32, smallest / len(cuts), top_value / len(cuts)))
        loudness = loudness * jnp.repeat(draws, extent[axis_at] // blocks).reshape([-1 if axis == axis_at else 1 for axis in range(len(extent))])
    return loudness


def normal_values(stream_key, dims, spread, bound, cuts=(), kind=jnp.bfloat16):
    values = jax.random.normal(stream_key, dims, jnp.float32) * spread
    if len(cuts) > 0:
        values = steps_of(stream_key, dims, cuts, -0.22, 0.18) * values
    return jnp.clip(values, min=-bound, max=bound).astype(kind)


def setup_inputs(seed: int = 0) -> dict:
    key_list = jax.random.split(jax.random.key(seed), 13)
    dense_in = normal_values(key_list[0], (SAMPLES, DENSE), 1.0, 6.0, ((0, 128),), jnp.float32)
    lookup_owner = draw_lookup_owner(jax.random.fold_in(key_list[12], 71), 0)
    lookup_row = plant(jax.random.randint(key_list[2], (SAMPLES, NT, HOT), 0, ROWS_DEV), jax.random.fold_in(key_list[2], 1), 0, ROWS_DEV - 1).astype(jnp.int32)
    bag_length = plant(jax.random.randint(key_list[3], (SAMPLES, NT), 1, HOT + 1), jax.random.fold_in(key_list[3], 1), 1, HOT).astype(jnp.int32)
    logit_grad = normal_values(key_list[4], (SAMPLES,), 1.0, 6.0, ((0, 128),), jnp.float32)
    table = normal_values(key_list[5], (ROWS, E), 0.2, 1.2, ((0, 128),), jnp.float32)
    parity = normal_values(key_list[6], (N_GROUP * ROWS_DEV, 2 * E), 0.5, 3.0, ((0, 128),), jnp.float32)
    w_bottom0 = normal_values(key_list[7], (DENSE, BOT1), DENSE ** -0.5, 1.75, (), jnp.float32)
    w_bottom1 = normal_values(key_list[8], (BOT1, BOT2), BOT1 ** -0.5, 0.25, (), jnp.float32)
    w_bottom2 = normal_values(key_list[9], (BOT2, E), BOT2 ** -0.5, 0.375, (), jnp.float32)
    w_top0 = normal_values(key_list[10], (TOPIN, TOPH), TOPIN ** -0.5, 0.5, (), jnp.float32)
    w_top1 = normal_values(key_list[11], (TOPH,), TOPH ** -0.5, 0.1875, (), jnp.float32)
    return dict(dense_in=dense_in, lookup_owner=lookup_owner, lookup_row=lookup_row, bag_length=bag_length, logit_grad=logit_grad, table=table, parity=parity, w_bottom0=w_bottom0, w_bottom1=w_bottom1, w_bottom2=w_bottom2, w_top0=w_top0, w_top1=w_top1)


embed_rate = 1.0

def network(w_bottom0, w_bottom1, w_bottom2, w_top0, w_top1, pooled, dense_in):
    highest = lax.Precision.HIGHEST
    hidden_one = jax.nn.silu(jnp.dot(dense_in, w_bottom0, precision=highest))
    hidden_two = jax.nn.silu(jnp.dot(hidden_one, w_bottom1, precision=highest))
    bottom = jax.nn.silu(jnp.dot(hidden_two, w_bottom2, precision=highest))
    stacked = jnp.concatenate([bottom[:, None, :], pooled], axis=1)
    gram_dots = jnp.einsum('sie,sje->sij', stacked, stacked, precision=highest)
    lower_rows, lower_cols = np.tril_indices(stacked.shape[1], -1)
    pair_dots = gram_dots[:, lower_rows, lower_cols]
    top_in = jnp.concatenate([bottom, pair_dots], axis=1)
    hidden = jax.nn.silu(jnp.dot(top_in, w_top0, precision=highest))
    return jnp.dot(hidden, w_top1, precision=highest)

def reference(dense_in, lookup_owner, lookup_row, bag_length, logit_grad, table, parity, w_bottom0, w_bottom1, w_bottom2, w_top0, w_top1):
    highest = lax.Precision.HIGHEST
    flat_index = (lookup_owner * ROWS_DEV + lookup_row).astype(jnp.int32)
    live_mask = (jnp.arange(HOT, dtype=jnp.int32)[None, None, :] < bag_length[:, :, None]).astype(jnp.float32)
    pooled_list = []
    for table_index in range(NT):
        fetched = table[flat_index[:, table_index, :]].astype(jnp.bfloat16)
        fetched = lax.optimization_barrier(fetched).astype(jnp.float32)
        pooled_list.append(lax.optimization_barrier(jnp.sum(fetched * live_mask[:, table_index, :, None], axis=1)))
    pooled = jnp.stack(pooled_list, axis=1)

    def forward(first_w, second_w, third_w, top_first, top_second, pooled_in):
        return network(first_w, second_w, third_w, top_first, top_second, pooled_in, dense_in)
    logits, pullback = jax.vjp(forward, w_bottom0, w_bottom1, w_bottom2, w_top0, w_top1, pooled)
    gradients = pullback(logit_grad)
    pooled_grad = gradients[5].astype(jnp.bfloat16)
    pooled_grad = lax.optimization_barrier(pooled_grad).astype(jnp.float32)
    row_grad = jnp.zeros(table.shape, jnp.float32)
    for table_index in range(NT):
        updates = pooled_grad[:, table_index, None, :] * live_mask[:, table_index, :, None]
        row_grad = row_grad.at[flat_index[:, table_index, :].reshape(-1)].add(updates.reshape(-1, table.shape[1]))
    new_table = table - embed_rate * row_grad
    change = (-embed_rate * row_grad).reshape(N_GROUP, N_MEMBER, ROWS_DEV, table.shape[1])
    parity_index = jnp.arange(2, dtype=jnp.float32)
    member_index = jnp.arange(N_MEMBER, dtype=jnp.float32)
    coeffs = 1.0 / (1.0 + parity_index[:, None] + member_index[None, :] / N_MEMBER)
    update = jnp.einsum('gmre,km->grke', change, coeffs, precision=highest)
    new_parity = parity + update.reshape(N_GROUP * ROWS_DEV, 2 * table.shape[1])
    return (new_table, new_parity, gradients[0], gradients[1], gradients[2], gradients[3], gradients[4])
```

```python
import functools

import jax
import jax.numpy as jnp
import numpy as np
from jax import lax
from jax.experimental import pallas as pl
from jax.experimental.pallas import tpu as pltpu
from jax.sharding import PartitionSpec as P

embed_rate = 1.0

MESH = pl.DeviceIdType.MESH
N_DEV = 128
N_GROUP = 8
N_MEMBER = 16
E = 128
ROWS_DEV = 8192
NT = 8
HOT = 8
BAGS = 1024
MAIN = 96
GROUP = 8
PAIRS = [(i, j) for i in range(9) for j in range(i)]
BOT1, BOT2, TOPH, DENSE, TOPIN = 512, 256, 1024, 13, 164

TOP0_ROWS = 176
OFF_TOP0 = 0
OFF_BOT1 = 8 * TOP0_ROWS
OFF_BOT2 = OFF_BOT1 + 2 * BOT1
OFF_BOT0 = OFF_BOT2 + BOT2
OFF_TOP1 = OFF_BOT0 + 4 * 16
FLAT = 3072
PIECE = FLAT // N_GROUP
SMALL = PIECE // N_MEMBER

f32, bf16, i32 = jnp.float32, jnp.bfloat16, jnp.int32
VM = pltpu.VMEM


def iota(shape, dim):
    return lax.broadcasted_iota(i32, shape, dim)


def dot(a, b, dims):
    return lax.dot_general(a, b, (dims, ((), ())), preferred_element_type=f32)


NN = ((1,), (0,))
NT_ = ((1,), (1,))
TN = ((0,), (0,))


def halves(a):
    hi = a.astype(bf16)
    return hi, (a - hi.astype(f32)).astype(bf16)


def dot3(a, b, dims):
    return dot(a[0], b[0], dims) + (dot(a[0], b[1], dims) + dot(a[1], b[0], dims))


def coords():
    g, m = lax.axis_index("group"), lax.axis_index("member")
    return g // 2, g % 2, m // 4, m % 4


def peer(k):
    z, c, x, y = coords()
    kx = k % 4
    ky = (k // 4 + kx) % 4
    kz = (k // 16 + ky) % 4
    kc = k // 64
    return ((z + kz) % 4) * 2 + (c + kc) % 2, ((x + kx) % 4) * 4 + (y + ky) % 4


def origin(k):
    z, c, x, y = coords()
    kx = k % 4
    ky = (k // 4 + kx) % 4
    kz = (k // 16 + ky) % 4
    kc = k // 64
    return ((z + 4 - kz) % 4) * 2 + (c + 2 - kc) % 2, ((x + 4 - kx) % 4) * 4 + (y + 4 - ky) % 4


def sigmoid(v):
    return 1.0 / (1.0 + jnp.exp(-v))


def exchange_kernel(
    own_ref, row_ref, len_ref, x_ref, lg_ref, table_hbm, w0_ref, w1_ref, w2_ref, wt0_ref, wt1_ref,
    ids_out, gmain_out, gextra_out, flat_out,
    table_v, ids_send, ids_recv, ids_smem, stage, send_main, send_extra, recv_main, recv_extra,
    bag_of, bag_extra, st, pooled, pg, wt0_p, top_in, hid, dup,
    table_sem, smem_sem, ids_ssem, ids_rsem, row_ssem, row_esem, rowm_rsem, rowe_rsem,
    g_ssem, g_esem, gm_rsem, ge_rsem,
):
    g, m = lax.axis_index("group"), lax.axis_index("member")
    me = g * N_MEMBER + m

    table_copy = pltpu.make_async_copy(table_hbm, table_v, table_sem)
    table_copy.start()
    barrier = pltpu.get_barrier_semaphore()

    def greet(k, c):
        pl.semaphore_signal(barrier, 1, device_id=peer(k), device_id_type=MESH)
        return c

    lax.fori_loop(1, N_DEV, greet, 0)

    upper = (iota((256, 384), 0) < iota((256, 384), 1)).astype(bf16)
    dev_of = iota((128, 256), 0)
    lane = iota((1, 128), 1)

    def place(j, carry):
        count, acc = carry
        t = j // 4
        h = (2 * j) % 8
        length = len_ref[pl.ds(t, 1), :]
        own = jnp.concatenate([own_ref[pl.ds(2 * j, 1), :], own_ref[pl.ds(2 * j + 1, 1), :]], axis=1)
        row = jnp.concatenate([row_ref[pl.ds(2 * j, 1), :], row_ref[pl.ds(2 * j + 1, 1), :]], axis=1)
        own = jnp.where(jnp.concatenate([h < length, h + 1 < length], axis=1), own, -1)
        hit = own == dev_of
        hit_f = hit.astype(f32)
        hit_b = hit_f.astype(bf16)
        ranks = dot(hit_b, upper, NN)
        before = ranks[:, 0:256] + jnp.concatenate([count, count], axis=1)
        pos = jnp.sum(before * hit_f, axis=0, keepdims=True).astype(i32)
        at = (pos == dev_of).astype(f32)
        bag_lo = jnp.concatenate([lane, lane], axis=1).astype(f32)
        vals = jnp.concatenate(
            [
                at * (row // 128).astype(f32),
                at * (row % 128).astype(f32),
                at * (t + 1).astype(f32),
                at * bag_lo,
            ],
            axis=0,
        ).astype(bf16)
        return count + ranks[:, 256:384], acc + dot(vals, hit_b, NT_)

    count, acc = lax.fori_loop(
        0, 32, place, (jnp.zeros((128, 128), f32), jnp.zeros((512, 128), f32)), unroll=2
    )
    ids = (acc[0:128] * 128.0 + acc[128:256]).T
    ids = jnp.where(iota((128, 128), 1) == 127, count, ids).astype(i32)
    for d in range(N_DEV):
        ids_send[d] = ids[d : d + 1, :]
    bag = acc[256:384] * 128.0 + acc[384:512] - 128.0
    pl.semaphore_wait(barrier, N_DEV - 1)

    def ids_copy(k):
        to_g, to_m = peer(k)
        return pltpu.make_async_remote_copy(
            ids_send.at[to_g * N_MEMBER + to_m], ids_recv.at[me], ids_ssem, ids_rsem,
            device_id=(to_g, to_m), device_id_type=MESH,
        )

    def send_ids(k, c):
        ids_copy(k).start()
        return c

    lax.fori_loop(1, N_DEV, send_ids, 0)
    ids_recv[me] = ids_send[me]

    bag_i = bag.astype(i32)
    for d in range(N_DEV):
        bag_of[d] = jnp.broadcast_to(bag_i[0:MAIN, d : d + 1], (MAIN, 128))
    bag_t = bag.T.astype(i32)
    bag_extra[...] = jnp.broadcast_to(bag_t[:, MAIN : MAIN + 1], (128, 128))
    wait_ids = pltpu.make_async_copy(ids_send.at[pl.ds(0, 127)], ids_recv.at[pl.ds(0, 127)], ids_rsem)
    wait_ids.wait()
    ids_recv[...] = jnp.clip(ids_recv[...], 0, ROWS_DEV - 1)
    smem_copy = pltpu.make_async_copy(ids_recv, ids_smem, smem_sem)
    smem_copy.start()
    smem_copy.wait()
    table_copy.wait()

    def gather(d, slot):
        for i in range(MAIN):
            stage[i : i + 1, :] = table_v[pl.ds(ids_smem[d, 0, i] & (ROWS_DEV - 1), 1), :]
        send_main[slot] = stage[...].astype(bf16)
        send_extra[slot] = table_v[pl.ds(ids_smem[d, 0, MAIN] & (ROWS_DEV - 1), 1), :]

    def rows_copies(k):
        to = peer(k)
        return (
            pltpu.make_async_remote_copy(
                send_main.at[k], recv_main.at[k], row_ssem, rowm_rsem.at[k // GROUP],
                device_id=to, device_id_type=MESH,
            ),
            pltpu.make_async_remote_copy(
                send_extra.at[k], recv_extra.at[k], row_esem, rowe_rsem,
                device_id=to, device_id_type=MESH,
            ),
        )

    def serve(k, c):
        to_g, to_m = peer(k)
        gather(to_g * N_MEMBER + to_m, k)
        for copy in rows_copies(k):
            copy.start()
        return c

    lax.fori_loop(1, N_DEV, serve, 0)
    gather(me, 0)
    recv_main[0] = send_main[0]
    recv_extra[0] = send_extra[0]

    top_in[...] = jnp.zeros_like(top_in)
    top_in[0:DENSE, :] = x_ref[...]
    x_pad = top_in[0:128, :]
    x_h = halves(x_pad)
    w0_t = jnp.concatenate([w0_ref[...], jnp.zeros((128 - DENSE, BOT1), f32)], axis=0).T
    w0_th = halves(w0_t)
    h1p = dot3(w0_th, x_h, NN)
    s1 = sigmoid(h1p)
    h1_h = halves(h1p * s1)
    d1 = s1 * (1.0 + h1p * (1.0 - s1))
    w1_h = halves(w1_ref[...])
    w1_th = halves(w1_ref[...].T)
    h2p = dot3(w1_th, h1_h, NN)
    s2 = sigmoid(h2p)
    h2_h = halves(h2p * s2)
    d2 = s2 * (1.0 + h2p * (1.0 - s2))
    w2_h = halves(w2_ref[...])
    w2_th = halves(w2_ref[...].T)
    bp = dot3(w2_th, h2_h, NN)
    s3 = sigmoid(bp)
    bottom = bp * s3
    d3 = s3 * (1.0 + bp * (1.0 - s3))
    top_in[0:128, :] = bottom
    wt0_p[...] = jnp.zeros_like(wt0_p)
    wt0_p[0:TOPIN, :] = wt0_ref[...]
    wt0_h = halves(wt0_p[...])
    wt0_th = halves(wt0_p[...].T)

    def one_hot(bags):
        return jnp.concatenate(
            [(bags == iota((1, 128), 1) + 128 * t).astype(f32).astype(bf16) for t in range(NT)], axis=1
        )

    def pool_main(q):
        for i in range(GROUP):
            from_g, from_m = origin(q * GROUP + i)
            st[pl.ds(i * MAIN, MAIN), :] = one_hot(bag_of[from_g * N_MEMBER + from_m])
        rows = recv_main[pl.ds(q * GROUP, GROUP)].reshape(GROUP * MAIN, E)
        pooled[...] += dot(rows, st[...], TN)

    def wait_rows(q, count):
        pltpu.make_async_copy(
            send_main.at[pl.ds(0, count)], recv_main.at[pl.ds(0, count)], rowm_rsem.at[q]
        ).wait()

    pooled[...] = jnp.zeros_like(pooled)
    wait_rows(0, GROUP - 1)
    pool_main(0)

    def pool_step(q, c):
        wait_rows(q, GROUP)
        pool_main(q)
        return c

    lax.fori_loop(1, N_DEV // GROUP, pool_step, 0)
    pltpu.make_async_copy(
        send_extra.at[pl.ds(0, 127)], recv_extra.at[pl.ds(0, 127)], rowe_rsem
    ).wait()
    for k in range(N_DEV):
        from_g, from_m = origin(k)
        hid[pl.ds(from_g * N_MEMBER + from_m, 1), :] = recv_extra[k]
    pooled[...] += dot(hid[0:128, :].astype(bf16), one_hot(bag_extra[...]), TN)

    z = [bottom] + [pooled[:, 128 * t : 128 * (t + 1)] for t in range(NT)]
    for n, (i, j) in enumerate(PAIRS):
        top_in[128 + n : 129 + n, :] = jnp.sum(z[i] * z[j], axis=0, keepdims=True)
    top_h = halves(top_in[...])
    up = dot3(wt0_th, top_h, NN)
    su = sigmoid(up)
    hid[...] = up * su
    lg = lg_ref[...]
    wt1_col = jnp.broadcast_to(wt1_ref[...], (128, TOPH)).T
    dup[...] = wt1_col * lg * (su * (1.0 + up * (1.0 - su)))
    dup_h = halves(dup[...])
    d_top = dot3(wt0_h, dup_h, NN)
    d_pair = {}
    for n, (i, j) in enumerate(PAIRS):
        d_pair[i, j] = d_pair[j, i] = d_top[128 + n : 129 + n, :]
    d_z = []
    for i in range(9):
        total = None
        for j in range(9):
            if j != i:
                term = d_pair[i, j] * z[j]
                total = term if total is None else total + term
        d_z.append(total)
        if i > 0:
            pg[128 * (i - 1) : 128 * i, :] = total.T.astype(bf16)

    pltpu.make_async_copy(send_main.at[pl.ds(0, 127)], recv_main.at[pl.ds(0, 127)], row_ssem).wait()
    pltpu.make_async_copy(send_extra.at[pl.ds(0, 127)], recv_extra.at[pl.ds(0, 127)], row_esem).wait()

    extra = dot(one_hot(bag_extra[...]), pg[...], NN)
    for d in range(N_DEV):
        send_extra[d] = extra[d : d + 1, :]

    def grad_copies(k):
        to_g, to_m = peer(k)
        return (
            pltpu.make_async_remote_copy(
                send_main.at[k], gmain_out.at[me], g_ssem, gm_rsem,
                device_id=(to_g, to_m), device_id_type=MESH,
            ),
            pltpu.make_async_remote_copy(
                send_extra.at[to_g * N_MEMBER + to_m], gextra_out.at[me], g_esem, ge_rsem,
                device_id=(to_g, to_m), device_id_type=MESH,
            ),
        )

    def expand(q):
        for i in range(GROUP):
            to_g, to_m = peer(q * GROUP + i)
            st[pl.ds(i * MAIN, MAIN), :] = one_hot(bag_of[to_g * N_MEMBER + to_m])
        grads = dot(st[...], pg[...], NN).astype(bf16)
        send_main[pl.ds(q * GROUP, GROUP)] = grads.reshape(GROUP, MAIN, E)

    def start_grads(k, c):
        for copy in grad_copies(k):
            copy.start()
        return c

    expand(0)
    lax.fori_loop(1, GROUP, start_grads, 0)

    def expand_step(q, c):
        expand(q)
        lax.fori_loop(q * GROUP, q * GROUP + GROUP, start_grads, 0)
        return c

    lax.fori_loop(1, N_DEV // GROUP, expand_step, 0)
    gmain_out[me] = send_main[0]
    gextra_out[me] = send_extra[me]
    ids_out[...] = ids_recv[...]

    flat_out[...] = jnp.zeros_like(flat_out)
    g_t0 = dot3(top_h, dup_h, NT_).astype(bf16)
    for c in range(8):
        flat_out[OFF_TOP0 + c * TOP0_ROWS : OFF_TOP0 + (c + 1) * TOP0_ROWS, :] = g_t0[
            0:TOP0_ROWS, 128 * c : 128 * (c + 1)
        ]
    lg_h = halves(jnp.broadcast_to(lg, (8, 128)))
    g_t1 = dot3(lg_h, halves(hid[...]), NT_)[0:1]
    g_t1 = jnp.concatenate([g_t1[:, 128 * c : 128 * (c + 1)] for c in range(8)], axis=0)
    flat_out[OFF_TOP1 : OFF_TOP1 + 16, :] = jnp.concatenate([g_t1, g_t1], axis=0).astype(bf16)
    d_bp = halves((d_top[0:128] + d_z[0]) * d3)
    flat_out[OFF_BOT2 : OFF_BOT2 + BOT2, :] = dot3(h2_h, d_bp, NT_).astype(bf16)
    d_h2p = halves(dot3(w2_h, d_bp, NN) * d2)
    g_b1 = dot3(h1_h, d_h2p, NT_).astype(bf16)
    for c in range(2):
        flat_out[OFF_BOT1 + c * BOT1 : OFF_BOT1 + (c + 1) * BOT1, :] = g_b1[:, 128 * c : 128 * (c + 1)]
    d_h1p = halves(dot3(w1_h, d_h2p, NN) * d1)
    g_b0 = dot3(x_h, d_h1p, NT_)[0:16].astype(bf16)
    for c in range(4):
        flat_out[OFF_BOT0 + c * 16 : OFF_BOT0 + (c + 1) * 16, :] = g_b0[:, 128 * c : 128 * (c + 1)]

    pltpu.make_async_copy(ids_send.at[pl.ds(0, 127)], ids_recv.at[pl.ds(0, 127)], ids_ssem).wait()
    pltpu.make_async_copy(send_main.at[pl.ds(0, 127)], recv_main.at[pl.ds(0, 127)], g_ssem).wait()
    pltpu.make_async_copy(send_extra.at[pl.ds(0, 127)], recv_extra.at[pl.ds(0, 127)], g_esem).wait()
    pltpu.make_async_copy(send_main.at[pl.ds(0, 127)], gmain_out.at[pl.ds(0, 127)], gm_rsem).wait()
    pltpu.make_async_copy(send_extra.at[pl.ds(0, 127)], gextra_out.at[pl.ds(0, 127)], ge_rsem).wait()


WAYS = 4


def scatter_kernel(ids_ref, gmain_ref, gextra_ref, table_ref, new_ref, change_ref, sums, stage):
    sums[...] = jnp.zeros_like(sums)

    def source(s, c):
        stage[0:MAIN, :] = gmain_ref[s].astype(f32)
        stage[MAIN : MAIN + 1, :] = gextra_ref[s]
        count = ids_ref[s, 0, 127]

        def batch(b, c):
            first = b * 8
            for half in range(0, 8, WAYS):
                rows, total = [], []
                for i in range(WAYS):
                    r = ids_ref[s, 0, first + half + i]
                    rows.append(r)
                    total.append(
                        sums[i, pl.ds(r, 1), :] + stage[pl.ds(first + half + i, 1), :]
                    )
                for i in range(WAYS):
                    sums[i, pl.ds(rows[i], 1), :] = total[i]
            return c

        lax.fori_loop(0, (count + 7) // 8, batch, 0)
        return c

    stage[...] = jnp.zeros_like(stage)
    lax.fori_loop(0, N_DEV, source, 0)

    def finish(b, c):
        at = pl.ds(pl.multiple_of(b * 256, 256), 256)
        total = sums[0, at, :]
        for i in range(1, WAYS):
            total = total + sums[i, at, :]
        total = -embed_rate * total
        new_ref[at, :] = table_ref[at, :] + total
        change_ref[at, :] = total.astype(bf16)
        return c

    lax.fori_loop(0, ROWS_DEV // 256, finish, 0)


def member_peer(k, sign):
    x, y = lax.axis_index("member") // 4, lax.axis_index("member") % 4
    kx = k % 4
    ky = (k // 4 + kx) % 4
    if sign < 0:
        kx, ky = (4 - kx) % 4, (4 - ky) % 4
    return ((x + kx) % 4) * 4 + (y + ky) % 4


def parity_kernel(
    change_ref, parity_ref, flat_ref,
    new_ref, g0_ref, g1_ref, g2_ref, gt0_ref, gt1_ref,
    pieces, part_z, sum_z, part_xy, sum_xy, all_xy, all_z_send, all_z,
    ch_ssem, ch_rsem, rz_ssem, rz_rsem, rx_ssem, rx_rsem, ax_ssem, ax_rsem, az_ssem, az_rsem,
):
    g, m = lax.axis_index("group"), lax.axis_index("member")
    barrier = pltpu.get_barrier_semaphore()
    for j in range(1, N_GROUP):
        pl.semaphore_signal(barrier, 1, device_id=((g + j) % N_GROUP, m), device_id_type=MESH)
    for k in range(1, N_MEMBER):
        pl.semaphore_signal(barrier, 1, device_id=(g, member_peer(k, 1)), device_id_type=MESH)
    pl.semaphore_wait(barrier, N_GROUP - 1 + N_MEMBER - 1)

    def remote(src, dst, ssem, rsem, to):
        return pltpu.make_async_remote_copy(src, dst, ssem, rsem, device_id=to, device_id_type=MESH)

    rows = ROWS_DEV // N_MEMBER

    def change_copy(k):
        to = member_peer(k, 1)
        return remote(
            change_ref.at[pl.ds(pl.multiple_of(to * rows, rows), rows)], pieces.at[k], ch_ssem.at[k], ch_rsem.at[k],
            (g, to),
        )

    def rz_copy(j):
        to = (g + j) % N_GROUP
        return remote(
            flat_ref.at[pl.ds(pl.multiple_of(to * PIECE, PIECE), PIECE)], part_z.at[j], rz_ssem.at[j], rz_rsem.at[j],
            (to, m),
        )

    def rx_copy(k):
        to = member_peer(k, 1)
        return remote(
            sum_z.at[pl.ds(pl.multiple_of(to * SMALL, SMALL), SMALL)], part_xy.at[k], rx_ssem.at[k], rx_rsem.at[k],
            (g, to),
        )

    def ax_copy(k):
        return remote(sum_xy, all_xy.at[m], ax_ssem.at[k], ax_rsem.at[k], (g, member_peer(k, 1)))

    def az_copy(j):
        return remote(all_z_send, all_z.at[g], az_ssem.at[j], az_rsem.at[j], ((g + j) % N_GROUP, m))

    for j in range(1, N_GROUP):
        rz_copy(j).start()
    for k in range(1, 6):
        change_copy(k).start()
    total = flat_ref[pl.ds(pl.multiple_of(g * PIECE, PIECE), PIECE), :].astype(f32)
    for j in range(1, N_GROUP):
        rz_copy(j).wait()
        total = total + part_z[j].astype(f32)
    sum_z[...] = total
    for k in range(1, N_MEMBER):
        rx_copy(k).start()
    for k in range(6, 11):
        change_copy(k).start()
    total = sum_z[pl.ds(pl.multiple_of(m * SMALL, SMALL), SMALL), :]
    for k in range(1, N_MEMBER):
        rx_copy(k).wait()
        total = total + part_xy[k]
    sum_xy[...] = total
    for k in range(1, N_MEMBER):
        ax_copy(k).start()
    for k in range(11, N_MEMBER):
        change_copy(k).start()
    all_xy[m] = total
    for k in range(1, N_MEMBER):
        ax_copy(k).wait()
    all_z_send[...] = all_xy[...].reshape(PIECE, E).astype(bf16)
    for j in range(1, N_GROUP):
        az_copy(j).start()

    def weights(k):
        source = member_peer(k, -1).astype(f32) / N_MEMBER
        one = jnp.ones((1, 128), f32)
        return 1.0 / (one + source), 1.0 / (one * 2.0 + source)

    for k in range(1, N_MEMBER):
        change_copy(k).wait()
    coef = [weights(k) for k in range(N_MEMBER)]
    own_at = m * rows

    def combine(b, c):
        at = pl.ds(pl.multiple_of(b * 32, 32), 32)
        part = change_ref[pl.ds(pl.multiple_of(own_at + b * 32, 32), 32), :].astype(f32)
        first, second = coef[0][0] * part, coef[0][1] * part
        for k in range(1, N_MEMBER):
            part = pieces[k, at, :].astype(f32)
            first = first + coef[k][0] * part
            second = second + coef[k][1] * part
        new_ref[at, 0:128] = parity_ref[at, 0:128] + first
        new_ref[at, 128:256] = parity_ref[at, 128:256] + second
        return c

    lax.fori_loop(0, rows // 32, combine, 0)

    all_z[g] = all_z_send[...]
    for j in range(1, N_GROUP):
        az_copy(j).wait()
    for c in range(8):
        gt0_ref[:, 128 * c : 128 * (c + 1)] = piece_rows(all_z, OFF_TOP0 + c * TOP0_ROWS, TOP0_ROWS)[0:TOPIN]
    for c in range(2):
        g1_ref[:, 128 * c : 128 * (c + 1)] = piece_rows(all_z, OFF_BOT1 + c * BOT1, BOT1)
    g2_ref[...] = piece_rows(all_z, OFF_BOT2, BOT2)
    for c in range(4):
        g0_ref[:, 128 * c : 128 * (c + 1)] = piece_rows(all_z, OFF_BOT0 + c * 16, 16)[0:DENSE]
    top1 = piece_rows(all_z, OFF_TOP1, 16)
    for c in range(8):
        gt1_ref[:, 128 * c : 128 * (c + 1)] = top1[c : c + 1, :]


def piece_rows(ref, start, count):
    out = []
    while count > 0:
        p, at = start // PIECE, start % PIECE
        n = min(count, PIECE - at)
        out.append(ref[p, at : at + n, :].astype(f32))
        start, count = start + n, count - n
    return out[0] if len(out) == 1 else jnp.concatenate(out, axis=0)


def body(
    dense_in, lookup_owner, lookup_row, bag_length, logit_grad, table, parity,
    w_bottom0, w_bottom1, w_bottom2, w_top0, w_top1,
):
    owner = lookup_owner.transpose(1, 2, 0).reshape(NT * HOT, 128)
    row = lookup_row.transpose(1, 2, 0).reshape(NT * HOT, 128)
    vmem = pl.BlockSpec(memory_space=VM)
    anyw = pl.BlockSpec(memory_space=pl.ANY)
    smem = pl.BlockSpec(memory_space=pltpu.SMEM)
    dma = pltpu.SemaphoreType.DMA
    sds = jax.ShapeDtypeStruct
    ids, gmain, gextra, flat = pl.pallas_call(
        exchange_kernel,
        out_shape=(
            sds((N_DEV, 1, 128), i32),
            sds((N_DEV, MAIN, E), bf16),
            sds((N_DEV, 1, E), f32),
            sds((FLAT, E), bf16),
        ),
        in_specs=[vmem] * 5 + [anyw] + [vmem] * 5,
        out_specs=(vmem,) * 4,
        scratch_shapes=[
            VM((ROWS_DEV, E), f32),
            VM((N_DEV, 1, 128), i32),
            VM((N_DEV, 1, 128), i32),
            pltpu.SMEM((N_DEV, 1, 128), i32),
            VM((MAIN, E), f32),
            VM((N_DEV, MAIN, E), bf16),
            VM((N_DEV, 1, E), f32),
            VM((N_DEV, MAIN, E), bf16),
            VM((N_DEV, 1, E), f32),
            VM((N_DEV, MAIN, 128), i32),
            VM((128, 128), i32),
            VM((GROUP * MAIN, BAGS), bf16),
            VM((E, BAGS), f32),
            VM((BAGS, E), bf16),
            VM((256, TOPH), f32),
            VM((256, 128), f32),
            VM((TOPH, 128), f32),
            VM((TOPH, 128), f32),
            dma, dma, dma, dma, dma, dma, dma((N_DEV // GROUP,)), dma, dma, dma, dma, dma,
        ],
        compiler_params=pltpu.CompilerParams(
            collective_id=0, has_side_effects=True, vmem_limit_bytes=56 << 20
        ),
    )(
        owner, row, bag_length.T, dense_in.T, logit_grad.reshape(1, 128), table,
        w_bottom0, w_bottom1, w_bottom2, w_top0, w_top1.reshape(1, TOPH),
    )
    new_table, change = pl.pallas_call(
        scatter_kernel,
        out_shape=(sds((ROWS_DEV, E), f32), sds((ROWS_DEV, E), bf16)),
        in_specs=[smem, vmem, vmem, vmem],
        out_specs=(vmem, vmem),
        scratch_shapes=[VM((WAYS, ROWS_DEV, E), f32), VM((MAIN + 8, E), f32)],
        compiler_params=pltpu.CompilerParams(vmem_limit_bytes=56 << 20),
    )(ids, gmain, gextra, table)
    new_parity, g0, g1, g2, gt0, gt1 = pl.pallas_call(
        parity_kernel,
        out_shape=(
            sds(parity.shape, f32),
            sds((DENSE, BOT1), f32),
            sds((BOT1, BOT2), f32),
            sds((BOT2, E), f32),
            sds((TOPIN, TOPH), f32),
            sds((1, TOPH), f32),
        ),
        in_specs=[vmem] * 3,
        out_specs=(vmem,) * 6,
        scratch_shapes=[
            VM((N_MEMBER, ROWS_DEV // N_MEMBER, E), bf16),
            VM((N_GROUP, PIECE, E), bf16),
            VM((PIECE, E), f32),
            VM((N_MEMBER, SMALL, E), f32),
            VM((SMALL, E), f32),
            VM((N_MEMBER, SMALL, E), f32),
            VM((PIECE, E), bf16),
            VM((N_GROUP, PIECE, E), bf16),
            dma((N_MEMBER,)), dma((N_MEMBER,)), dma((N_GROUP,)), dma((N_GROUP,)),
            dma((N_MEMBER,)), dma((N_MEMBER,)), dma((N_MEMBER,)), dma((N_MEMBER,)),
            dma((N_GROUP,)), dma((N_GROUP,)),
        ],
        compiler_params=pltpu.CompilerParams(
            collective_id=1, has_side_effects=True, vmem_limit_bytes=56 << 20
        ),
    )(change, parity, flat)
    return new_table, new_parity, g0, g1, g2, gt0, gt1.reshape(TOPH)


def solution(mesh):
    rows = P(("group", "member"), None)
    cube = P(("group", "member"), None, None)
    in_specs = (rows, cube, cube, rows, P(("group", "member")), rows, rows, P(), P(), P(), P(), P())
    out_specs = (rows, rows, P(), P(), P(), P(), P())
    return jax.shard_map(body, mesh=mesh, in_specs=in_specs, out_specs=out_specs, check_vma=False)
```

```python
import functools

import jax
import jax.numpy as jnp
import numpy as np
from jax import lax
from jax.experimental import pallas as pl
from jax.experimental.pallas import tpu as pltpu
from jax.sharding import PartitionSpec as P

embed_rate = 1.0

MESH = pl.DeviceIdType.MESH
N_DEV = 128
N_GROUP = 8
N_MEMBER = 16
E = 128
ROWS_DEV = 8192
NT = 8
HOT = 8
BAGS = 1024
MAIN = 96
SERVE = 16
GROUP = 8
PAIRS = [(i, j) for i in range(9) for j in range(i)]
BOT1, BOT2, TOPH, DENSE, TOPIN = 512, 256, 1024, 13, 164

TOP0_ROWS = 176
OFF_TOP0 = 0
OFF_BOT1 = 8 * TOP0_ROWS
OFF_BOT2 = OFF_BOT1 + 2 * BOT1
OFF_BOT0 = OFF_BOT2 + BOT2
OFF_TOP1 = OFF_BOT0 + 4 * 16
FLAT = 3072
HALF = FLAT // 2
PIECE = FLAT // N_GROUP
SMALL = PIECE // N_MEMBER

f32, bf16, i32 = jnp.float32, jnp.bfloat16, jnp.int32
VM = pltpu.VMEM


def iota(shape, dim):
    return lax.broadcasted_iota(i32, shape, dim)


def dot(a, b, dims):
    return lax.dot_general(a, b, (dims, ((), ())), preferred_element_type=f32)


NN = ((1,), (0,))
NT_ = ((1,), (1,))
TN = ((0,), (0,))


def halves(a):
    hi = a.astype(bf16)
    return hi, (a - hi.astype(f32)).astype(bf16)


def dot3(a, b, dims):
    return dot(a[0], b[0], dims) + (dot(a[0], b[1], dims) + dot(a[1], b[0], dims))


def coords():
    g, m = lax.axis_index("group"), lax.axis_index("member")
    return g // 2, g % 2, m // 4, m % 4


def peer(k):
    z, c, x, y = coords()
    kx = k % 4
    ky = (k // 4 + kx) % 4
    kz = (k // 16 + ky) % 4
    kc = k // 64
    return ((z + kz) % 4) * 2 + (c + kc) % 2, ((x + kx) % 4) * 4 + (y + ky) % 4


def origin(k):
    z, c, x, y = coords()
    kx = k % 4
    ky = (k // 4 + kx) % 4
    kz = (k // 16 + ky) % 4
    kc = k // 64
    return ((z + 4 - kz) % 4) * 2 + (c + 2 - kc) % 2, ((x + 4 - kx) % 4) * 4 + (y + 4 - ky) % 4


def each_peer(act):
    z, c, x, y = coords()
    member = [((x + r % 4) % 4) * 4 + (y + (r // 4 + r % 4) % 4) % 4 for r in range(16)]

    def sixteen(a, first):
        group = [((z + a + ky) % 4) * 2 + (c + a // 4) % 2 for ky in range(4)]
        for r in range(first, 16):
            act(a * 16 + r, (group[(r // 4 + r % 4) % 4], member[r]))

    sixteen(0, 1)

    def loop(a, carry):
        sixteen(a, 0)
        return carry

    lax.fori_loop(1, 8, loop, 0)


def sigmoid(v):
    return 1.0 / (1.0 + jnp.exp(-v))


def exchange_kernel(
    own_ref, row_ref, len_ref, x_ref, lg_ref, table_hbm, w0_ref, w1_ref, w2_ref, wt0_ref, wt1_ref,
    ids_out, gmain_out, gextra_out, flat_out,
    table_v, ids_send, ids_recv, ids_smem, stage, send_main, send_extra, recv_main, recv_extra,
    hits, vals, bag_of, bag_extra, st, pooled, pg, wt0_p, top_in, hid, dup,
    table_sem, smem_sem, ids_ssem, ids_rsem, row_ssem, row_esem, rowm_rsem, rowe_rsem,
    g_ssem, g_esem, gm_rsem, ge_rsem, flat, flat_half, own_sem, half_ssem, half_rsem,
):
    g, m = lax.axis_index("group"), lax.axis_index("member")
    me = g * N_MEMBER + m

    table_copy = pltpu.make_async_copy(table_hbm, table_v, table_sem)
    table_copy.start()
    barrier = pltpu.get_barrier_semaphore()

    each_peer(lambda k, to: pl.semaphore_signal(barrier, 1, device_id=to, device_id_type=MESH))

    upper = (iota((256, 384), 0) < iota((256, 384), 1)).astype(bf16)
    dev_of = iota((128, 256), 0)
    lane = iota((1, 128), 1)
    bag_lo = jnp.concatenate([lane, lane], axis=1).astype(f32).astype(bf16)

    def place(j, count):
        t = j // 4
        h = (2 * j) % 8
        length = len_ref[pl.ds(t, 1), :]
        own = jnp.concatenate([own_ref[pl.ds(2 * j, 1), :], own_ref[pl.ds(2 * j + 1, 1), :]], axis=1)
        row = jnp.concatenate([row_ref[pl.ds(2 * j, 1), :], row_ref[pl.ds(2 * j + 1, 1), :]], axis=1)
        own = jnp.where(jnp.concatenate([h < length, h + 1 < length], axis=1), own, -1)
        hit = (own == dev_of).astype(f32)
        hit_b = hit.astype(bf16)
        ranks = dot(hit_b, upper, NN)
        before = ranks[:, 0:256] + jnp.concatenate([count, count], axis=1)
        pos = jnp.sum(before * hit, axis=0, keepdims=True).astype(i32)
        at = (pos == dev_of).astype(f32).astype(bf16)
        hits[j] = hit_b
        vals[j, 0:128, :] = at * (row // 128).astype(f32).astype(bf16)
        vals[j, 128:256, :] = at * (row % 128).astype(f32).astype(bf16)
        vals[j, 256:384, :] = at * (t + 1).astype(f32).astype(bf16)
        vals[j, 384:512, :] = at * bag_lo
        return count + ranks[:, 256:384]

    count = lax.fori_loop(0, 32, place, jnp.zeros((128, 128), f32), unroll=4)
    acc = dot(vals[0], hits[0], NT_)
    for j in range(1, 32):
        acc = acc + dot(vals[j], hits[j], NT_)
    ids = (acc[0:128] * 128.0 + acc[128:256]).T
    ids = jnp.where(iota((128, 128), 1) == 127, count, ids).astype(i32)
    for d in range(N_DEV):
        ids_send[d] = ids[d : d + 1, :]
    bag = acc[256:384] * 128.0 + acc[384:512] - 128.0
    pl.semaphore_wait(barrier, N_DEV - 1)

    def send_ids(k, to):
        pltpu.make_async_remote_copy(
            ids_send.at[to[0] * N_MEMBER + to[1]], ids_recv.at[k], ids_ssem, ids_rsem.at[k // SERVE],
            device_id=to, device_id_type=MESH,
        ).start()

    each_peer(send_ids)
    ids_recv[0] = ids_send[me]

    def take_ids(c, count):
        pltpu.make_async_copy(
            ids_send.at[pl.ds(0, count)], ids_recv.at[pl.ds(0, count)], ids_rsem.at[c]
        ).wait()
        at = pl.ds(c * SERVE, SERVE)
        ids_recv[at] = jnp.clip(ids_recv[at], 0, ROWS_DEV - 1)
        smem_copy(c).start()

    def smem_copy(c):
        at = pl.ds(c * SERVE, SERVE)
        return pltpu.make_async_copy(ids_recv.at[at], ids_smem.at[at], smem_sem.at[c])

    take_ids(0, SERVE - 1)
    table_copy.wait()

    def gather(slot):
        for i in range(MAIN):
            stage[i : i + 1, :] = table_v[pl.ds(ids_smem[slot, 0, i] & (ROWS_DEV - 1), 1), :]
        send_main[slot] = stage[...].astype(bf16)
        send_extra[slot] = table_v[pl.ds(ids_smem[slot, 0, MAIN] & (ROWS_DEV - 1), 1), :]

    def rows_copies(k):
        to = origin(k)
        return (
            pltpu.make_async_remote_copy(
                send_main.at[k], recv_main.at[k], row_ssem, rowm_rsem.at[k // GROUP],
                device_id=to, device_id_type=MESH,
            ),
            pltpu.make_async_remote_copy(
                send_extra.at[k], recv_extra.at[k], row_esem, rowe_rsem,
                device_id=to, device_id_type=MESH,
            ),
        )

    def serve(k, c):
        gather(k)
        for copy in rows_copies(k):
            copy.start()
        return c

    def serve_chunk(c, carry):
        take_ids(c + 1, SERVE)
        smem_copy(c).wait()
        lax.fori_loop(jnp.maximum(c * SERVE, 1), c * SERVE + SERVE, serve, 0)
        return carry

    lax.fori_loop(0, N_DEV // SERVE - 1, serve_chunk, 0)
    smem_copy(N_DEV // SERVE - 1).wait()
    lax.fori_loop(N_DEV - SERVE, N_DEV, serve, 0)
    gather(0)
    recv_main[0] = send_main[0]
    recv_extra[0] = send_extra[0]

    bag_i = bag.astype(i32)
    for d in range(N_DEV):
        bag_of[d] = jnp.broadcast_to(bag_i[0:MAIN, d : d + 1], (MAIN, 128))
    bag_t = bag.T.astype(i32)
    bag_extra[...] = jnp.broadcast_to(bag_t[:, MAIN : MAIN + 1], (128, 128))

    top_in[...] = jnp.zeros_like(top_in)
    top_in[0:DENSE, :] = x_ref[...]
    x_pad = top_in[0:128, :]
    x_h = halves(x_pad)
    w0_t = jnp.concatenate([w0_ref[...], jnp.zeros((128 - DENSE, BOT1), f32)], axis=0).T
    w0_th = halves(w0_t)
    h1p = dot3(w0_th, x_h, NN)
    s1 = sigmoid(h1p)
    h1_h = halves(h1p * s1)
    d1 = s1 * (1.0 + h1p * (1.0 - s1))
    w1_h = halves(w1_ref[...])
    w1_th = halves(w1_ref[...].T)
    h2p = dot3(w1_th, h1_h, NN)
    s2 = sigmoid(h2p)
    h2_h = halves(h2p * s2)
    d2 = s2 * (1.0 + h2p * (1.0 - s2))
    w2_h = halves(w2_ref[...])
    w2_th = halves(w2_ref[...].T)
    bp = dot3(w2_th, h2_h, NN)
    s3 = sigmoid(bp)
    bottom = bp * s3
    d3 = s3 * (1.0 + bp * (1.0 - s3))
    top_in[0:128, :] = bottom
    wt0_p[...] = jnp.zeros_like(wt0_p)
    wt0_p[0:TOPIN, :] = wt0_ref[...]
    wt0_h = halves(wt0_p[...])
    wt0_th = halves(wt0_p[...].T)

    def one_hot(bags):
        return jnp.concatenate(
            [(bags == iota((1, 128), 1) + 128 * t).astype(f32).astype(bf16) for t in range(NT)], axis=1
        )

    def pool_main(q):
        for i in range(GROUP):
            from_g, from_m = peer(q * GROUP + i)
            st[pl.ds(i * MAIN, MAIN), :] = one_hot(bag_of[from_g * N_MEMBER + from_m])
        rows = recv_main[pl.ds(q * GROUP, GROUP)].reshape(GROUP * MAIN, E)
        pooled[...] += dot(rows, st[...], TN)

    def wait_rows(q, count):
        pltpu.make_async_copy(
            send_main.at[pl.ds(0, count)], recv_main.at[pl.ds(0, count)], rowm_rsem.at[q]
        ).wait()

    pooled[...] = jnp.zeros_like(pooled)
    wait_rows(0, GROUP - 1)
    pool_main(0)

    def pool_step(q, c):
        wait_rows(q, GROUP)
        pool_main(q)
        return c

    lax.fori_loop(1, N_DEV // GROUP, pool_step, 0)
    pltpu.make_async_copy(
        send_extra.at[pl.ds(0, 127)], recv_extra.at[pl.ds(0, 127)], rowe_rsem
    ).wait()
    for k in range(N_DEV):
        from_g, from_m = peer(k)
        hid[pl.ds(from_g * N_MEMBER + from_m, 1), :] = recv_extra[k]
    pooled[...] += dot(hid[0:128, :].astype(bf16), one_hot(bag_extra[...]), TN)

    z = [bottom] + [pooled[:, 128 * t : 128 * (t + 1)] for t in range(NT)]
    for n, (i, j) in enumerate(PAIRS):
        top_in[128 + n : 129 + n, :] = jnp.sum(z[i] * z[j], axis=0, keepdims=True)
    top_h = halves(top_in[...])
    up = dot3(wt0_th, top_h, NN)
    su = sigmoid(up)
    hid[...] = up * su
    lg = lg_ref[...]
    wt1_col = jnp.broadcast_to(wt1_ref[...], (128, TOPH)).T
    dup[...] = wt1_col * lg * (su * (1.0 + up * (1.0 - su)))
    dup_h = halves(dup[...])
    d_top = dot3(wt0_h, dup_h, NN)
    d_pair = {}
    for n, (i, j) in enumerate(PAIRS):
        d_pair[i, j] = d_pair[j, i] = d_top[128 + n : 129 + n, :]
    d_z = []
    for i in range(9):
        total = None
        for j in range(9):
            if j != i:
                term = d_pair[i, j] * z[j]
                total = term if total is None else total + term
        d_z.append(total)
        if i > 0:
            pg[128 * (i - 1) : 128 * i, :] = total.T.astype(bf16)

    pltpu.make_async_copy(send_main.at[pl.ds(0, 127)], recv_main.at[pl.ds(0, 127)], row_ssem).wait()
    pltpu.make_async_copy(send_extra.at[pl.ds(0, 127)], recv_extra.at[pl.ds(0, 127)], row_esem).wait()

    extra = dot(one_hot(bag_extra[...]), pg[...], NN)
    for d in range(N_DEV):
        send_extra[d] = extra[d : d + 1, :]

    def grad_copies(k):
        to_g, to_m = peer(k)
        return (
            pltpu.make_async_remote_copy(
                send_main.at[k], gmain_out.at[k], g_ssem, gm_rsem,
                device_id=(to_g, to_m), device_id_type=MESH,
            ),
            pltpu.make_async_remote_copy(
                send_extra.at[to_g * N_MEMBER + to_m], gextra_out.at[k], g_esem, ge_rsem,
                device_id=(to_g, to_m), device_id_type=MESH,
            ),
        )

    def expand(q):
        for i in range(GROUP):
            to_g, to_m = peer(q * GROUP + i)
            st[pl.ds(i * MAIN, MAIN), :] = one_hot(bag_of[to_g * N_MEMBER + to_m])
        grads = dot(st[...], pg[...], NN).astype(bf16)
        send_main[pl.ds(q * GROUP, GROUP)] = grads.reshape(GROUP, MAIN, E)

    def start_grads(k, c):
        for copy in grad_copies(k):
            copy.start()
        return c

    expand(0)
    lax.fori_loop(1, GROUP, start_grads, 0)

    def expand_step(q, c):
        expand(q)
        lax.fori_loop(q * GROUP, q * GROUP + GROUP, start_grads, 0)
        return c

    lax.fori_loop(1, N_DEV // GROUP, expand_step, 0)
    own_copy = pltpu.make_async_copy(send_main.at[0], gmain_out.at[0], own_sem)
    own_copy.start()
    gextra_out[0] = send_extra[me]
    ids_out[...] = ids_recv[...]

    flat[...] = jnp.zeros_like(flat)
    g_t0 = dot3(top_h, dup_h, NT_)
    for c in range(8):
        flat[OFF_TOP0 + c * TOP0_ROWS : OFF_TOP0 + (c + 1) * TOP0_ROWS, :] = g_t0[
            0:TOP0_ROWS, 128 * c : 128 * (c + 1)
        ]
    lg_h = halves(jnp.broadcast_to(lg, (8, 128)))
    g_t1 = dot3(lg_h, halves(hid[...]), NT_)[0:1]
    g_t1 = jnp.concatenate([g_t1[:, 128 * c : 128 * (c + 1)] for c in range(8)], axis=0)
    flat[OFF_TOP1 : OFF_TOP1 + 16, :] = jnp.concatenate([g_t1, g_t1], axis=0)
    d_bp = halves((d_top[0:128] + d_z[0]) * d3)
    flat[OFF_BOT2 : OFF_BOT2 + BOT2, :] = dot3(h2_h, d_bp, NT_)
    d_h2p = halves(dot3(w2_h, d_bp, NN) * d2)
    g_b1 = dot3(h1_h, d_h2p, NT_)
    for c in range(2):
        flat[OFF_BOT1 + c * BOT1 : OFF_BOT1 + (c + 1) * BOT1, :] = g_b1[:, 128 * c : 128 * (c + 1)]
    d_h1p = halves(dot3(w1_h, d_h2p, NN) * d1)
    g_b0 = dot3(x_h, d_h1p, NT_)[0:16]
    for c in range(4):
        flat[OFF_BOT0 + c * 16 : OFF_BOT0 + (c + 1) * 16, :] = g_b0[:, 128 * c : 128 * (c + 1)]

    core = g % 2
    half_copy = pltpu.make_async_remote_copy(
        flat.at[pl.ds(pl.multiple_of((1 - core) * HALF, HALF), HALF)], flat_half, half_ssem, half_rsem,
        device_id=(g + 1 - 2 * core, m), device_id_type=MESH,
    )
    half_copy.start()
    half_copy.wait()
    own_half = flat[pl.ds(pl.multiple_of(core * HALF, HALF), HALF), :]
    flat_out[...] = (own_half + flat_half[...]).astype(bf16)

    own_copy.wait()
    pltpu.make_async_copy(ids_send.at[pl.ds(0, 127)], ids_recv.at[pl.ds(0, 127)], ids_ssem).wait()
    pltpu.make_async_copy(send_main.at[pl.ds(0, 127)], recv_main.at[pl.ds(0, 127)], g_ssem).wait()
    pltpu.make_async_copy(send_extra.at[pl.ds(0, 127)], recv_extra.at[pl.ds(0, 127)], g_esem).wait()
    pltpu.make_async_copy(send_main.at[pl.ds(1, 127)], gmain_out.at[pl.ds(1, 127)], gm_rsem).wait()
    pltpu.make_async_copy(send_extra.at[pl.ds(0, 127)], gextra_out.at[pl.ds(0, 127)], ge_rsem).wait()


WAYS = 8
CHUNK = 512


def scatter_kernel(ids_ref, gmain_hbm, gextra_ref, table_hbm, new_hbm, change_hbm,
                   sums, stage, gmain, table, change, gmain_sem, table_sem, new_sem, change_sem):
    gmain_copy = pltpu.make_async_copy(gmain_hbm, gmain, gmain_sem)
    gmain_copy.start()
    table_copy = pltpu.make_async_copy(table_hbm, table, table_sem)
    table_copy.start()
    sums[...] = jnp.zeros_like(sums)
    stage[...] = jnp.zeros_like(stage)
    gmain_copy.wait()

    def source(s, c):
        stage[0:MAIN, :] = gmain[s].astype(f32)
        stage[MAIN : MAIN + 1, :] = gextra_ref[s]
        count = ids_ref[s, 0, 127]

        def fetch(first):
            return (
                [ids_ref[s, 0, first + i] for i in range(WAYS)],
                [stage[pl.ds(first + i, 1), :] for i in range(WAYS)],
            )

        def batch(b, carry):
            rows, terms = carry
            total = [sums[i, pl.ds(rows[i], 1), :] + terms[i] for i in range(WAYS)]
            ahead = fetch((b + 1) * WAYS)
            for i in range(WAYS):
                sums[i, pl.ds(rows[i], 1), :] = total[i]
            return ahead

        lax.fori_loop(0, (count + WAYS - 1) // WAYS, batch, fetch(0))
        return c

    lax.fori_loop(0, N_DEV, source, 0)
    table_copy.wait()

    def finish(b, c):
        start = pl.multiple_of(b * CHUNK, CHUNK)
        for r in range(0, CHUNK, 64):
            at = pl.ds(pl.multiple_of(start + r, 64), 64)
            total = sums[0, at, :]
            for i in range(1, WAYS):
                total = total + sums[i, at, :]
            total = -embed_rate * total
            table[at, :] = table[at, :] + total
            change[at, :] = total.astype(bf16)
        at = pl.ds(start, CHUNK)
        pltpu.make_async_copy(table.at[at], new_hbm.at[at], new_sem).start()
        pltpu.make_async_copy(change.at[at], change_hbm.at[at], change_sem).start()
        return c

    lax.fori_loop(0, ROWS_DEV // CHUNK, finish, 0)
    pltpu.make_async_copy(table, new_hbm, new_sem).wait()
    pltpu.make_async_copy(change, change_hbm, change_sem).wait()


def member_peer(k, sign):
    x, y = lax.axis_index("member") // 4, lax.axis_index("member") % 4
    kx = k % 4
    ky = (k // 4 + kx) % 4
    if sign < 0:
        kx, ky = (4 - kx) % 4, (4 - ky) % 4
    return ((x + kx) % 4) * 4 + (y + ky) % 4


CUT = (5, 9, 13)


def parity_kernel(
    change_ref, parity_ref, flat_ref,
    new_ref, all_z,
    pieces, part_z, sum_z, part_xy, sum_xy, all_xy, all_z_send,
    ch_ssem, ch_rsem, rz_ssem, rz_rsem, rx_ssem, rx_rsem, ax_ssem, ax_rsem, az_ssem, az_rsem,
):
    g, m = lax.axis_index("group"), lax.axis_index("member")
    barrier = pltpu.get_barrier_semaphore()
    for j in range(1, N_GROUP):
        pl.semaphore_signal(barrier, 1, device_id=((g + j) % N_GROUP, m), device_id_type=MESH)
    for k in range(1, N_MEMBER):
        pl.semaphore_signal(barrier, 1, device_id=(g, member_peer(k, 1)), device_id_type=MESH)
    pl.semaphore_wait(barrier, N_GROUP - 1 + N_MEMBER - 1)

    def remote(src, dst, ssem, rsem, to):
        return pltpu.make_async_remote_copy(src, dst, ssem, rsem, device_id=to, device_id_type=MESH)

    rows = ROWS_DEV // N_MEMBER

    def change_copy(k):
        to = member_peer(k, 1)
        return remote(
            change_ref.at[pl.ds(pl.multiple_of(to * rows, rows), rows)], pieces.at[k], ch_ssem.at[k], ch_rsem.at[k],
            (g, to),
        )

    z, core = g // 2, g % 2

    def rz_copy(j):
        to = (z + j) % 4
        return remote(
            flat_ref.at[pl.ds(pl.multiple_of(to * PIECE, PIECE), PIECE)], part_z.at[j], rz_ssem.at[j], rz_rsem.at[j],
            (to * 2 + core, m),
        )

    def rx_copy(k):
        to = member_peer(k, 1)
        return remote(
            sum_z.at[pl.ds(pl.multiple_of(to * SMALL, SMALL), SMALL)], part_xy.at[k], rx_ssem.at[k], rx_rsem.at[k],
            (g, to),
        )

    def ax_copy(k):
        return remote(sum_xy, all_xy.at[m], ax_ssem.at[k], ax_rsem.at[k], (g, member_peer(k, 1)))

    place = core * 4 + z

    def az_copy(j):
        return remote(all_z_send, all_z.at[place], az_ssem.at[j], az_rsem.at[j], ((g + j) % N_GROUP, m))

    for j in range(1, 4):
        rz_copy(j).start()
    for k in range(1, CUT[0]):
        change_copy(k).start()
    total = flat_ref[pl.ds(pl.multiple_of(z * PIECE, PIECE), PIECE), :].astype(f32)
    for j in range(1, 4):
        rz_copy(j).wait()
        total = total + part_z[j].astype(f32)
    sum_z[...] = total
    for k in range(1, N_MEMBER):
        rx_copy(k).start()
    for k in range(CUT[0], CUT[1]):
        change_copy(k).start()
    total = sum_z[pl.ds(pl.multiple_of(m * SMALL, SMALL), SMALL), :]
    for k in range(1, N_MEMBER):
        rx_copy(k).wait()
        total = total + part_xy[k]
    sum_xy[...] = total
    for k in range(1, N_MEMBER):
        ax_copy(k).start()
    for k in range(CUT[1], CUT[2]):
        change_copy(k).start()
    all_xy[m] = total
    for k in range(1, N_MEMBER):
        ax_copy(k).wait()
    all_z_send[...] = all_xy[...].reshape(PIECE, E).astype(bf16)
    for j in range(1, N_GROUP):
        az_copy(j).start()
    for k in range(CUT[2], N_MEMBER):
        change_copy(k).start()

    def weights(k):
        source = member_peer(k, -1).astype(f32) / N_MEMBER
        one = jnp.ones((1, 128), f32)
        return 1.0 / (one + source), 1.0 / (one * 2.0 + source)

    for k in range(1, N_MEMBER):
        change_copy(k).wait()
    coef = [weights(k) for k in range(N_MEMBER)]
    own_at = m * rows

    def combine(b, c):
        at = pl.ds(pl.multiple_of(b * 32, 32), 32)
        part = change_ref[pl.ds(pl.multiple_of(own_at + b * 32, 32), 32), :].astype(f32)
        first, second = coef[0][0] * part, coef[0][1] * part
        for k in range(1, N_MEMBER):
            part = pieces[k, at, :].astype(f32)
            first = first + coef[k][0] * part
            second = second + coef[k][1] * part
        new_ref[at, 0:128] = parity_ref[at, 0:128] + first
        new_ref[at, 128:256] = parity_ref[at, 128:256] + second
        return c

    lax.fori_loop(0, rows // 32, combine, 0)

    all_z[place] = all_z_send[...]
    for j in range(1, N_GROUP):
        az_copy(j).wait()


def unpack_kernel(parity_ref, all_z, new_ref, g0_ref, g1_ref, g2_ref, gt0_ref, gt1_ref):
    new_ref[...] = parity_ref[...]
    for c in range(8):
        gt0_ref[:, 128 * c : 128 * (c + 1)] = piece_rows(all_z, OFF_TOP0 + c * TOP0_ROWS, TOP0_ROWS)[0:TOPIN]
    for c in range(2):
        g1_ref[:, 128 * c : 128 * (c + 1)] = piece_rows(all_z, OFF_BOT1 + c * BOT1, BOT1)
    g2_ref[...] = piece_rows(all_z, OFF_BOT2, BOT2)
    for c in range(4):
        g0_ref[:, 128 * c : 128 * (c + 1)] = piece_rows(all_z, OFF_BOT0 + c * 16, 16)[0:DENSE]
    top1 = piece_rows(all_z, OFF_TOP1, 16)
    for c in range(8):
        gt1_ref[:, 128 * c : 128 * (c + 1)] = top1[c : c + 1, :]


def piece_rows(ref, start, count):
    out = []
    while count > 0:
        p, at = start // PIECE, start % PIECE
        n = min(count, PIECE - at)
        out.append(ref[p, at : at + n, :].astype(f32))
        start, count = start + n, count - n
    return out[0] if len(out) == 1 else jnp.concatenate(out, axis=0)


def body(
    dense_in, lookup_owner, lookup_row, bag_length, logit_grad, table, parity,
    w_bottom0, w_bottom1, w_bottom2, w_top0, w_top1,
):
    owner = lookup_owner.transpose(1, 2, 0).reshape(NT * HOT, 128)
    row = lookup_row.transpose(1, 2, 0).reshape(NT * HOT, 128)
    vmem = pl.BlockSpec(memory_space=VM)
    anyw = pl.BlockSpec(memory_space=pl.ANY)
    smem = pl.BlockSpec(memory_space=pltpu.SMEM)
    dma = pltpu.SemaphoreType.DMA
    sds = jax.ShapeDtypeStruct
    ids, gmain, gextra, flat = pl.pallas_call(
        exchange_kernel,
        out_shape=(
            sds((N_DEV, 1, 128), i32),
            sds((N_DEV, MAIN, E), bf16),
            sds((N_DEV, 1, E), f32),
            sds((HALF, E), bf16),
        ),
        in_specs=[vmem] * 5 + [anyw] + [vmem] * 5,
        out_specs=(vmem, anyw, vmem, vmem),
        scratch_shapes=[
            VM((ROWS_DEV, E), f32),
            VM((N_DEV, 1, 128), i32),
            VM((N_DEV, 1, 128), i32),
            pltpu.SMEM((N_DEV, 1, 128), i32),
            VM((MAIN, E), f32),
            VM((N_DEV, MAIN, E), bf16),
            VM((N_DEV, 1, E), f32),
            VM((N_DEV, MAIN, E), bf16),
            VM((N_DEV, 1, E), f32),
            VM((32, 128, 256), bf16),
            VM((32, 512, 256), bf16),
            VM((N_DEV, MAIN, 128), i32),
            VM((128, 128), i32),
            VM((GROUP * MAIN, BAGS), bf16),
            VM((E, BAGS), f32),
            VM((BAGS, E), bf16),
            VM((256, TOPH), f32),
            VM((256, 128), f32),
            VM((TOPH, 128), f32),
            VM((TOPH, 128), f32),
            dma, dma((N_DEV // SERVE,)), dma, dma((N_DEV // SERVE,)), dma, dma, dma((N_DEV // GROUP,)), dma,
            dma, dma, dma, dma,
            VM((FLAT, E), f32),
            VM((HALF, E), f32),
            dma, dma, dma,
        ],
        compiler_params=pltpu.CompilerParams(
            collective_id=0, has_side_effects=True, vmem_limit_bytes=56 << 20
        ),
    )(
        owner, row, bag_length.T, dense_in.T, logit_grad.reshape(1, 128), table,
        w_bottom0, w_bottom1, w_bottom2, w_top0, w_top1.reshape(1, TOPH),
    )
    new_table, change = pl.pallas_call(
        scatter_kernel,
        out_shape=(sds((ROWS_DEV, E), f32), sds((ROWS_DEV, E), bf16)),
        in_specs=[smem, anyw, vmem, anyw],
        out_specs=(anyw, anyw),
        scratch_shapes=[
            VM((WAYS, ROWS_DEV, E), f32),
            VM((MAIN + 16, E), f32),
            VM((N_DEV, MAIN, E), bf16),
            VM((ROWS_DEV, E), f32),
            VM((ROWS_DEV, E), bf16),
            dma, dma, dma, dma,
        ],
        compiler_params=pltpu.CompilerParams(vmem_limit_bytes=56 << 20),
    )(ids, gmain, gextra, table)
    parity_sum, all_z = pl.pallas_call(
        parity_kernel,
        out_shape=(sds(parity.shape, f32), sds((N_GROUP, PIECE, E), bf16)),
        in_specs=[vmem] * 3,
        out_specs=(vmem, vmem),
        scratch_shapes=[
            VM((N_MEMBER, ROWS_DEV // N_MEMBER, E), bf16),
            VM((4, PIECE, E), bf16),
            VM((PIECE, E), f32),
            VM((N_MEMBER, SMALL, E), f32),
            VM((SMALL, E), f32),
            VM((N_MEMBER, SMALL, E), f32),
            VM((PIECE, E), bf16),
            dma((N_MEMBER,)), dma((N_MEMBER,)), dma((4,)), dma((4,)),
            dma((N_MEMBER,)), dma((N_MEMBER,)), dma((N_MEMBER,)), dma((N_MEMBER,)),
            dma((N_GROUP,)), dma((N_GROUP,)),
        ],
        compiler_params=pltpu.CompilerParams(
            collective_id=1, has_side_effects=True, vmem_limit_bytes=56 << 20
        ),
    )(change, parity, flat)
    new_parity, g0, g1, g2, gt0, gt1 = pl.pallas_call(
        unpack_kernel,
        out_shape=(
            sds(parity.shape, f32),
            sds((DENSE, BOT1), f32),
            sds((BOT1, BOT2), f32),
            sds((BOT2, E), f32),
            sds((TOPIN, TOPH), f32),
            sds((1, TOPH), f32),
        ),
        in_specs=[vmem] * 2,
        out_specs=(vmem,) * 6,
        compiler_params=pltpu.CompilerParams(vmem_limit_bytes=32 << 20),
    )(parity_sum, all_z)
    return new_table, new_parity, g0, g1, g2, gt0, gt1.reshape(TOPH)


def solution(mesh):
    rows = P(("group", "member"), None)
    cube = P(("group", "member"), None, None)
    in_specs = (rows, cube, cube, rows, P(("group", "member")), rows, rows, P(), P(), P(), P(), P())
    out_specs = (rows, rows, P(), P(), P(), P(), P())
    return jax.shard_map(body, mesh=mesh, in_specs=in_specs, out_specs=out_specs, check_vma=False)
```

```python
import functools

import jax
import jax.numpy as jnp
import numpy as np
from jax import lax
from jax.experimental import pallas as pl
from jax.experimental.pallas import tpu as pltpu
from jax.sharding import PartitionSpec as P

embed_rate = 1.0

MESH = pl.DeviceIdType.MESH
N_DEV = 128
N_GROUP = 8
N_MEMBER = 16
E = 128
ROWS_DEV = 8192
NT = 8
HOT = 8
BAGS = 1024
MAIN = 96
SERVE = 16
GROUP = 8
PAIRS = [(i, j) for i in range(9) for j in range(i)]
BOT1, BOT2, TOPH, DENSE, TOPIN = 512, 256, 1024, 13, 164

TOP0_ROWS = 176
OFF_TOP0 = 0
OFF_BOT1 = 8 * TOP0_ROWS
OFF_BOT2 = OFF_BOT1 + 2 * BOT1
OFF_BOT0 = OFF_BOT2 + BOT2
OFF_TOP1 = OFF_BOT0 + 4 * 16
FLAT = 3072
HALF = FLAT // 2
PIECE = FLAT // N_GROUP
SMALL = PIECE // N_MEMBER

f32, bf16, i32 = jnp.float32, jnp.bfloat16, jnp.int32
VM = pltpu.VMEM


def iota(shape, dim):
    return lax.broadcasted_iota(i32, shape, dim)


def dot(a, b, dims):
    return lax.dot_general(a, b, (dims, ((), ())), preferred_element_type=f32)


NN = ((1,), (0,))
NT_ = ((1,), (1,))
TN = ((0,), (0,))


def halves(a):
    hi = a.astype(bf16)
    return hi, (a - hi.astype(f32)).astype(bf16)


def dot3(a, b, dims):
    return dot(a[0], b[0], dims) + (dot(a[0], b[1], dims) + dot(a[1], b[0], dims))


def coords():
    g, m = lax.axis_index("group"), lax.axis_index("member")
    return g // 2, g % 2, m // 4, m % 4


def peer(k):
    z, c, x, y = coords()
    kx = k % 4
    ky = (k // 4 + kx) % 4
    kz = (k // 16 + ky) % 4
    kc = k // 64
    return ((z + kz) % 4) * 2 + (c + kc) % 2, ((x + kx) % 4) * 4 + (y + ky) % 4


def origin(k):
    z, c, x, y = coords()
    kx = k % 4
    ky = (k // 4 + kx) % 4
    kz = (k // 16 + ky) % 4
    kc = k // 64
    return ((z + 4 - kz) % 4) * 2 + (c + 2 - kc) % 2, ((x + 4 - kx) % 4) * 4 + (y + 4 - ky) % 4


def each_peer(act):
    z, c, x, y = coords()
    member = [((x + r % 4) % 4) * 4 + (y + (r // 4 + r % 4) % 4) % 4 for r in range(16)]

    def sixteen(a, first):
        group = [((z + a + ky) % 4) * 2 + (c + a // 4) % 2 for ky in range(4)]
        for r in range(first, 16):
            act(a * 16 + r, (group[(r // 4 + r % 4) % 4], member[r]))

    sixteen(0, 1)

    def loop(a, carry):
        sixteen(a, 0)
        return carry

    lax.fori_loop(1, 8, loop, 0)


def sigmoid(v):
    return 1.0 / (1.0 + jnp.exp(-v))


def exchange_kernel(
    own_ref, row_ref, len_ref, x_ref, lg_ref, table_hbm, w0_hbm, w1_hbm, w2_hbm, wt0_hbm, wt1_ref,
    ids_out, gmain_out, gextra_out, flat_out,
    table_v, ids_send, ids_recv, ids_smem, stage, send_main, send_extra, recv_main, recv_extra,
    hits, vals, bag_of, bag_extra, st, st_extra, pooled, pg, wt0_p, top_in, hid, dup,
    table_sem, smem_sem, ids_ssem, ids_rsem, row_ssem, row_esem, rowm_rsem, rowe_rsem,
    g_ssem, g_esem, gm_rsem, ge_rsem, flat, flat_half, own_sem, half_ssem, half_rsem,
    w0_ref, w1_ref, w2_ref, wt0_ref, w_sem,
):
    g, m = lax.axis_index("group"), lax.axis_index("member")
    me = g * N_MEMBER + m

    table_copy = pltpu.make_async_copy(table_hbm, table_v, table_sem)
    table_copy.start()
    barrier = pltpu.get_barrier_semaphore()
    weight_copies = [
        pltpu.make_async_copy(src, dst, w_sem.at[i])
        for i, (src, dst) in enumerate([(w0_hbm, w0_ref), (w1_hbm, w1_ref), (w2_hbm, w2_ref), (wt0_hbm, wt0_ref)])
    ]
    for copy in weight_copies:
        copy.start()

    each_peer(lambda k, to: pl.semaphore_signal(barrier, 1, device_id=to, device_id_type=MESH))

    upper = (iota((256, 384), 0) < iota((256, 384), 1)).astype(bf16)
    dev_of = iota((128, 256), 0)
    lane = iota((1, 128), 1)
    bag_lo = jnp.concatenate([lane, lane], axis=1).astype(f32).astype(bf16)

    def place(j, count):
        t = j // 4
        h = (2 * j) % 8
        length = len_ref[pl.ds(t, 1), :]
        own = jnp.concatenate([own_ref[pl.ds(2 * j, 1), :], own_ref[pl.ds(2 * j + 1, 1), :]], axis=1)
        row = jnp.concatenate([row_ref[pl.ds(2 * j, 1), :], row_ref[pl.ds(2 * j + 1, 1), :]], axis=1)
        own = jnp.where(jnp.concatenate([h < length, h + 1 < length], axis=1), own, -1)
        hit = (own == dev_of).astype(f32)
        hit_b = hit.astype(bf16)
        ranks = dot(hit_b, upper, NN)
        before = ranks[:, 0:256] + jnp.concatenate([count, count], axis=1)
        pos = jnp.sum(before * hit, axis=0, keepdims=True).astype(i32)
        at = (pos == dev_of).astype(f32).astype(bf16)
        hits[j] = hit_b
        vals[j, 0:128, :] = at * (row // 128).astype(f32).astype(bf16)
        vals[j, 128:256, :] = at * (row % 128).astype(f32).astype(bf16)
        vals[j, 256:384, :] = at * (t + 1).astype(f32).astype(bf16)
        vals[j, 384:512, :] = at * bag_lo
        return count + ranks[:, 256:384]

    count = lax.fori_loop(0, 32, place, jnp.zeros((128, 128), f32), unroll=4)
    acc = dot(vals[0], hits[0], NT_)
    for j in range(1, 32):
        acc = acc + dot(vals[j], hits[j], NT_)
    ids = (acc[0:128] * 128.0 + acc[128:256]).T
    ids = jnp.where(iota((128, 128), 1) == 127, count, ids).astype(i32)
    for d in range(N_DEV):
        ids_send[d] = ids[d : d + 1, :]
    bag = acc[256:384] * 128.0 + acc[384:512] - 128.0
    pl.semaphore_wait(barrier, N_DEV - 1)

    def send_ids(k, to):
        pltpu.make_async_remote_copy(
            ids_send.at[to[0] * N_MEMBER + to[1]], ids_recv.at[k], ids_ssem, ids_rsem.at[k // SERVE],
            device_id=to, device_id_type=MESH,
        ).start()

    each_peer(send_ids)
    ids_recv[0] = ids_send[me]

    def take_ids(c, count):
        pltpu.make_async_copy(
            ids_send.at[pl.ds(0, count)], ids_recv.at[pl.ds(0, count)], ids_rsem.at[c]
        ).wait()
        at = pl.ds(c * SERVE, SERVE)
        ids_recv[at] = jnp.clip(ids_recv[at], 0, ROWS_DEV - 1)
        smem_copy(c).start()

    def smem_copy(c):
        at = pl.ds(c * SERVE, SERVE)
        return pltpu.make_async_copy(ids_recv.at[at], ids_smem.at[at], smem_sem.at[c])

    take_ids(0, SERVE - 1)
    table_copy.wait()

    def gather(slot):
        for i in range(MAIN):
            stage[i : i + 1, :] = table_v[pl.ds(ids_smem[slot, 0, i] & (ROWS_DEV - 1), 1), :]
        send_main[slot] = stage[...].astype(bf16)
        send_extra[slot] = table_v[pl.ds(ids_smem[slot, 0, MAIN] & (ROWS_DEV - 1), 1), :]

    def rows_copies(k):
        to = origin(k)
        return (
            pltpu.make_async_remote_copy(
                send_main.at[k], recv_main.at[k], row_ssem, rowm_rsem.at[k // GROUP],
                device_id=to, device_id_type=MESH,
            ),
            pltpu.make_async_remote_copy(
                send_extra.at[k], recv_extra.at[k], row_esem, rowe_rsem.at[k // GROUP],
                device_id=to, device_id_type=MESH,
            ),
        )

    def serve(k, c):
        gather(k)
        for copy in rows_copies(k):
            copy.start()
        return c

    def serve_chunk(c, carry):
        take_ids(c + 1, SERVE)
        smem_copy(c).wait()
        lax.fori_loop(jnp.maximum(c * SERVE, 1), c * SERVE + SERVE, serve, 0)
        return carry

    lax.fori_loop(0, N_DEV // SERVE - 1, serve_chunk, 0)
    smem_copy(N_DEV // SERVE - 1).wait()
    lax.fori_loop(N_DEV - SERVE, N_DEV, serve, 0)
    gather(0)
    recv_main[0] = send_main[0]
    recv_extra[0] = send_extra[0]

    bag_i = bag.astype(i32)
    for d in range(N_DEV):
        bag_of[d] = jnp.broadcast_to(bag_i[0:MAIN, d : d + 1], (MAIN, 128))
    bag_t = bag.T.astype(i32)
    bag_extra[...] = jnp.broadcast_to(bag_t[:, MAIN : MAIN + 1], (128, 128))

    for copy in weight_copies:
        copy.wait()

    top_in[...] = jnp.zeros_like(top_in)
    top_in[0:DENSE, :] = x_ref[...]
    x_pad = top_in[0:128, :]
    x_h = halves(x_pad)
    w0_t = jnp.concatenate([w0_ref[...], jnp.zeros((128 - DENSE, BOT1), f32)], axis=0).T
    w0_th = halves(w0_t)
    h1p = dot3(w0_th, x_h, NN)
    s1 = sigmoid(h1p)
    h1_h = halves(h1p * s1)
    d1 = s1 * (1.0 + h1p * (1.0 - s1))
    w1_h = halves(w1_ref[...])
    w1_th = halves(w1_ref[...].T)
    h2p = dot3(w1_th, h1_h, NN)
    s2 = sigmoid(h2p)
    h2_h = halves(h2p * s2)
    d2 = s2 * (1.0 + h2p * (1.0 - s2))
    w2_h = halves(w2_ref[...])
    w2_th = halves(w2_ref[...].T)
    bp = dot3(w2_th, h2_h, NN)
    s3 = sigmoid(bp)
    bottom = bp * s3
    d3 = s3 * (1.0 + bp * (1.0 - s3))
    top_in[0:128, :] = bottom
    wt0_p[...] = jnp.zeros_like(wt0_p)
    wt0_p[0:TOPIN, :] = wt0_ref[...]
    wt0_h = halves(wt0_p[...])
    wt0_th = halves(wt0_p[...].T)

    def one_hot(bags):
        return jnp.concatenate(
            [(bags == iota((1, 128), 1) + 128 * t).astype(f32).astype(bf16) for t in range(NT)], axis=1
        )

    def pool_main(q):
        for i in range(GROUP):
            from_g, from_m = peer(q * GROUP + i)
            st[pl.ds(i * MAIN, MAIN), :] = one_hot(bag_of[from_g * N_MEMBER + from_m])
            hid[pl.ds(from_g * N_MEMBER + from_m, 1), :] = recv_extra[q * GROUP + i]
        rows = recv_main[pl.ds(q * GROUP, GROUP)].reshape(GROUP * MAIN, E)
        pooled[...] += dot(rows, st[...], TN)

    def wait_rows(q, count):
        pltpu.make_async_copy(
            send_main.at[pl.ds(0, count)], recv_main.at[pl.ds(0, count)], rowm_rsem.at[q]
        ).wait()
        pltpu.make_async_copy(
            send_extra.at[pl.ds(0, count)], recv_extra.at[pl.ds(0, count)], rowe_rsem.at[q]
        ).wait()

    st_extra[...] = one_hot(bag_extra[...])
    pooled[...] = jnp.zeros_like(pooled)
    wait_rows(0, GROUP - 1)
    pool_main(0)

    def pool_step(q, c):
        wait_rows(q, GROUP)
        pool_main(q)
        return c

    lax.fori_loop(1, N_DEV // GROUP, pool_step, 0)
    pooled[...] += dot(hid[0:128, :].astype(bf16), st_extra[...], TN)

    z = [bottom] + [pooled[:, 128 * t : 128 * (t + 1)] for t in range(NT)]
    for n, (i, j) in enumerate(PAIRS):
        top_in[128 + n : 129 + n, :] = jnp.sum(z[i] * z[j], axis=0, keepdims=True)
    top_h = halves(top_in[...])
    up = dot3(wt0_th, top_h, NN)
    su = sigmoid(up)
    hid[...] = up * su
    lg = lg_ref[...]
    wt1_col = jnp.broadcast_to(wt1_ref[...], (128, TOPH)).T
    dup[...] = wt1_col * lg * (su * (1.0 + up * (1.0 - su)))
    dup_h = halves(dup[...])
    d_top = dot3(wt0_h, dup_h, NN)
    d_pair = {}
    for n, (i, j) in enumerate(PAIRS):
        d_pair[i, j] = d_pair[j, i] = d_top[128 + n : 129 + n, :]
    d_z = []
    for i in range(9):
        total = None
        for j in range(9):
            if j != i:
                term = d_pair[i, j] * z[j]
                total = term if total is None else total + term
        d_z.append(total)
        if i > 0:
            pg[128 * (i - 1) : 128 * i, :] = total.T.astype(bf16)

    pltpu.make_async_copy(send_main.at[pl.ds(0, 127)], recv_main.at[pl.ds(0, 127)], row_ssem).wait()
    pltpu.make_async_copy(send_extra.at[pl.ds(0, 127)], recv_extra.at[pl.ds(0, 127)], row_esem).wait()

    def main_copy(k):
        return pltpu.make_async_remote_copy(
            send_main.at[k], gmain_out.at[k], g_ssem, gm_rsem, device_id=peer(k), device_id_type=MESH
        )

    def send_grad_extra(k, to):
        pltpu.make_async_remote_copy(
            send_extra.at[to[0] * N_MEMBER + to[1]], gextra_out.at[k], g_esem, ge_rsem,
            device_id=to, device_id_type=MESH,
        ).start()

    def expand(q):
        for i in range(GROUP):
            to_g, to_m = peer(q * GROUP + i)
            st[pl.ds(i * MAIN, MAIN), :] = one_hot(bag_of[to_g * N_MEMBER + to_m])
        grads = dot(st[...], pg[...], NN).astype(bf16)
        send_main[pl.ds(q * GROUP, GROUP)] = grads.reshape(GROUP, MAIN, E)

    def start_grads(k, c):
        main_copy(k).start()
        return c

    expand(0)
    lax.fori_loop(1, GROUP, start_grads, 0)

    def expand_step(q, c):
        expand(q)
        lax.fori_loop(q * GROUP, q * GROUP + GROUP, start_grads, 0)
        return c

    lax.fori_loop(1, N_DEV // GROUP // 2, expand_step, 0)
    extra = dot(st_extra[...], pg[...], NN)
    for d in range(N_DEV):
        send_extra[d] = extra[d : d + 1, :]
    each_peer(send_grad_extra)
    lax.fori_loop(N_DEV // GROUP // 2, N_DEV // GROUP, expand_step, 0)
    own_copy = pltpu.make_async_copy(send_main.at[0], gmain_out.at[0], own_sem)
    own_copy.start()
    gextra_out[0] = send_extra[me]
    ids_out[...] = ids_recv[...]

    flat[...] = jnp.zeros_like(flat)
    g_t0 = dot3(top_h, dup_h, NT_)
    for c in range(8):
        flat[OFF_TOP0 + c * TOP0_ROWS : OFF_TOP0 + (c + 1) * TOP0_ROWS, :] = g_t0[
            0:TOP0_ROWS, 128 * c : 128 * (c + 1)
        ]
    lg_h = halves(jnp.broadcast_to(lg, (8, 128)))
    g_t1 = dot3(lg_h, halves(hid[...]), NT_)[0:1]
    g_t1 = jnp.concatenate([g_t1[:, 128 * c : 128 * (c + 1)] for c in range(8)], axis=0)
    flat[OFF_TOP1 : OFF_TOP1 + 16, :] = jnp.concatenate([g_t1, g_t1], axis=0)
    d_bp = halves((d_top[0:128] + d_z[0]) * d3)
    flat[OFF_BOT2 : OFF_BOT2 + BOT2, :] = dot3(h2_h, d_bp, NT_)
    d_h2p = halves(dot3(w2_h, d_bp, NN) * d2)
    g_b1 = dot3(h1_h, d_h2p, NT_)
    for c in range(2):
        flat[OFF_BOT1 + c * BOT1 : OFF_BOT1 + (c + 1) * BOT1, :] = g_b1[:, 128 * c : 128 * (c + 1)]
    d_h1p = halves(dot3(w1_h, d_h2p, NN) * d1)
    g_b0 = dot3(x_h, d_h1p, NT_)[0:16]
    for c in range(4):
        flat[OFF_BOT0 + c * 16 : OFF_BOT0 + (c + 1) * 16, :] = g_b0[:, 128 * c : 128 * (c + 1)]

    core = g % 2
    half_copy = pltpu.make_async_remote_copy(
        flat.at[pl.ds(pl.multiple_of((1 - core) * HALF, HALF), HALF)], flat_half, half_ssem, half_rsem,
        device_id=(g + 1 - 2 * core, m), device_id_type=MESH,
    )
    half_copy.start()
    half_copy.wait()
    own_half = flat[pl.ds(pl.multiple_of(core * HALF, HALF), HALF), :]
    flat_out[...] = (own_half + flat_half[...]).astype(bf16)

    own_copy.wait()
    pltpu.make_async_copy(ids_send.at[pl.ds(0, 127)], ids_recv.at[pl.ds(0, 127)], ids_ssem).wait()
    pltpu.make_async_copy(send_main.at[pl.ds(0, 127)], recv_main.at[pl.ds(0, 127)], g_ssem).wait()
    pltpu.make_async_copy(send_extra.at[pl.ds(0, 127)], recv_extra.at[pl.ds(0, 127)], g_esem).wait()
    pltpu.make_async_copy(send_main.at[pl.ds(1, 127)], gmain_out.at[pl.ds(1, 127)], gm_rsem).wait()
    pltpu.make_async_copy(send_extra.at[pl.ds(0, 127)], gextra_out.at[pl.ds(0, 127)], ge_rsem).wait()


WAYS = 4
BATCH = 32
CHUNK = 512


def scatter_kernel(ids_ref, gmain_hbm, gextra_ref, table_hbm, new_hbm, change_hbm,
                   sums, stage, gmain, table, change, gmain_sem, table_sem, new_sem, change_sem):
    def gmain_copy(q):
        at = pl.ds(q * SERVE, SERVE)
        return pltpu.make_async_copy(gmain_hbm.at[at], gmain.at[at], gmain_sem.at[q])

    for q in range(N_DEV // SERVE):
        gmain_copy(q).start()
    table_copy = pltpu.make_async_copy(table_hbm, table, table_sem)
    table_copy.start()
    sums[...] = jnp.zeros_like(sums)

    def convert(s, c):
        stage[s, 0:MAIN, :] = gmain[s].astype(f32)
        stage[s, MAIN : MAIN + 8, :] = jnp.where(iota((8, 128), 0) == 0, gextra_ref[s], 0.0)
        stage[s, MAIN + 8 : 128, :] = jnp.zeros((24, 128), f32)
        return c

    def source(s, c):
        count = ids_ref[s, 0, 127]

        def batch(b, c):
            first = pl.multiple_of(b * BATCH, BATCH)
            for h in range(0, BATCH, WAYS):
                rows = [ids_ref[s, 0, first + h + i] for i in range(WAYS)]
                total = [
                    sums[i, pl.ds(rows[i], 1), :] + stage[s, pl.ds(first + h + i, 1), :] for i in range(WAYS)
                ]
                for i in range(WAYS):
                    sums[i, pl.ds(rows[i], 1), :] = total[i]
            return c

        lax.fori_loop(0, (count + BATCH - 1) // BATCH, batch, 0)
        return c

    def chunk(q, c):
        gmain_copy(q).wait()
        lax.fori_loop(0, SERVE, lambda i, c: convert(q * SERVE + i, c), 0, unroll=4)
        lax.fori_loop(q * SERVE, q * SERVE + SERVE, source, 0)
        return c

    lax.fori_loop(0, N_DEV // SERVE, chunk, 0)
    table_copy.wait()

    def finish(b, c):
        start = pl.multiple_of(b * CHUNK, CHUNK)
        for r in range(0, CHUNK, 64):
            at = pl.ds(pl.multiple_of(start + r, 64), 64)
            total = sums[0, at, :]
            for i in range(1, WAYS):
                total = total + sums[i, at, :]
            total = -embed_rate * total
            table[at, :] = table[at, :] + total
            change[at, :] = total.astype(bf16)
        at = pl.ds(start, CHUNK)
        pltpu.make_async_copy(table.at[at], new_hbm.at[at], new_sem).start()
        pltpu.make_async_copy(change.at[at], change_hbm.at[at], change_sem).start()
        return c

    lax.fori_loop(0, ROWS_DEV // CHUNK, finish, 0)
    pltpu.make_async_copy(table, new_hbm, new_sem).wait()
    pltpu.make_async_copy(change, change_hbm, change_sem).wait()


def member_peer(k, sign):
    x, y = lax.axis_index("member") // 4, lax.axis_index("member") % 4
    kx = k % 4
    ky = (k // 4 + kx) % 4
    if sign < 0:
        kx, ky = (4 - kx) % 4, (4 - ky) % 4
    return ((x + kx) % 4) * 4 + (y + ky) % 4


CUT = (5, 9, 13)


def parity_kernel(
    change_ref, parity_ref, flat_ref,
    new_ref, all_z,
    pieces, part_z, sum_z, part_xy, sum_xy, all_xy,
    ch_ssem, ch_rsem, rz_ssem, rz_rsem, rx_ssem, rx_rsem, ax_ssem, ax_rsem, az_ssem, az_rsem, ac_ssem, ac_rsem,
):
    g, m = lax.axis_index("group"), lax.axis_index("member")
    barrier = pltpu.get_barrier_semaphore()
    for j in range(1, N_GROUP):
        pl.semaphore_signal(barrier, 1, device_id=((g + j) % N_GROUP, m), device_id_type=MESH)
    for k in range(1, N_MEMBER):
        pl.semaphore_signal(barrier, 1, device_id=(g, member_peer(k, 1)), device_id_type=MESH)
    pl.semaphore_wait(barrier, N_GROUP - 1 + N_MEMBER - 1)

    def remote(src, dst, ssem, rsem, to):
        return pltpu.make_async_remote_copy(src, dst, ssem, rsem, device_id=to, device_id_type=MESH)

    rows = ROWS_DEV // N_MEMBER

    def change_copy(k):
        to = member_peer(k, 1)
        return remote(
            change_ref.at[pl.ds(pl.multiple_of(to * rows, rows), rows)], pieces.at[k], ch_ssem.at[k], ch_rsem.at[k],
            (g, to),
        )

    z, core = g // 2, g % 2

    def rz_copy(j):
        to = (z + j) % 4
        return remote(
            flat_ref.at[pl.ds(pl.multiple_of(to * PIECE, PIECE), PIECE)], part_z.at[j], rz_ssem.at[j], rz_rsem.at[j],
            (to * 2 + core, m),
        )

    def rx_copy(k):
        to = member_peer(k, 1)
        return remote(
            sum_z.at[pl.ds(pl.multiple_of(to * SMALL, SMALL), SMALL)], part_xy.at[k], rx_ssem.at[k], rx_rsem.at[k],
            (g, to),
        )

    def ax_copy(k):
        return remote(sum_xy, all_xy.at[m], ax_ssem.at[k], ax_rsem.at[k], (g, member_peer(k, 1)))

    place = core * 4 + z

    def az_copy(j):
        return remote(
            all_z.at[place], all_z.at[place], az_ssem.at[j], az_rsem.at[j], ((z + j) % 4 * 2 + core, m)
        )

    def across_copy(j):
        slot = core * 4 + (z + 4 - j) % 4
        return remote(
            all_z.at[slot], all_z.at[slot], ac_ssem.at[j], ac_rsem.at[j], (z * 2 + 1 - core, m)
        )

    for j in range(1, 4):
        rz_copy(j).start()
    for k in range(1, CUT[0]):
        change_copy(k).start()
    total = flat_ref[pl.ds(pl.multiple_of(z * PIECE, PIECE), PIECE), :].astype(f32)
    for j in range(1, 4):
        rz_copy(j).wait()
        total = total + part_z[j].astype(f32)
    sum_z[...] = total
    for k in range(1, N_MEMBER):
        rx_copy(k).start()
    for k in range(CUT[0], CUT[1]):
        change_copy(k).start()
    total = sum_z[pl.ds(pl.multiple_of(m * SMALL, SMALL), SMALL), :]
    for k in range(1, N_MEMBER):
        rx_copy(k).wait()
        total = total + part_xy[k]
    sum_xy[...] = total
    for k in range(1, N_MEMBER):
        ax_copy(k).start()
    for k in range(CUT[1], CUT[2]):
        change_copy(k).start()
    all_xy[m] = total
    for k in range(1, N_MEMBER):
        ax_copy(k).wait()
    all_z[place] = all_xy[...].reshape(PIECE, E).astype(bf16)
    for j in range(1, 4):
        az_copy(j).start()
    across_copy(0).start()
    for k in range(CUT[2], N_MEMBER):
        change_copy(k).start()

    def weights(k):
        source = member_peer(k, -1).astype(f32) / N_MEMBER
        one = jnp.ones((1, 128), f32)
        return 1.0 / (one + source), 1.0 / (one * 2.0 + source)

    for j in range(1, 4):
        az_copy(j).wait_recv()
        across_copy(j).start()

    def add(k, part_of, base_of):
        first, second = weights(k)

        def step(b, c):
            at = pl.ds(pl.multiple_of(b * 64, 64), 64)
            part = part_of(b).astype(f32)
            new_ref[at, 0:128] = base_of[at, 0:128] + first * part
            new_ref[at, 128:256] = base_of[at, 128:256] + second * part
            return c

        lax.fori_loop(0, rows // 64, step, 0)

    add(0, lambda b: change_ref[pl.ds(pl.multiple_of(m * rows + b * 64, 64), 64), :], parity_ref)
    for k in range(1, N_MEMBER):
        change_copy(k).wait()
        add(k, lambda b: pieces[k, pl.ds(pl.multiple_of(b * 64, 64), 64), :], new_ref)

    for j in range(4):
        if j > 0:
            az_copy(j).wait_send()
        across_copy(j).wait()


def unpack_kernel(
    parity_hbm, all_z_hbm, new_hbm, g0_ref, g1_ref, g2_ref, gt0_ref, gt1_ref, all_z, parity_sem, all_z_sem
):
    parity_copy = pltpu.make_async_copy(parity_hbm, new_hbm, parity_sem)
    parity_copy.start()
    all_z_copy = pltpu.make_async_copy(all_z_hbm, all_z, all_z_sem)
    all_z_copy.start()
    all_z_copy.wait()
    for c in range(8):
        gt0_ref[:, 128 * c : 128 * (c + 1)] = piece_rows(all_z, OFF_TOP0 + c * TOP0_ROWS, TOP0_ROWS)[0:TOPIN]
    for c in range(2):
        g1_ref[:, 128 * c : 128 * (c + 1)] = piece_rows(all_z, OFF_BOT1 + c * BOT1, BOT1)
    g2_ref[...] = piece_rows(all_z, OFF_BOT2, BOT2)
    for c in range(4):
        g0_ref[:, 128 * c : 128 * (c + 1)] = piece_rows(all_z, OFF_BOT0 + c * 16, 16)[0:DENSE]
    top1 = piece_rows(all_z, OFF_TOP1, 16)
    for c in range(8):
        gt1_ref[:, 128 * c : 128 * (c + 1)] = top1[c : c + 1, :]
    parity_copy.wait()


def piece_rows(ref, start, count):
    out = []
    while count > 0:
        p, at = start // PIECE, start % PIECE
        n = min(count, PIECE - at)
        out.append(ref[p, at : at + n, :].astype(f32))
        start, count = start + n, count - n
    return out[0] if len(out) == 1 else jnp.concatenate(out, axis=0)


def body(
    dense_in, lookup_owner, lookup_row, bag_length, logit_grad, table, parity,
    w_bottom0, w_bottom1, w_bottom2, w_top0, w_top1,
):
    owner = lookup_owner.transpose(1, 2, 0).reshape(NT * HOT, 128)
    row = lookup_row.transpose(1, 2, 0).reshape(NT * HOT, 128)
    vmem = pl.BlockSpec(memory_space=VM)
    anyw = pl.BlockSpec(memory_space=pl.ANY)
    smem = pl.BlockSpec(memory_space=pltpu.SMEM)
    dma = pltpu.SemaphoreType.DMA
    sds = jax.ShapeDtypeStruct
    ids, gmain, gextra, flat = pl.pallas_call(
        exchange_kernel,
        out_shape=(
            sds((N_DEV, 1, 128), i32),
            sds((N_DEV, MAIN, E), bf16),
            sds((N_DEV, 1, E), f32),
            sds((HALF, E), bf16),
        ),
        in_specs=[vmem] * 5 + [anyw] * 5 + [vmem],
        out_specs=(vmem, anyw, vmem, vmem),
        scratch_shapes=[
            VM((ROWS_DEV, E), f32),
            VM((N_DEV, 1, 128), i32),
            VM((N_DEV, 1, 128), i32),
            pltpu.SMEM((N_DEV, 1, 128), i32),
            VM((MAIN, E), f32),
            VM((N_DEV, MAIN, E), bf16),
            VM((N_DEV, 1, E), f32),
            VM((N_DEV, MAIN, E), bf16),
            VM((N_DEV, 1, E), f32),
            VM((32, 128, 256), bf16),
            VM((32, 512, 256), bf16),
            VM((N_DEV, MAIN, 128), i32),
            VM((128, 128), i32),
            VM((GROUP * MAIN, BAGS), bf16),
            VM((N_DEV, BAGS), bf16),
            VM((E, BAGS), f32),
            VM((BAGS, E), bf16),
            VM((256, TOPH), f32),
            VM((256, 128), f32),
            VM((TOPH, 128), f32),
            VM((TOPH, 128), f32),
            dma, dma((N_DEV // SERVE,)), dma, dma((N_DEV // SERVE,)), dma, dma,
            dma((N_DEV // GROUP,)), dma((N_DEV // GROUP,)),
            dma, dma, dma, dma,
            VM((FLAT, E), f32),
            VM((HALF, E), f32),
            dma, dma, dma,
            VM((DENSE, BOT1), f32),
            VM((BOT1, BOT2), f32),
            VM((BOT2, E), f32),
            VM((TOPIN, TOPH), f32),
            dma((4,)),
        ],
        compiler_params=pltpu.CompilerParams(
            collective_id=0, has_side_effects=True, vmem_limit_bytes=56 << 20
        ),
    )(
        owner, row, bag_length.T, dense_in.T, logit_grad.reshape(1, 128), table,
        w_bottom0, w_bottom1, w_bottom2, w_top0, w_top1.reshape(1, TOPH),
    )
    new_table, change = pl.pallas_call(
        scatter_kernel,
        out_shape=(sds((ROWS_DEV, E), f32), sds((ROWS_DEV, E), bf16)),
        in_specs=[smem, anyw, vmem, anyw],
        out_specs=(anyw, anyw),
        scratch_shapes=[
            VM((WAYS, ROWS_DEV, E), f32),
            VM((N_DEV, 128, E), f32),
            VM((N_DEV, MAIN, E), bf16),
            VM((ROWS_DEV, E), f32),
            VM((ROWS_DEV, E), bf16),
            dma((N_DEV // SERVE,)), dma, dma, dma,
        ],
        compiler_params=pltpu.CompilerParams(vmem_limit_bytes=56 << 20),
    )(ids, gmain, gextra, table)
    parity_sum, all_z = pl.pallas_call(
        parity_kernel,
        out_shape=(sds(parity.shape, f32), sds((N_GROUP, PIECE, E), bf16)),
        in_specs=[vmem] * 3,
        out_specs=(vmem, vmem),
        scratch_shapes=[
            VM((N_MEMBER, ROWS_DEV // N_MEMBER, E), bf16),
            VM((4, PIECE, E), bf16),
            VM((PIECE, E), f32),
            VM((N_MEMBER, SMALL, E), f32),
            VM((SMALL, E), f32),
            VM((N_MEMBER, SMALL, E), f32),
            dma((N_MEMBER,)), dma((N_MEMBER,)), dma((4,)), dma((4,)),
            dma((N_MEMBER,)), dma((N_MEMBER,)), dma((N_MEMBER,)), dma((N_MEMBER,)),
            dma((4,)), dma((4,)), dma((4,)), dma((4,)),
        ],
        compiler_params=pltpu.CompilerParams(
            collective_id=1, has_side_effects=True, vmem_limit_bytes=56 << 20
        ),
    )(change, parity, flat)
    new_parity, g0, g1, g2, gt0, gt1 = pl.pallas_call(
        unpack_kernel,
        out_shape=(
            sds(parity.shape, f32),
            sds((DENSE, BOT1), f32),
            sds((BOT1, BOT2), f32),
            sds((BOT2, E), f32),
            sds((TOPIN, TOPH), f32),
            sds((1, TOPH), f32),
        ),
        in_specs=[anyw] * 2,
        out_specs=(anyw,) + (vmem,) * 5,
        scratch_shapes=[VM((N_GROUP, PIECE, E), bf16), dma, dma],
        compiler_params=pltpu.CompilerParams(vmem_limit_bytes=60 << 20),
    )(parity_sum, all_z)
    return new_table, new_parity, g0, g1, g2, gt0, gt1.reshape(TOPH)


def solution(mesh):
    rows = P(("group", "member"), None)
    cube = P(("group", "member"), None, None)
    in_specs = (rows, cube, cube, rows, P(("group", "member")), rows, rows, P(), P(), P(), P(), P())
    out_specs = (rows, rows, P(), P(), P(), P(), P())
    return jax.shard_map(body, mesh=mesh, in_specs=in_specs, out_specs=out_specs, check_vma=False)
```

```python
import functools

import jax
import jax.numpy as jnp
import numpy as np
from jax import lax
from jax.experimental import pallas as pl
from jax.experimental.pallas import tpu as pltpu
from jax.sharding import PartitionSpec as P

embed_rate = 1.0

MESH = pl.DeviceIdType.MESH
N_DEV = 128
N_GROUP = 8
N_MEMBER = 16
E = 128
ROWS_DEV = 8192
NT = 8
HOT = 8
BAGS = 1024
MAIN = 96
SERVE = 16
GROUP = 8
PAIRS = [(i, j) for i in range(9) for j in range(i)]
BOT1, BOT2, TOPH, DENSE, TOPIN = 512, 256, 1024, 13, 164

TOP0_ROWS = 176
OFF_TOP0 = 0
OFF_BOT1 = 8 * TOP0_ROWS
OFF_BOT2 = OFF_BOT1 + 2 * BOT1
OFF_BOT0 = OFF_BOT2 + BOT2
OFF_TOP1 = OFF_BOT0 + 4 * 16
FLAT = 3072
HALF = FLAT // 2
PIECE = FLAT // N_GROUP
SMALL = PIECE // N_MEMBER

f32, bf16, i32 = jnp.float32, jnp.bfloat16, jnp.int32
VM = pltpu.VMEM


def iota(shape, dim):
    return lax.broadcasted_iota(i32, shape, dim)


def dot(a, b, dims):
    return lax.dot_general(a, b, (dims, ((), ())), preferred_element_type=f32)


NN = ((1,), (0,))
NT_ = ((1,), (1,))
TN = ((0,), (0,))


def halves(a):
    hi = a.astype(bf16)
    return hi, (a - hi.astype(f32)).astype(bf16)


def dot3(a, b, dims):
    return dot(a[0], b[0], dims) + (dot(a[0], b[1], dims) + dot(a[1], b[0], dims))


def coords():
    g, m = lax.axis_index("group"), lax.axis_index("member")
    return g // 2, g % 2, m // 4, m % 4


def peer(k):
    z, c, x, y = coords()
    kx = k % 4
    ky = (k // 4 + kx) % 4
    kz = (k // 16 + ky) % 4
    kc = k // 64
    return ((z + kz) % 4) * 2 + (c + kc) % 2, ((x + kx) % 4) * 4 + (y + ky) % 4


def origin(k):
    z, c, x, y = coords()
    kx = k % 4
    ky = (k // 4 + kx) % 4
    kz = (k // 16 + ky) % 4
    kc = k // 64
    return ((z + 4 - kz) % 4) * 2 + (c + 2 - kc) % 2, ((x + 4 - kx) % 4) * 4 + (y + 4 - ky) % 4


def each_peer(act):
    z, c, x, y = coords()
    member = [((x + r % 4) % 4) * 4 + (y + (r // 4 + r % 4) % 4) % 4 for r in range(16)]

    def sixteen(a, first):
        group = [((z + a + ky) % 4) * 2 + (c + a // 4) % 2 for ky in range(4)]
        for r in range(first, 16):
            act(a * 16 + r, (group[(r // 4 + r % 4) % 4], member[r]))

    sixteen(0, 1)

    def loop(a, carry):
        sixteen(a, 0)
        return carry

    lax.fori_loop(1, 8, loop, 0)


def sigmoid(v):
    return 1.0 / (1.0 + jnp.exp(-v))


def exchange_kernel(
    own_ref, row_ref, len_ref, x_ref, lg_ref, table_hbm, w0_hbm, w1_hbm, w2_hbm, wt0_hbm, wt1_ref,
    ids_out, gmain_out, gextra_out, flat_out,
    table_v, ids_send, ids_recv, ids_smem, stage, send_main, send_extra, recv_main, recv_extra,
    hits, vals, bag_of, bag_extra, st, st_extra, pooled, pg, wt0_p, top_in, hid, dup,
    table_sem, smem_sem, ids_ssem, ids_rsem, row_ssem, row_esem, rowm_rsem, rowe_rsem,
    g_ssem, g_esem, gm_rsem, ge_rsem, flat, flat_half, own_sem, half_ssem, half_rsem,
    w0_ref, w1_ref, w2_ref, wt0_ref, w_sem,
):
    g, m = lax.axis_index("group"), lax.axis_index("member")
    me = g * N_MEMBER + m

    table_copy = pltpu.make_async_copy(table_hbm, table_v, table_sem)
    table_copy.start()
    barrier = pltpu.get_barrier_semaphore()
    weight_copies = [
        pltpu.make_async_copy(src, dst, w_sem.at[i])
        for i, (src, dst) in enumerate([(w0_hbm, w0_ref), (w1_hbm, w1_ref), (w2_hbm, w2_ref), (wt0_hbm, wt0_ref)])
    ]
    for copy in weight_copies:
        copy.start()

    each_peer(lambda k, to: pl.semaphore_signal(barrier, 1, device_id=to, device_id_type=MESH))

    upper = (iota((256, 384), 0) < iota((256, 384), 1)).astype(bf16)
    dev_of = iota((128, 256), 0)
    lane = iota((1, 128), 1)
    bag_lo = (jnp.concatenate([lane, lane], axis=1) + 128).astype(f32).astype(bf16)

    def place(j, count):
        t = j // 4
        h = (2 * j) % 8
        length = len_ref[pl.ds(t, 1), :]
        own = jnp.concatenate([own_ref[pl.ds(2 * j, 1), :], own_ref[pl.ds(2 * j + 1, 1), :]], axis=1)
        row = jnp.concatenate([row_ref[pl.ds(2 * j, 1), :], row_ref[pl.ds(2 * j + 1, 1), :]], axis=1)
        own = jnp.where(jnp.concatenate([h < length, h + 1 < length], axis=1), own, -1)
        hit = (own == dev_of).astype(f32)
        hit_b = hit.astype(bf16)
        ranks = dot(hit_b, upper, NN)
        before = ranks[:, 0:256] + jnp.concatenate([count, count], axis=1)
        pos = jnp.sum(before * hit, axis=0, keepdims=True).astype(i32)
        at = (pos == dev_of).astype(f32).astype(bf16)
        hits[j] = hit_b
        vals[j, 0:128, :] = at * (row // 32).astype(f32).astype(bf16)
        vals[j, 128:256, :] = at * (row % 32 * 8 + t).astype(f32).astype(bf16)
        vals[j, 256:384, :] = at * bag_lo
        return count + ranks[:, 256:384]

    count = lax.fori_loop(0, 32, place, jnp.zeros((128, 128), f32), unroll=4)
    acc = dot(vals[0], hits[0], NT_)
    for j in range(1, 32):
        acc = acc + dot(vals[j], hits[j], NT_)
    mixed = acc[128:256].astype(i32)
    ids = (acc[0:128] * 32.0 + (mixed // 8).astype(f32)).T
    ids = jnp.where(iota((128, 128), 1) == 127, count, ids).astype(i32)
    for d in range(N_DEV):
        ids_send[d] = ids[d : d + 1, :]
    sample = acc[256:384] - 128.0
    bag = jnp.where(sample >= 0.0, (mixed % 8).astype(f32) * 128.0 + sample, -1.0)
    pl.semaphore_wait(barrier, N_DEV - 1)

    def send_ids(k, to):
        pltpu.make_async_remote_copy(
            ids_send.at[to[0] * N_MEMBER + to[1]], ids_recv.at[k], ids_ssem, ids_rsem.at[k // SERVE],
            device_id=to, device_id_type=MESH,
        ).start()

    each_peer(send_ids)
    ids_recv[0] = ids_send[me]

    def take_ids(c, count):
        pltpu.make_async_copy(
            ids_send.at[pl.ds(0, count)], ids_recv.at[pl.ds(0, count)], ids_rsem.at[c]
        ).wait()
        at = pl.ds(c * SERVE, SERVE)
        ids_recv[at] = jnp.clip(ids_recv[at], 0, ROWS_DEV - 1)
        smem_copy(c).start()

    def smem_copy(c):
        at = pl.ds(c * SERVE, SERVE)
        return pltpu.make_async_copy(ids_recv.at[at], ids_smem.at[at], smem_sem.at[c])

    take_ids(0, SERVE - 1)
    table_copy.wait()

    def gather(slot):
        for i in range(MAIN):
            stage[i : i + 1, :] = table_v[pl.ds(ids_smem[slot, 0, i] & (ROWS_DEV - 1), 1), :]
        send_main[slot] = stage[...].astype(bf16)
        send_extra[slot] = table_v[pl.ds(ids_smem[slot, 0, MAIN] & (ROWS_DEV - 1), 1), :]

    def rows_copies(k):
        to = origin(k)
        return (
            pltpu.make_async_remote_copy(
                send_main.at[k], recv_main.at[k], row_ssem, rowm_rsem.at[k // GROUP],
                device_id=to, device_id_type=MESH,
            ),
            pltpu.make_async_remote_copy(
                send_extra.at[k], recv_extra.at[k], row_esem, rowe_rsem.at[k // GROUP],
                device_id=to, device_id_type=MESH,
            ),
        )

    def serve(k, c):
        gather(k)
        for copy in rows_copies(k):
            copy.start()
        return c

    def serve_chunk(c, carry):
        take_ids(c + 1, SERVE)
        smem_copy(c).wait()
        lax.fori_loop(jnp.maximum(c * SERVE, 1), c * SERVE + SERVE, serve, 0)
        return carry

    lax.fori_loop(0, N_DEV // SERVE - 1, serve_chunk, 0)
    smem_copy(N_DEV // SERVE - 1).wait()
    lax.fori_loop(N_DEV - SERVE, N_DEV, serve, 0)
    gather(0)
    recv_main[0] = send_main[0]
    recv_extra[0] = send_extra[0]

    bag_i = bag.astype(i32)
    for d in range(N_DEV):
        bag_of[d] = jnp.broadcast_to(bag_i[0:MAIN, d : d + 1], (MAIN, 128))
    bag_t = bag.T.astype(i32)
    bag_extra[...] = jnp.broadcast_to(bag_t[:, MAIN : MAIN + 1], (128, 128))

    for copy in weight_copies:
        copy.wait()

    top_in[...] = jnp.zeros_like(top_in)
    top_in[0:DENSE, :] = x_ref[...]
    x_pad = top_in[0:128, :]
    x_h = halves(x_pad)
    w0_t = jnp.concatenate([w0_ref[...], jnp.zeros((128 - DENSE, BOT1), f32)], axis=0).T
    w0_th = halves(w0_t)
    h1p = dot3(w0_th, x_h, NN)
    s1 = sigmoid(h1p)
    h1_h = halves(h1p * s1)
    d1 = s1 * (1.0 + h1p * (1.0 - s1))
    w1_h = halves(w1_ref[...])
    w1_th = halves(w1_ref[...].T)
    h2p = dot3(w1_th, h1_h, NN)
    s2 = sigmoid(h2p)
    h2_h = halves(h2p * s2)
    d2 = s2 * (1.0 + h2p * (1.0 - s2))
    w2_h = halves(w2_ref[...])
    w2_th = halves(w2_ref[...].T)
    bp = dot3(w2_th, h2_h, NN)
    s3 = sigmoid(bp)
    bottom = bp * s3
    d3 = s3 * (1.0 + bp * (1.0 - s3))
    top_in[0:128, :] = bottom
    wt0_p[...] = jnp.zeros_like(wt0_p)
    wt0_p[0:TOPIN, :] = wt0_ref[...]
    wt0_h = halves(wt0_p[...])
    wt0_th = halves(wt0_p[...].T)

    def one_hot(bags):
        return jnp.concatenate(
            [(bags == iota((1, 128), 1) + 128 * t).astype(f32).astype(bf16) for t in range(NT)], axis=1
        )

    def pool_main(q):
        for i in range(GROUP):
            from_g, from_m = peer(q * GROUP + i)
            st[pl.ds(i * MAIN, MAIN), :] = one_hot(bag_of[from_g * N_MEMBER + from_m])
            hid[pl.ds(from_g * N_MEMBER + from_m, 1), :] = recv_extra[q * GROUP + i]
        rows = recv_main[pl.ds(q * GROUP, GROUP)].reshape(GROUP * MAIN, E)
        pooled[...] += dot(rows, st[...], TN)

    def wait_rows(q, count):
        pltpu.make_async_copy(
            send_main.at[pl.ds(0, count)], recv_main.at[pl.ds(0, count)], rowm_rsem.at[q]
        ).wait()
        pltpu.make_async_copy(
            send_extra.at[pl.ds(0, count)], recv_extra.at[pl.ds(0, count)], rowe_rsem.at[q]
        ).wait()

    st_extra[...] = one_hot(bag_extra[...])
    pooled[...] = jnp.zeros_like(pooled)
    wait_rows(0, GROUP - 1)
    pool_main(0)

    def pool_step(q, c):
        wait_rows(q, GROUP)
        pool_main(q)
        return c

    lax.fori_loop(1, N_DEV // GROUP, pool_step, 0)
    pooled[...] += dot(hid[0:128, :].astype(bf16), st_extra[...], TN)

    z = [bottom] + [pooled[:, 128 * t : 128 * (t + 1)] for t in range(NT)]
    for n, (i, j) in enumerate(PAIRS):
        top_in[128 + n : 129 + n, :] = jnp.sum(z[i] * z[j], axis=0, keepdims=True)
    top_h = halves(top_in[...])
    up = dot3(wt0_th, top_h, NN)
    su = sigmoid(up)
    hid[...] = up * su
    lg = lg_ref[...]
    wt1_col = jnp.broadcast_to(wt1_ref[...], (128, TOPH)).T
    dup[...] = wt1_col * lg * (su * (1.0 + up * (1.0 - su)))
    dup_h = halves(dup[...])
    d_top = dot3(wt0_h, dup_h, NN)
    d_pair = {}
    for n, (i, j) in enumerate(PAIRS):
        d_pair[i, j] = d_pair[j, i] = d_top[128 + n : 129 + n, :]
    d_z = []
    for i in range(9):
        total = None
        for j in range(9):
            if j != i:
                term = d_pair[i, j] * z[j]
                total = term if total is None else total + term
        d_z.append(total)
        if i > 0:
            pg[128 * (i - 1) : 128 * i, :] = total.T.astype(bf16)

    pltpu.make_async_copy(send_main.at[pl.ds(0, 127)], recv_main.at[pl.ds(0, 127)], row_ssem).wait()
    pltpu.make_async_copy(send_extra.at[pl.ds(0, 127)], recv_extra.at[pl.ds(0, 127)], row_esem).wait()

    def main_copy(k):
        return pltpu.make_async_remote_copy(
            send_main.at[k], gmain_out.at[k], g_ssem, gm_rsem, device_id=peer(k), device_id_type=MESH
        )

    def send_grad_extra(k, to):
        pltpu.make_async_remote_copy(
            send_extra.at[to[0] * N_MEMBER + to[1]], gextra_out.at[k], g_esem, ge_rsem,
            device_id=to, device_id_type=MESH,
        ).start()

    def expand(q):
        for i in range(GROUP):
            to_g, to_m = peer(q * GROUP + i)
            st[pl.ds(i * MAIN, MAIN), :] = one_hot(bag_of[to_g * N_MEMBER + to_m])
        grads = dot(st[...], pg[...], NN).astype(bf16)
        send_main[pl.ds(q * GROUP, GROUP)] = grads.reshape(GROUP, MAIN, E)

    def start_grads(k, c):
        main_copy(k).start()
        return c

    expand(0)
    lax.fori_loop(1, GROUP, start_grads, 0)

    def expand_step(q, c):
        expand(q)
        lax.fori_loop(q * GROUP, q * GROUP + GROUP, start_grads, 0)
        return c

    lax.fori_loop(1, N_DEV // GROUP // 2, expand_step, 0)
    extra = dot(st_extra[...], pg[...], NN)
    for d in range(N_DEV):
        send_extra[d] = extra[d : d + 1, :]
    each_peer(send_grad_extra)
    lax.fori_loop(N_DEV // GROUP // 2, N_DEV // GROUP, expand_step, 0)
    own_copy = pltpu.make_async_copy(send_main.at[0], gmain_out.at[0], own_sem)
    own_copy.start()
    gextra_out[0] = send_extra[me]
    ids_out[...] = ids_recv[...]

    flat[...] = jnp.zeros_like(flat)
    g_t0 = dot3(top_h, dup_h, NT_)
    for c in range(8):
        flat[OFF_TOP0 + c * TOP0_ROWS : OFF_TOP0 + (c + 1) * TOP0_ROWS, :] = g_t0[
            0:TOP0_ROWS, 128 * c : 128 * (c + 1)
        ]
    lg_h = halves(jnp.broadcast_to(lg, (8, 128)))
    g_t1 = dot3(lg_h, halves(hid[...]), NT_)[0:1]
    g_t1 = jnp.concatenate([g_t1[:, 128 * c : 128 * (c + 1)] for c in range(8)], axis=0)
    flat[OFF_TOP1 : OFF_TOP1 + 16, :] = jnp.concatenate([g_t1, g_t1], axis=0)
    d_bp = halves((d_top[0:128] + d_z[0]) * d3)
    flat[OFF_BOT2 : OFF_BOT2 + BOT2, :] = dot3(h2_h, d_bp, NT_)
    d_h2p = halves(dot3(w2_h, d_bp, NN) * d2)
    g_b1 = dot3(h1_h, d_h2p, NT_)
    for c in range(2):
        flat[OFF_BOT1 + c * BOT1 : OFF_BOT1 + (c + 1) * BOT1, :] = g_b1[:, 128 * c : 128 * (c + 1)]
    d_h1p = halves(dot3(w1_h, d_h2p, NN) * d1)
    g_b0 = dot3(x_h, d_h1p, NT_)[0:16]
    for c in range(4):
        flat[OFF_BOT0 + c * 16 : OFF_BOT0 + (c + 1) * 16, :] = g_b0[:, 128 * c : 128 * (c + 1)]

    core = g % 2
    half_copy = pltpu.make_async_remote_copy(
        flat.at[pl.ds(pl.multiple_of((1 - core) * HALF, HALF), HALF)], flat_half, half_ssem, half_rsem,
        device_id=(g + 1 - 2 * core, m), device_id_type=MESH,
    )
    half_copy.start()
    half_copy.wait()
    own_half = flat[pl.ds(pl.multiple_of(core * HALF, HALF), HALF), :]
    flat_out[...] = (own_half + flat_half[...]).astype(bf16)

    own_copy.wait()
    pltpu.make_async_copy(ids_send.at[pl.ds(0, 127)], ids_recv.at[pl.ds(0, 127)], ids_ssem).wait()
    pltpu.make_async_copy(send_main.at[pl.ds(0, 127)], recv_main.at[pl.ds(0, 127)], g_ssem).wait()
    pltpu.make_async_copy(send_extra.at[pl.ds(0, 127)], recv_extra.at[pl.ds(0, 127)], g_esem).wait()
    pltpu.make_async_copy(send_main.at[pl.ds(1, 127)], gmain_out.at[pl.ds(1, 127)], gm_rsem).wait()
    pltpu.make_async_copy(send_extra.at[pl.ds(0, 127)], gextra_out.at[pl.ds(0, 127)], ge_rsem).wait()


WAYS = 4
BATCH = 32
CHUNK = 512


def scatter_kernel(ids_ref, gmain_hbm, gextra_ref, table_hbm, new_hbm, change_hbm,
                   sums, stage, gmain, table, change, gmain_sem, table_sem, new_sem, change_sem):
    def gmain_copy(q):
        at = pl.ds(q * SERVE, SERVE)
        return pltpu.make_async_copy(gmain_hbm.at[at], gmain.at[at], gmain_sem.at[q])

    for q in range(N_DEV // SERVE):
        gmain_copy(q).start()
    table_copy = pltpu.make_async_copy(table_hbm, table, table_sem)
    table_copy.start()
    sums[...] = jnp.zeros_like(sums)

    def convert(s, c):
        stage[s, 0:MAIN, :] = gmain[s].astype(f32)
        stage[s, MAIN : MAIN + 8, :] = jnp.where(iota((8, 128), 0) == 0, gextra_ref[s], 0.0)
        stage[s, MAIN + 8 : 128, :] = jnp.zeros((24, 128), f32)
        return c

    def source(s, c):
        count = ids_ref[s, 0, 127]

        def batch(b, c):
            first = pl.multiple_of(b * BATCH, BATCH)
            for h in range(0, BATCH, WAYS):
                rows = [ids_ref[s, 0, first + h + i] for i in range(WAYS)]
                total = [
                    sums[i, pl.ds(rows[i], 1), :] + stage[s, pl.ds(first + h + i, 1), :] for i in range(WAYS)
                ]
                for i in range(WAYS):
                    sums[i, pl.ds(rows[i], 1), :] = total[i]
            return c

        lax.fori_loop(0, (count + BATCH - 1) // BATCH, batch, 0)
        return c

    def chunk(q, c):
        gmain_copy(q).wait()
        lax.fori_loop(0, SERVE, lambda i, c: convert(q * SERVE + i, c), 0, unroll=4)
        lax.fori_loop(q * SERVE, q * SERVE + SERVE, source, 0)
        return c

    lax.fori_loop(0, N_DEV // SERVE, chunk, 0)
    table_copy.wait()

    def finish(b, c):
        start = pl.multiple_of(b * CHUNK, CHUNK)
        for r in range(0, CHUNK, 64):
            at = pl.ds(pl.multiple_of(start + r, 64), 64)
            total = sums[0, at, :]
            for i in range(1, WAYS):
                total = total + sums[i, at, :]
            total = -embed_rate * total
            table[at, :] = table[at, :] + total
            change[at, :] = total.astype(bf16)
        at = pl.ds(start, CHUNK)
        pltpu.make_async_copy(table.at[at], new_hbm.at[at], new_sem).start()
        pltpu.make_async_copy(change.at[at], change_hbm.at[at], change_sem).start()
        return c

    lax.fori_loop(0, ROWS_DEV // CHUNK, finish, 0)
    pltpu.make_async_copy(table, new_hbm, new_sem).wait()
    pltpu.make_async_copy(change, change_hbm, change_sem).wait()


def member_peer(k, sign):
    x, y = lax.axis_index("member") // 4, lax.axis_index("member") % 4
    kx = k % 4
    ky = (k // 4 + kx) % 4
    if sign < 0:
        kx, ky = (4 - kx) % 4, (4 - ky) % 4
    return ((x + kx) % 4) * 4 + (y + ky) % 4


CUT = (5, 9, 13)


def parity_kernel(
    change_ref, parity_ref, flat_ref,
    new_ref, all_z,
    pieces, part_z, sum_z, part_xy, sum_xy, all_xy,
    ch_ssem, ch_rsem, rz_ssem, rz_rsem, rx_ssem, rx_rsem, ax_ssem, ax_rsem, az_ssem, az_rsem, ac_ssem, ac_rsem,
):
    g, m = lax.axis_index("group"), lax.axis_index("member")
    barrier = pltpu.get_barrier_semaphore()
    for j in range(1, N_GROUP):
        pl.semaphore_signal(barrier, 1, device_id=((g + j) % N_GROUP, m), device_id_type=MESH)
    for k in range(1, N_MEMBER):
        pl.semaphore_signal(barrier, 1, device_id=(g, member_peer(k, 1)), device_id_type=MESH)
    pl.semaphore_wait(barrier, N_GROUP - 1 + N_MEMBER - 1)

    def remote(src, dst, ssem, rsem, to):
        return pltpu.make_async_remote_copy(src, dst, ssem, rsem, device_id=to, device_id_type=MESH)

    rows = ROWS_DEV // N_MEMBER

    def change_copy(k):
        to = member_peer(k, 1)
        return remote(
            change_ref.at[pl.ds(pl.multiple_of(to * rows, rows), rows)], pieces.at[k], ch_ssem.at[k], ch_rsem.at[k],
            (g, to),
        )

    z, core = g // 2, g % 2

    def rz_copy(j):
        to = (z + j) % 4
        return remote(
            flat_ref.at[pl.ds(pl.multiple_of(to * PIECE, PIECE), PIECE)], part_z.at[j], rz_ssem.at[j], rz_rsem.at[j],
            (to * 2 + core, m),
        )

    def rx_copy(k):
        to = member_peer(k, 1)
        return remote(
            sum_z.at[pl.ds(pl.multiple_of(to * SMALL, SMALL), SMALL)], part_xy.at[k], rx_ssem.at[k], rx_rsem.at[k],
            (g, to),
        )

    def ax_copy(k):
        return remote(sum_xy, all_xy.at[m], ax_ssem.at[k], ax_rsem.at[k], (g, member_peer(k, 1)))

    place = core * 4 + z

    def az_copy(j):
        return remote(
            all_z.at[place], all_z.at[place], az_ssem.at[j], az_rsem.at[j], ((z + j) % 4 * 2 + core, m)
        )

    def across_copy(j):
        slot = core * 4 + (z + 4 - j) % 4
        return remote(
            all_z.at[slot], all_z.at[slot], ac_ssem.at[j], ac_rsem.at[j], (z * 2 + 1 - core, m)
        )

    for j in range(1, 4):
        rz_copy(j).start()
    for k in range(1, CUT[0]):
        change_copy(k).start()
    total = flat_ref[pl.ds(pl.multiple_of(z * PIECE, PIECE), PIECE), :].astype(f32)
    for j in range(1, 4):
        rz_copy(j).wait()
        total = total + part_z[j].astype(f32)
    sum_z[...] = total
    for k in range(1, N_MEMBER):
        rx_copy(k).start()
    for k in range(CUT[0], CUT[1]):
        change_copy(k).start()
    total = sum_z[pl.ds(pl.multiple_of(m * SMALL, SMALL), SMALL), :]
    for k in range(1, N_MEMBER):
        rx_copy(k).wait()
        total = total + part_xy[k]
    sum_xy[...] = total
    for k in range(1, N_MEMBER):
        ax_copy(k).start()
    for k in range(CUT[1], CUT[2]):
        change_copy(k).start()
    all_xy[m] = total
    for k in range(1, N_MEMBER):
        ax_copy(k).wait()
    all_z[place] = all_xy[...].reshape(PIECE, E).astype(bf16)
    for j in range(1, 4):
        az_copy(j).start()
    across_copy(0).start()
    for k in range(CUT[2], N_MEMBER):
        change_copy(k).start()

    def weights(k):
        source = member_peer(k, -1).astype(f32) / N_MEMBER
        one = jnp.ones((1, 128), f32)
        return 1.0 / (one + source), 1.0 / (one * 2.0 + source)

    for j in range(1, 4):
        az_copy(j).wait_recv()
        across_copy(j).start()

    def add(k, part_of, base_of):
        first, second = weights(k)

        def step(b, c):
            at = pl.ds(pl.multiple_of(b * 64, 64), 64)
            part = part_of(b).astype(f32)
            new_ref[at, 0:128] = base_of[at, 0:128] + first * part
            new_ref[at, 128:256] = base_of[at, 128:256] + second * part
            return c

        lax.fori_loop(0, rows // 64, step, 0)

    add(0, lambda b: change_ref[pl.ds(pl.multiple_of(m * rows + b * 64, 64), 64), :], parity_ref)
    for k in range(1, N_MEMBER):
        change_copy(k).wait()
        add(k, lambda b: pieces[k, pl.ds(pl.multiple_of(b * 64, 64), 64), :], new_ref)

    for j in range(4):
        if j > 0:
            az_copy(j).wait_send()
        across_copy(j).wait()


def unpack_kernel(
    parity_hbm, all_z_hbm, new_hbm, g0_ref, g1_ref, g2_ref, gt0_ref, gt1_ref,
    all_z, parity, parity_sem, all_z_sem, new_sem,
):
    parity_copy = pltpu.make_async_copy(parity_hbm, parity, parity_sem)
    parity_copy.start()
    all_z_copy = pltpu.make_async_copy(all_z_hbm, all_z, all_z_sem)
    all_z_copy.start()
    parity_copy.wait()
    new_copy = pltpu.make_async_copy(parity, new_hbm, new_sem)
    new_copy.start()
    all_z_copy.wait()
    for c in range(8):
        gt0_ref[:, 128 * c : 128 * (c + 1)] = piece_rows(all_z, OFF_TOP0 + c * TOP0_ROWS, TOP0_ROWS)[0:TOPIN]
    for c in range(2):
        g1_ref[:, 128 * c : 128 * (c + 1)] = piece_rows(all_z, OFF_BOT1 + c * BOT1, BOT1)
    g2_ref[...] = piece_rows(all_z, OFF_BOT2, BOT2)
    for c in range(4):
        g0_ref[:, 128 * c : 128 * (c + 1)] = piece_rows(all_z, OFF_BOT0 + c * 16, 16)[0:DENSE]
    top1 = piece_rows(all_z, OFF_TOP1, 16)
    for c in range(8):
        gt1_ref[:, 128 * c : 128 * (c + 1)] = top1[c : c + 1, :]
    new_copy.wait()


def piece_rows(ref, start, count):
    out = []
    while count > 0:
        p, at = start // PIECE, start % PIECE
        n = min(count, PIECE - at)
        out.append(ref[p, at : at + n, :].astype(f32))
        start, count = start + n, count - n
    return out[0] if len(out) == 1 else jnp.concatenate(out, axis=0)


def body(
    dense_in, lookup_owner, lookup_row, bag_length, logit_grad, table, parity,
    w_bottom0, w_bottom1, w_bottom2, w_top0, w_top1,
):
    owner = lookup_owner.transpose(1, 2, 0).reshape(NT * HOT, 128)
    row = lookup_row.transpose(1, 2, 0).reshape(NT * HOT, 128)
    vmem = pl.BlockSpec(memory_space=VM)
    anyw = pl.BlockSpec(memory_space=pl.ANY)
    smem = pl.BlockSpec(memory_space=pltpu.SMEM)
    dma = pltpu.SemaphoreType.DMA
    sds = jax.ShapeDtypeStruct
    ids, gmain, gextra, flat = pl.pallas_call(
        exchange_kernel,
        out_shape=(
            sds((N_DEV, 1, 128), i32),
            sds((N_DEV, MAIN, E), bf16),
            sds((N_DEV, 1, E), f32),
            sds((HALF, E), bf16),
        ),
        in_specs=[vmem] * 5 + [anyw] * 5 + [vmem],
        out_specs=(vmem, anyw, vmem, vmem),
        scratch_shapes=[
            VM((ROWS_DEV, E), f32),
            VM((N_DEV, 1, 128), i32),
            VM((N_DEV, 1, 128), i32),
            pltpu.SMEM((N_DEV, 1, 128), i32),
            VM((MAIN, E), f32),
            VM((N_DEV, MAIN, E), bf16),
            VM((N_DEV, 1, E), f32),
            VM((N_DEV, MAIN, E), bf16),
            VM((N_DEV, 1, E), f32),
            VM((32, 128, 256), bf16),
            VM((32, 384, 256), bf16),
            VM((N_DEV, MAIN, 128), i32),
            VM((128, 128), i32),
            VM((GROUP * MAIN, BAGS), bf16),
            VM((N_DEV, BAGS), bf16),
            VM((E, BAGS), f32),
            VM((BAGS, E), bf16),
            VM((256, TOPH), f32),
            VM((256, 128), f32),
            VM((TOPH, 128), f32),
            VM((TOPH, 128), f32),
            dma, dma((N_DEV // SERVE,)), dma, dma((N_DEV // SERVE,)), dma, dma,
            dma((N_DEV // GROUP,)), dma((N_DEV // GROUP,)),
            dma, dma, dma, dma,
            VM((FLAT, E), f32),
            VM((HALF, E), f32),
            dma, dma, dma,
            VM((DENSE, BOT1), f32),
            VM((BOT1, BOT2), f32),
            VM((BOT2, E), f32),
            VM((TOPIN, TOPH), f32),
            dma((4,)),
        ],
        compiler_params=pltpu.CompilerParams(
            collective_id=0, has_side_effects=True, vmem_limit_bytes=56 << 20
        ),
    )(
        owner, row, bag_length.T, dense_in.T, logit_grad.reshape(1, 128), table,
        w_bottom0, w_bottom1, w_bottom2, w_top0, w_top1.reshape(1, TOPH),
    )
    new_table, change = pl.pallas_call(
        scatter_kernel,
        out_shape=(sds((ROWS_DEV, E), f32), sds((ROWS_DEV, E), bf16)),
        in_specs=[smem, anyw, vmem, anyw],
        out_specs=(anyw, anyw),
        scratch_shapes=[
            VM((WAYS, ROWS_DEV, E), f32),
            VM((N_DEV, 128, E), f32),
            VM((N_DEV, MAIN, E), bf16),
            VM((ROWS_DEV, E), f32),
            VM((ROWS_DEV, E), bf16),
            dma((N_DEV // SERVE,)), dma, dma, dma,
        ],
        compiler_params=pltpu.CompilerParams(vmem_limit_bytes=56 << 20),
    )(ids, gmain, gextra, table)
    parity_sum, all_z = pl.pallas_call(
        parity_kernel,
        out_shape=(sds(parity.shape, f32), sds((N_GROUP, PIECE, E), bf16)),
        in_specs=[vmem] * 3,
        out_specs=(vmem, vmem),
        scratch_shapes=[
            VM((N_MEMBER, ROWS_DEV // N_MEMBER, E), bf16),
            VM((4, PIECE, E), bf16),
            VM((PIECE, E), f32),
            VM((N_MEMBER, SMALL, E), f32),
            VM((SMALL, E), f32),
            VM((N_MEMBER, SMALL, E), f32),
            dma((N_MEMBER,)), dma((N_MEMBER,)), dma((4,)), dma((4,)),
            dma((N_MEMBER,)), dma((N_MEMBER,)), dma((N_MEMBER,)), dma((N_MEMBER,)),
            dma((4,)), dma((4,)), dma((4,)), dma((4,)),
        ],
        compiler_params=pltpu.CompilerParams(
            collective_id=1, has_side_effects=True, vmem_limit_bytes=56 << 20
        ),
    )(change, parity, flat)
    new_parity, g0, g1, g2, gt0, gt1 = pl.pallas_call(
        unpack_kernel,
        out_shape=(
            sds(parity.shape, f32),
            sds((DENSE, BOT1), f32),
            sds((BOT1, BOT2), f32),
            sds((BOT2, E), f32),
            sds((TOPIN, TOPH), f32),
            sds((1, TOPH), f32),
        ),
        in_specs=[anyw] * 2,
        out_specs=(anyw,) + (vmem,) * 5,
        scratch_shapes=[VM((N_GROUP, PIECE, E), bf16), VM(parity.shape, f32), dma, dma, dma],
        compiler_params=pltpu.CompilerParams(vmem_limit_bytes=60 << 20),
    )(parity_sum, all_z)
    return new_table, new_parity, g0, g1, g2, gt0, gt1.reshape(TOPH)


def solution(mesh):
    rows = P(("group", "member"), None)
    cube = P(("group", "member"), None, None)
    in_specs = (rows, cube, cube, rows, P(("group", "member")), rows, rows, P(), P(), P(), P(), P())
    out_specs = (rows, rows, P(), P(), P(), P(), P())
    return jax.shard_map(body, mesh=mesh, in_specs=in_specs, out_specs=out_specs, check_vma=False)
```

```python
import functools

import jax
import jax.numpy as jnp
import numpy as np
from jax import lax
from jax.experimental import pallas as pl
from jax.experimental.pallas import tpu as pltpu
from jax.sharding import PartitionSpec as P

embed_rate = 1.0

MESH = pl.DeviceIdType.MESH
N_DEV = 128
N_GROUP = 8
N_MEMBER = 16
E = 128
ROWS_DEV = 8192
NT = 8
HOT = 8
BAGS = 1024
MAIN = 96
SERVE = 16
GROUP = 8
PAIRS = [(i, j) for i in range(9) for j in range(i)]
BOT1, BOT2, TOPH, DENSE, TOPIN = 512, 256, 1024, 13, 164

TOP0_ROWS = 176
OFF_TOP0 = 0
OFF_BOT1 = 8 * TOP0_ROWS
OFF_BOT2 = OFF_BOT1 + 2 * BOT1
OFF_BOT0 = OFF_BOT2 + BOT2
OFF_TOP1 = OFF_BOT0 + 4 * 16
FLAT = 3072
HALF = FLAT // 2
PIECE = FLAT // N_GROUP
SMALL = PIECE // N_MEMBER

f32, bf16, i32 = jnp.float32, jnp.bfloat16, jnp.int32
VM = pltpu.VMEM


def iota(shape, dim):
    return lax.broadcasted_iota(i32, shape, dim)


def dot(a, b, dims):
    return lax.dot_general(a, b, (dims, ((), ())), preferred_element_type=f32)


NN = ((1,), (0,))
NT_ = ((1,), (1,))
TN = ((0,), (0,))


def halves(a):
    hi = a.astype(bf16)
    return hi, (a - hi.astype(f32)).astype(bf16)


def dot3(a, b, dims):
    return dot(a[0], b[0], dims) + (dot(a[0], b[1], dims) + dot(a[1], b[0], dims))


def coords():
    g, m = lax.axis_index("group"), lax.axis_index("member")
    return g // 2, g % 2, m // 4, m % 4


def peer(k):
    z, c, x, y = coords()
    kx = k % 4
    ky = (k // 4 + kx) % 4
    kz = (k // 16 + ky) % 4
    kc = k // 64
    return ((z + kz) % 4) * 2 + (c + kc) % 2, ((x + kx) % 4) * 4 + (y + ky) % 4


def origin(k):
    z, c, x, y = coords()
    kx = k % 4
    ky = (k // 4 + kx) % 4
    kz = (k // 16 + ky) % 4
    kc = k // 64
    return ((z + 4 - kz) % 4) * 2 + (c + 2 - kc) % 2, ((x + 4 - kx) % 4) * 4 + (y + 4 - ky) % 4


def each_peer(act):
    z, c, x, y = coords()
    member = [((x + r % 4) % 4) * 4 + (y + (r // 4 + r % 4) % 4) % 4 for r in range(16)]

    def sixteen(a, first):
        group = [((z + a + ky) % 4) * 2 + (c + a // 4) % 2 for ky in range(4)]
        for r in range(first, 16):
            act(a * 16 + r, (group[(r // 4 + r % 4) % 4], member[r]))

    sixteen(0, 1)

    def loop(a, carry):
        sixteen(a, 0)
        return carry

    lax.fori_loop(1, 8, loop, 0)


def sigmoid(v):
    return 1.0 / (1.0 + jnp.exp(-v))


def exchange_kernel(
    own_ref, row_ref, len_ref, x_ref, lg_ref, table_hbm, w0_hbm, w1_hbm, w2_hbm, wt0_hbm, wt1_ref,
    ids_out, gmain_out, gextra_out, flat_out,
    table_v, ids_send, ids_recv, ids_smem, stage, send_main, send_extra, recv_main, recv_extra,
    hits, vals, bag_of, bag_extra, st, st_extra, pooled, pg, wt0_p, top_in, hid, dup,
    table_sem, smem_sem, ids_ssem, ids_rsem, row_ssem, row_esem, rowm_rsem, rowe_rsem,
    g_ssem, g_esem, gm_rsem, ge_rsem, flat, flat_half, own_sem, half_ssem, half_rsem,
    w0_ref, w1_ref, w2_ref, wt0_ref, w_sem,
    flat_z, part_z, sum_z, part_xy, rz_ssem, rz_rsem, rx_ssem, rx_rsem,
):
    g, m = lax.axis_index("group"), lax.axis_index("member")
    me = g * N_MEMBER + m

    table_copy = pltpu.make_async_copy(table_hbm, table_v, table_sem)
    table_copy.start()
    barrier = pltpu.get_barrier_semaphore()
    weight_copies = [
        pltpu.make_async_copy(src, dst, w_sem.at[i])
        for i, (src, dst) in enumerate([(w0_hbm, w0_ref), (w1_hbm, w1_ref), (w2_hbm, w2_ref), (wt0_hbm, wt0_ref)])
    ]
    for copy in weight_copies:
        copy.start()

    each_peer(lambda k, to: pl.semaphore_signal(barrier, 1, device_id=to, device_id_type=MESH))

    upper = (iota((256, 384), 0) < iota((256, 384), 1)).astype(bf16)
    dev_of = iota((128, 256), 0)
    lane = iota((1, 128), 1)
    bag_lo = (jnp.concatenate([lane, lane], axis=1) + 128).astype(f32).astype(bf16)

    def place(j, count):
        t = j // 4
        h = (2 * j) % 8
        length = len_ref[pl.ds(t, 1), :]
        own = jnp.concatenate([own_ref[pl.ds(2 * j, 1), :], own_ref[pl.ds(2 * j + 1, 1), :]], axis=1)
        row = jnp.concatenate([row_ref[pl.ds(2 * j, 1), :], row_ref[pl.ds(2 * j + 1, 1), :]], axis=1)
        own = jnp.where(jnp.concatenate([h < length, h + 1 < length], axis=1), own, -1)
        hit = (own == dev_of).astype(f32)
        hit_b = hit.astype(bf16)
        ranks = dot(hit_b, upper, NN)
        before = ranks[:, 0:256] + jnp.concatenate([count, count], axis=1)
        pos = jnp.sum(before * hit, axis=0, keepdims=True).astype(i32)
        at = (pos == dev_of).astype(f32).astype(bf16)
        hits[j] = hit_b
        vals[j, 0:128, :] = at * (row // 32).astype(f32).astype(bf16)
        vals[j, 128:256, :] = at * (row % 32 * 8 + t).astype(f32).astype(bf16)
        vals[j, 256:384, :] = at * bag_lo
        return count + ranks[:, 256:384]

    count = lax.fori_loop(0, 32, place, jnp.zeros((128, 128), f32), unroll=4)
    acc = dot(vals[0], hits[0], NT_)
    for j in range(1, 32):
        acc = acc + dot(vals[j], hits[j], NT_)
    mixed = acc[128:256].astype(i32)
    ids = (acc[0:128] * 32.0 + (mixed // 8).astype(f32)).T
    ids = jnp.where(iota((128, 128), 1) == 127, count, ids).astype(i32)
    for d in range(N_DEV):
        ids_send[d] = ids[d : d + 1, :]
    sample = acc[256:384] - 128.0
    bag = jnp.where(sample >= 0.0, (mixed % 8).astype(f32) * 128.0 + sample, -1.0)
    pl.semaphore_wait(barrier, N_DEV - 1)

    def send_ids(k, to):
        pltpu.make_async_remote_copy(
            ids_send.at[to[0] * N_MEMBER + to[1]], ids_recv.at[k], ids_ssem, ids_rsem.at[k // SERVE],
            device_id=to, device_id_type=MESH,
        ).start()

    each_peer(send_ids)
    ids_recv[0] = ids_send[me]

    def take_ids(c, count):
        pltpu.make_async_copy(
            ids_send.at[pl.ds(0, count)], ids_recv.at[pl.ds(0, count)], ids_rsem.at[c]
        ).wait()
        at = pl.ds(c * SERVE, SERVE)
        ids_recv[at] = jnp.clip(ids_recv[at], 0, ROWS_DEV - 1)
        smem_copy(c).start()

    def smem_copy(c):
        at = pl.ds(c * SERVE, SERVE)
        return pltpu.make_async_copy(ids_recv.at[at], ids_smem.at[at], smem_sem.at[c])

    take_ids(0, SERVE - 1)
    table_copy.wait()

    def gather(slot):
        for i in range(MAIN):
            stage[i : i + 1, :] = table_v[pl.ds(ids_smem[slot, 0, i] & (ROWS_DEV - 1), 1), :]
        send_main[slot] = stage[...].astype(bf16)
        send_extra[slot] = table_v[pl.ds(ids_smem[slot, 0, MAIN] & (ROWS_DEV - 1), 1), :]

    def rows_copies(k):
        to = origin(k)
        return (
            pltpu.make_async_remote_copy(
                send_main.at[k], recv_main.at[k], row_ssem, rowm_rsem.at[k // GROUP],
                device_id=to, device_id_type=MESH,
            ),
            pltpu.make_async_remote_copy(
                send_extra.at[k], recv_extra.at[k], row_esem, rowe_rsem.at[k // GROUP],
                device_id=to, device_id_type=MESH,
            ),
        )

    def serve(k, c):
        gather(k)
        for copy in rows_copies(k):
            copy.start()
        return c

    def serve_chunk(c, carry):
        take_ids(c + 1, SERVE)
        smem_copy(c).wait()
        lax.fori_loop(jnp.maximum(c * SERVE, 1), c * SERVE + SERVE, serve, 0)
        return carry

    lax.fori_loop(0, N_DEV // SERVE - 1, serve_chunk, 0)
    smem_copy(N_DEV // SERVE - 1).wait()
    lax.fori_loop(N_DEV - SERVE, N_DEV, serve, 0)
    gather(0)
    recv_main[0] = send_main[0]
    recv_extra[0] = send_extra[0]

    bag_i = bag.astype(i32)
    for d in range(N_DEV):
        bag_of[d] = jnp.broadcast_to(bag_i[0:MAIN, d : d + 1], (MAIN, 128))
    bag_t = bag.T.astype(i32)
    bag_extra[...] = jnp.broadcast_to(bag_t[:, MAIN : MAIN + 1], (128, 128))

    for copy in weight_copies:
        copy.wait()

    top_in[...] = jnp.zeros_like(top_in)
    top_in[0:DENSE, :] = x_ref[...]
    x_pad = top_in[0:128, :]
    x_h = halves(x_pad)
    w0_t = jnp.concatenate([w0_ref[...], jnp.zeros((128 - DENSE, BOT1), f32)], axis=0).T
    w0_th = halves(w0_t)
    h1p = dot3(w0_th, x_h, NN)
    s1 = sigmoid(h1p)
    h1_h = halves(h1p * s1)
    d1 = s1 * (1.0 + h1p * (1.0 - s1))
    w1_h = halves(w1_ref[...])
    w1_th = halves(w1_ref[...].T)
    h2p = dot3(w1_th, h1_h, NN)
    s2 = sigmoid(h2p)
    h2_h = halves(h2p * s2)
    d2 = s2 * (1.0 + h2p * (1.0 - s2))
    w2_h = halves(w2_ref[...])
    w2_th = halves(w2_ref[...].T)
    bp = dot3(w2_th, h2_h, NN)
    s3 = sigmoid(bp)
    bottom = bp * s3
    d3 = s3 * (1.0 + bp * (1.0 - s3))
    top_in[0:128, :] = bottom
    wt0_p[...] = jnp.zeros_like(wt0_p)
    wt0_p[0:TOPIN, :] = wt0_ref[...]
    wt0_h = halves(wt0_p[...])
    wt0_th = halves(wt0_p[...].T)

    def one_hot(bags):
        return jnp.concatenate(
            [(bags == iota((1, 128), 1) + 128 * t).astype(f32).astype(bf16) for t in range(NT)], axis=1
        )

    def pool_main(q):
        for i in range(GROUP):
            from_g, from_m = peer(q * GROUP + i)
            st[pl.ds(i * MAIN, MAIN), :] = one_hot(bag_of[from_g * N_MEMBER + from_m])
            hid[pl.ds(from_g * N_MEMBER + from_m, 1), :] = recv_extra[q * GROUP + i]
        rows = recv_main[pl.ds(q * GROUP, GROUP)].reshape(GROUP * MAIN, E)
        pooled[...] += dot(rows, st[...], TN)

    def wait_rows(q, count):
        pltpu.make_async_copy(
            send_main.at[pl.ds(0, count)], recv_main.at[pl.ds(0, count)], rowm_rsem.at[q]
        ).wait()
        pltpu.make_async_copy(
            send_extra.at[pl.ds(0, count)], recv_extra.at[pl.ds(0, count)], rowe_rsem.at[q]
        ).wait()

    st_extra[...] = one_hot(bag_extra[...])
    pooled[...] = jnp.zeros_like(pooled)
    wait_rows(0, GROUP - 1)
    pool_main(0)

    def pool_step(q, c):
        wait_rows(q, GROUP)
        pool_main(q)
        return c

    lax.fori_loop(1, N_DEV // GROUP, pool_step, 0)
    pooled[...] += dot(hid[0:128, :].astype(bf16), st_extra[...], TN)

    z = [bottom] + [pooled[:, 128 * t : 128 * (t + 1)] for t in range(NT)]
    for n, (i, j) in enumerate(PAIRS):
        top_in[128 + n : 129 + n, :] = jnp.sum(z[i] * z[j], axis=0, keepdims=True)
    top_h = halves(top_in[...])
    up = dot3(wt0_th, top_h, NN)
    su = sigmoid(up)
    hid[...] = up * su
    lg = lg_ref[...]
    wt1_col = jnp.broadcast_to(wt1_ref[...], (128, TOPH)).T
    dup[...] = wt1_col * lg * (su * (1.0 + up * (1.0 - su)))
    dup_h = halves(dup[...])
    d_top = dot3(wt0_h, dup_h, NN)
    d_pair = {}
    for n, (i, j) in enumerate(PAIRS):
        d_pair[i, j] = d_pair[j, i] = d_top[128 + n : 129 + n, :]
    d_z = []
    for i in range(9):
        total = None
        for j in range(9):
            if j != i:
                term = d_pair[i, j] * z[j]
                total = term if total is None else total + term
        d_z.append(total)
        if i > 0:
            pg[128 * (i - 1) : 128 * i, :] = total.T.astype(bf16)

    pltpu.make_async_copy(send_main.at[pl.ds(0, 127)], recv_main.at[pl.ds(0, 127)], row_ssem).wait()
    pltpu.make_async_copy(send_extra.at[pl.ds(0, 127)], recv_extra.at[pl.ds(0, 127)], row_esem).wait()

    def main_copy(k):
        return pltpu.make_async_remote_copy(
            send_main.at[k], gmain_out.at[k], g_ssem, gm_rsem, device_id=peer(k), device_id_type=MESH
        )

    def send_grad_extra(k, to):
        pltpu.make_async_remote_copy(
            send_extra.at[to[0] * N_MEMBER + to[1]], gextra_out.at[k], g_esem, ge_rsem,
            device_id=to, device_id_type=MESH,
        ).start()

    def expand(q):
        for i in range(GROUP):
            to_g, to_m = peer(q * GROUP + i)
            st[pl.ds(i * MAIN, MAIN), :] = one_hot(bag_of[to_g * N_MEMBER + to_m])
        grads = dot(st[...], pg[...], NN).astype(bf16)
        send_main[pl.ds(q * GROUP, GROUP)] = grads.reshape(GROUP, MAIN, E)

    def start_grads(k, c):
        main_copy(k).start()
        return c

    expand(0)
    lax.fori_loop(1, GROUP, start_grads, 0)

    def expand_step(q, c):
        expand(q)
        lax.fori_loop(q * GROUP, q * GROUP + GROUP, start_grads, 0)
        return c

    lax.fori_loop(1, N_DEV // GROUP // 2, expand_step, 0)
    extra = dot(st_extra[...], pg[...], NN)
    for d in range(N_DEV):
        send_extra[d] = extra[d : d + 1, :]
    each_peer(send_grad_extra)
    flat[...] = jnp.zeros_like(flat)
    g_t0 = dot3(top_h, dup_h, NT_)
    for c in range(8):
        flat[OFF_TOP0 + c * TOP0_ROWS : OFF_TOP0 + (c + 1) * TOP0_ROWS, :] = g_t0[
            0:TOP0_ROWS, 128 * c : 128 * (c + 1)
        ]
    lg_h = halves(jnp.broadcast_to(lg, (8, 128)))
    g_t1 = dot3(lg_h, halves(hid[...]), NT_)[0:1]
    g_t1 = jnp.concatenate([g_t1[:, 128 * c : 128 * (c + 1)] for c in range(8)], axis=0)
    flat[OFF_TOP1 : OFF_TOP1 + 16, :] = jnp.concatenate([g_t1, g_t1], axis=0)
    d_bp = halves((d_top[0:128] + d_z[0]) * d3)
    flat[OFF_BOT2 : OFF_BOT2 + BOT2, :] = dot3(h2_h, d_bp, NT_)
    d_h2p = halves(dot3(w2_h, d_bp, NN) * d2)
    g_b1 = dot3(h1_h, d_h2p, NT_)
    for c in range(2):
        flat[OFF_BOT1 + c * BOT1 : OFF_BOT1 + (c + 1) * BOT1, :] = g_b1[:, 128 * c : 128 * (c + 1)]
    d_h1p = halves(dot3(w1_h, d_h2p, NN) * d1)
    g_b0 = dot3(x_h, d_h1p, NT_)[0:16]
    for c in range(4):
        flat[OFF_BOT0 + c * 16 : OFF_BOT0 + (c + 1) * 16, :] = g_b0[:, 128 * c : 128 * (c + 1)]

    core = g % 2
    half_copy = pltpu.make_async_remote_copy(
        flat.at[pl.ds(pl.multiple_of((1 - core) * HALF, HALF), HALF)], flat_half, half_ssem, half_rsem,
        device_id=(g + 1 - 2 * core, m), device_id_type=MESH,
    )
    half_copy.start()
    half_copy.wait()
    own_half = flat[pl.ds(pl.multiple_of(core * HALF, HALF), HALF), :]
    flat_z[...] = (own_half + flat_half[...]).astype(bf16)
    z_at = g // 2

    def rz_copy(step):
        to = (z_at + step) % 4
        return pltpu.make_async_remote_copy(
            flat_z.at[pl.ds(pl.multiple_of(to * PIECE, PIECE), PIECE)], part_z.at[step],
            rz_ssem.at[step], rz_rsem.at[step], device_id=(to * 2 + core, m), device_id_type=MESH,
        )

    def rx_copy(step):
        to = member_peer(step, 1)
        return pltpu.make_async_remote_copy(
            sum_z.at[pl.ds(pl.multiple_of(to * SMALL, SMALL), SMALL)], part_xy.at[step],
            rx_ssem.at[step], rx_rsem.at[step], device_id=(g, to), device_id_type=MESH,
        )

    for step in range(1, 4):
        rz_copy(step).start()

    lax.fori_loop(N_DEV // GROUP // 2, N_DEV // GROUP, expand_step, 0)
    own_copy = pltpu.make_async_copy(send_main.at[0], gmain_out.at[0], own_sem)
    own_copy.start()
    gextra_out[0] = send_extra[me]
    ids_out[...] = ids_recv[...]

    total = flat_z[pl.ds(pl.multiple_of(z_at * PIECE, PIECE), PIECE), :].astype(f32)
    for step in range(1, 4):
        rz_copy(step).wait()
        total = total + part_z[step].astype(f32)
    sum_z[...] = total
    for step in range(1, N_MEMBER):
        rx_copy(step).start()
    total = sum_z[pl.ds(pl.multiple_of(m * SMALL, SMALL), SMALL), :]
    for step in range(1, N_MEMBER):
        rx_copy(step).wait()
        total = total + part_xy[step]
    flat_out[...] = total

    own_copy.wait()
    pltpu.make_async_copy(ids_send.at[pl.ds(0, 127)], ids_recv.at[pl.ds(0, 127)], ids_ssem).wait()
    pltpu.make_async_copy(send_main.at[pl.ds(0, 127)], recv_main.at[pl.ds(0, 127)], g_ssem).wait()
    pltpu.make_async_copy(send_extra.at[pl.ds(0, 127)], recv_extra.at[pl.ds(0, 127)], g_esem).wait()
    pltpu.make_async_copy(send_main.at[pl.ds(1, 127)], gmain_out.at[pl.ds(1, 127)], gm_rsem).wait()
    pltpu.make_async_copy(send_extra.at[pl.ds(0, 127)], gextra_out.at[pl.ds(0, 127)], ge_rsem).wait()


WAYS = 4
BATCH = 32
CHUNK = 512


def scatter_kernel(ids_ref, gmain_hbm, gextra_ref, table_hbm, new_hbm, change_hbm,
                   sums, stage, gmain, table, change, gmain_sem, table_sem, new_sem, change_sem):
    def gmain_copy(q):
        at = pl.ds(q * SERVE, SERVE)
        return pltpu.make_async_copy(gmain_hbm.at[at], gmain.at[at], gmain_sem.at[q])

    for q in range(N_DEV // SERVE):
        gmain_copy(q).start()
    table_copy = pltpu.make_async_copy(table_hbm, table, table_sem)
    table_copy.start()
    sums[...] = jnp.zeros_like(sums)

    def convert(s, c):
        stage[s, 0:MAIN, :] = gmain[s].astype(f32)
        stage[s, MAIN : MAIN + 8, :] = jnp.where(iota((8, 128), 0) == 0, gextra_ref[s], 0.0)
        stage[s, MAIN + 8 : 128, :] = jnp.zeros((24, 128), f32)
        return c

    def source(s, c):
        count = ids_ref[s, 0, 127]

        def batch(b, c):
            first = pl.multiple_of(b * BATCH, BATCH)
            for h in range(0, BATCH, WAYS):
                rows = [ids_ref[s, 0, first + h + i] for i in range(WAYS)]
                total = [
                    sums[i, pl.ds(rows[i], 1), :] + stage[s, pl.ds(first + h + i, 1), :] for i in range(WAYS)
                ]
                for i in range(WAYS):
                    sums[i, pl.ds(rows[i], 1), :] = total[i]
            return c

        lax.fori_loop(0, (count + BATCH - 1) // BATCH, batch, 0)
        return c

    def chunk(q, c):
        gmain_copy(q).wait()
        lax.fori_loop(0, SERVE, lambda i, c: convert(q * SERVE + i, c), 0, unroll=4)
        lax.fori_loop(q * SERVE, q * SERVE + SERVE, source, 0)
        return c

    lax.fori_loop(0, N_DEV // SERVE, chunk, 0)
    table_copy.wait()

    def finish(b, c):
        start = pl.multiple_of(b * CHUNK, CHUNK)
        for r in range(0, CHUNK, 64):
            at = pl.ds(pl.multiple_of(start + r, 64), 64)
            total = sums[0, at, :]
            for i in range(1, WAYS):
                total = total + sums[i, at, :]
            total = -embed_rate * total
            table[at, :] = table[at, :] + total
            change[at, :] = total.astype(bf16)
        at = pl.ds(start, CHUNK)
        pltpu.make_async_copy(table.at[at], new_hbm.at[at], new_sem).start()
        pltpu.make_async_copy(change.at[at], change_hbm.at[at], change_sem).start()
        return c

    lax.fori_loop(0, ROWS_DEV // CHUNK, finish, 0)
    pltpu.make_async_copy(table, new_hbm, new_sem).wait()
    pltpu.make_async_copy(change, change_hbm, change_sem).wait()


def member_peer(k, sign):
    x, y = lax.axis_index("member") // 4, lax.axis_index("member") % 4
    kx = k % 4
    ky = (k // 4 + kx) % 4
    if sign < 0:
        kx, ky = (4 - kx) % 4, (4 - ky) % 4
    return ((x + kx) % 4) * 4 + (y + ky) % 4


CUT = 5


def parity_kernel(
    change_ref, parity_ref, flat_ref,
    new_ref, all_z,
    pieces, all_xy,
    ch_ssem, ch_rsem, ax_ssem, ax_rsem, az_ssem, az_rsem, ac_ssem, ac_rsem,
):
    g, m = lax.axis_index("group"), lax.axis_index("member")
    barrier = pltpu.get_barrier_semaphore()
    for j in range(1, N_GROUP):
        pl.semaphore_signal(barrier, 1, device_id=((g + j) % N_GROUP, m), device_id_type=MESH)
    for k in range(1, N_MEMBER):
        pl.semaphore_signal(barrier, 1, device_id=(g, member_peer(k, 1)), device_id_type=MESH)
    pl.semaphore_wait(barrier, N_GROUP - 1 + N_MEMBER - 1)

    def remote(src, dst, ssem, rsem, to):
        return pltpu.make_async_remote_copy(src, dst, ssem, rsem, device_id=to, device_id_type=MESH)

    rows = ROWS_DEV // N_MEMBER

    def change_copy(k):
        to = member_peer(k, 1)
        return remote(
            change_ref.at[pl.ds(pl.multiple_of(to * rows, rows), rows)], pieces.at[k], ch_ssem.at[k], ch_rsem.at[k],
            (g, to),
        )

    z, core = g // 2, g % 2

    def ax_copy(k):
        return remote(flat_ref, all_xy.at[m], ax_ssem.at[k], ax_rsem.at[k], (g, member_peer(k, 1)))

    place = core * 4 + z

    def az_copy(j):
        return remote(
            all_z.at[place], all_z.at[place], az_ssem.at[j], az_rsem.at[j], ((z + j) % 4 * 2 + core, m)
        )

    def across_copy(j):
        slot = core * 4 + (z + 4 - j) % 4
        return remote(
            all_z.at[slot], all_z.at[slot], ac_ssem.at[j], ac_rsem.at[j], (z * 2 + 1 - core, m)
        )

    for k in range(1, N_MEMBER):
        ax_copy(k).start()
    for k in range(1, CUT):
        change_copy(k).start()
    all_xy[m] = flat_ref[...]
    for k in range(1, N_MEMBER):
        ax_copy(k).wait()
    all_z[place] = all_xy[...].reshape(PIECE, E).astype(bf16)
    for j in range(1, 4):
        az_copy(j).start()
    across_copy(0).start()
    for k in range(CUT, N_MEMBER):
        change_copy(k).start()

    def weights(k):
        source = member_peer(k, -1).astype(f32) / N_MEMBER
        one = jnp.ones((1, 128), f32)
        return 1.0 / (one + source), 1.0 / (one * 2.0 + source)

    for j in range(1, 4):
        az_copy(j).wait_recv()
        across_copy(j).start()

    def add(k, part_of, base_of):
        first, second = weights(k)

        def step(b, c):
            at = pl.ds(pl.multiple_of(b * 64, 64), 64)
            part = part_of(b).astype(f32)
            new_ref[at, 0:128] = base_of[at, 0:128] + first * part
            new_ref[at, 128:256] = base_of[at, 128:256] + second * part
            return c

        lax.fori_loop(0, rows // 64, step, 0)

    add(0, lambda b: change_ref[pl.ds(pl.multiple_of(m * rows + b * 64, 64), 64), :], parity_ref)
    for k in range(1, N_MEMBER):
        change_copy(k).wait()
        add(k, lambda b: pieces[k, pl.ds(pl.multiple_of(b * 64, 64), 64), :], new_ref)

    for j in range(4):
        if j > 0:
            az_copy(j).wait_send()
        across_copy(j).wait()


def unpack_kernel(
    parity_hbm, all_z_hbm, new_hbm, g0_ref, g1_ref, g2_ref, gt0_ref, gt1_ref,
    all_z, parity, parity_sem, all_z_sem, new_sem,
):
    parity_copy = pltpu.make_async_copy(parity_hbm, parity, parity_sem)
    parity_copy.start()
    all_z_copy = pltpu.make_async_copy(all_z_hbm, all_z, all_z_sem)
    all_z_copy.start()
    parity_copy.wait()
    new_copy = pltpu.make_async_copy(parity, new_hbm, new_sem)
    new_copy.start()
    all_z_copy.wait()
    for c in range(8):
        gt0_ref[:, 128 * c : 128 * (c + 1)] = piece_rows(all_z, OFF_TOP0 + c * TOP0_ROWS, TOP0_ROWS)[0:TOPIN]
    for c in range(2):
        g1_ref[:, 128 * c : 128 * (c + 1)] = piece_rows(all_z, OFF_BOT1 + c * BOT1, BOT1)
    g2_ref[...] = piece_rows(all_z, OFF_BOT2, BOT2)
    for c in range(4):
        g0_ref[:, 128 * c : 128 * (c + 1)] = piece_rows(all_z, OFF_BOT0 + c * 16, 16)[0:DENSE]
    top1 = piece_rows(all_z, OFF_TOP1, 16)
    for c in range(8):
        gt1_ref[:, 128 * c : 128 * (c + 1)] = top1[c : c + 1, :]
    new_copy.wait()


def piece_rows(ref, start, count):
    out = []
    while count > 0:
        p, at = start // PIECE, start % PIECE
        n = min(count, PIECE - at)
        out.append(ref[p, at : at + n, :].astype(f32))
        start, count = start + n, count - n
    return out[0] if len(out) == 1 else jnp.concatenate(out, axis=0)


def body(
    dense_in, lookup_owner, lookup_row, bag_length, logit_grad, table, parity,
    w_bottom0, w_bottom1, w_bottom2, w_top0, w_top1,
):
    owner = lookup_owner.transpose(1, 2, 0).reshape(NT * HOT, 128)
    row = lookup_row.transpose(1, 2, 0).reshape(NT * HOT, 128)
    vmem = pl.BlockSpec(memory_space=VM)
    anyw = pl.BlockSpec(memory_space=pl.ANY)
    smem = pl.BlockSpec(memory_space=pltpu.SMEM)
    dma = pltpu.SemaphoreType.DMA
    sds = jax.ShapeDtypeStruct
    ids, gmain, gextra, flat = pl.pallas_call(
        exchange_kernel,
        out_shape=(
            sds((N_DEV, 1, 128), i32),
            sds((N_DEV, MAIN, E), bf16),
            sds((N_DEV, 1, E), f32),
            sds((SMALL, E), f32),
        ),
        in_specs=[vmem] * 5 + [anyw] * 5 + [vmem],
        out_specs=(vmem, anyw, vmem, vmem),
        scratch_shapes=[
            VM((ROWS_DEV, E), f32),
            VM((N_DEV, 1, 128), i32),
            VM((N_DEV, 1, 128), i32),
            pltpu.SMEM((N_DEV, 1, 128), i32),
            VM((MAIN, E), f32),
            VM((N_DEV, MAIN, E), bf16),
            VM((N_DEV, 1, E), f32),
            VM((N_DEV, MAIN, E), bf16),
            VM((N_DEV, 1, E), f32),
            VM((32, 128, 256), bf16),
            VM((32, 384, 256), bf16),
            VM((N_DEV, MAIN, 128), i32),
            VM((128, 128), i32),
            VM((GROUP * MAIN, BAGS), bf16),
            VM((N_DEV, BAGS), bf16),
            VM((E, BAGS), f32),
            VM((BAGS, E), bf16),
            VM((256, TOPH), f32),
            VM((256, 128), f32),
            VM((TOPH, 128), f32),
            VM((TOPH, 128), f32),
            dma, dma((N_DEV // SERVE,)), dma, dma((N_DEV // SERVE,)), dma, dma,
            dma((N_DEV // GROUP,)), dma((N_DEV // GROUP,)),
            dma, dma, dma, dma,
            VM((FLAT, E), f32),
            VM((HALF, E), f32),
            dma, dma, dma,
            VM((DENSE, BOT1), f32),
            VM((BOT1, BOT2), f32),
            VM((BOT2, E), f32),
            VM((TOPIN, TOPH), f32),
            dma((4,)),
            VM((HALF, E), bf16),
            VM((4, PIECE, E), bf16),
            VM((PIECE, E), f32),
            VM((N_MEMBER, SMALL, E), f32),
            dma((4,)), dma((4,)), dma((N_MEMBER,)), dma((N_MEMBER,)),
        ],
        compiler_params=pltpu.CompilerParams(
            collective_id=0, has_side_effects=True, vmem_limit_bytes=56 << 20
        ),
    )(
        owner, row, bag_length.T, dense_in.T, logit_grad.reshape(1, 128), table,
        w_bottom0, w_bottom1, w_bottom2, w_top0, w_top1.reshape(1, TOPH),
    )
    new_table, change = pl.pallas_call(
        scatter_kernel,
        out_shape=(sds((ROWS_DEV, E), f32), sds((ROWS_DEV, E), bf16)),
        in_specs=[smem, anyw, vmem, anyw],
        out_specs=(anyw, anyw),
        scratch_shapes=[
            VM((WAYS, ROWS_DEV, E), f32),
            VM((N_DEV, 128, E), f32),
            VM((N_DEV, MAIN, E), bf16),
            VM((ROWS_DEV, E), f32),
            VM((ROWS_DEV, E), bf16),
            dma((N_DEV // SERVE,)), dma, dma, dma,
        ],
        compiler_params=pltpu.CompilerParams(vmem_limit_bytes=56 << 20),
    )(ids, gmain, gextra, table)
    parity_sum, all_z = pl.pallas_call(
        parity_kernel,
        out_shape=(sds(parity.shape, f32), sds((N_GROUP, PIECE, E), bf16)),
        in_specs=[vmem] * 3,
        out_specs=(vmem, vmem),
        scratch_shapes=[
            VM((N_MEMBER, ROWS_DEV // N_MEMBER, E), bf16),
            VM((N_MEMBER, SMALL, E), f32),
            dma((N_MEMBER,)), dma((N_MEMBER,)), dma((N_MEMBER,)), dma((N_MEMBER,)),
            dma((4,)), dma((4,)), dma((4,)), dma((4,)),
        ],
        compiler_params=pltpu.CompilerParams(
            collective_id=1, has_side_effects=True, vmem_limit_bytes=56 << 20
        ),
    )(change, parity, flat)
    new_parity, g0, g1, g2, gt0, gt1 = pl.pallas_call(
        unpack_kernel,
        out_shape=(
            sds(parity.shape, f32),
            sds((DENSE, BOT1), f32),
            sds((BOT1, BOT2), f32),
            sds((BOT2, E), f32),
            sds((TOPIN, TOPH), f32),
            sds((1, TOPH), f32),
        ),
        in_specs=[anyw] * 2,
        out_specs=(anyw,) + (vmem,) * 5,
        scratch_shapes=[VM((N_GROUP, PIECE, E), bf16), VM(parity.shape, f32), dma, dma, dma],
        compiler_params=pltpu.CompilerParams(vmem_limit_bytes=60 << 20),
    )(parity_sum, all_z)
    return new_table, new_parity, g0, g1, g2, gt0, gt1.reshape(TOPH)


def solution(mesh):
    rows = P(("group", "member"), None)
    cube = P(("group", "member"), None, None)
    in_specs = (rows, cube, cube, rows, P(("group", "member")), rows, rows, P(), P(), P(), P(), P())
    out_specs = (rows, rows, P(), P(), P(), P(), P())
    return jax.shard_map(body, mesh=mesh, in_specs=in_specs, out_specs=out_specs, check_vma=False)
```

```python
import functools

import jax
import jax.numpy as jnp
import numpy as np
from jax import lax
from jax.experimental import pallas as pl
from jax.experimental.pallas import tpu as pltpu
from jax.sharding import PartitionSpec as P

embed_rate = 1.0

MESH = pl.DeviceIdType.MESH
N_DEV = 128
N_GROUP = 8
N_MEMBER = 16
E = 128
ROWS_DEV = 8192
NT = 8
HOT = 8
BAGS = 1024
MAIN = 96
SERVE = 16
GROUP = 8
PAIRS = [(i, j) for i in range(9) for j in range(i)]
BOT1, BOT2, TOPH, DENSE, TOPIN = 512, 256, 1024, 13, 164

TOP0_ROWS = 176
OFF_TOP0 = 0
OFF_BOT1 = 8 * TOP0_ROWS
OFF_BOT2 = OFF_BOT1 + 2 * BOT1
OFF_BOT0 = OFF_BOT2 + BOT2
OFF_TOP1 = OFF_BOT0 + 4 * 16
FLAT = 3072
HALF = FLAT // 2
PIECE = FLAT // N_GROUP
SMALL = PIECE // N_MEMBER

f32, bf16, i32 = jnp.float32, jnp.bfloat16, jnp.int32
VM = pltpu.VMEM


def iota(shape, dim):
    return lax.broadcasted_iota(i32, shape, dim)


def dot(a, b, dims):
    return lax.dot_general(a, b, (dims, ((), ())), preferred_element_type=f32)


NN = ((1,), (0,))
NT_ = ((1,), (1,))
TN = ((0,), (0,))


def halves(a):
    hi = a.astype(bf16)
    return hi, (a - hi.astype(f32)).astype(bf16)


def dot3(a, b, dims):
    return dot(a[0], b[0], dims) + (dot(a[0], b[1], dims) + dot(a[1], b[0], dims))


def coords():
    g, m = lax.axis_index("group"), lax.axis_index("member")
    return g // 2, g % 2, m // 4, m % 4


def peer(k):
    z, c, x, y = coords()
    kx = k % 4
    ky = (k // 4 + kx) % 4
    kz = (k // 16 + ky) % 4
    kc = k // 64
    return ((z + kz) % 4) * 2 + (c + kc) % 2, ((x + kx) % 4) * 4 + (y + ky) % 4


def origin(k):
    z, c, x, y = coords()
    kx = k % 4
    ky = (k // 4 + kx) % 4
    kz = (k // 16 + ky) % 4
    kc = k // 64
    return ((z + 4 - kz) % 4) * 2 + (c + 2 - kc) % 2, ((x + 4 - kx) % 4) * 4 + (y + 4 - ky) % 4


def each_peer(act):
    z, c, x, y = coords()
    member = [((x + r % 4) % 4) * 4 + (y + (r // 4 + r % 4) % 4) % 4 for r in range(16)]

    def sixteen(a, first):
        group = [((z + a + ky) % 4) * 2 + (c + a // 4) % 2 for ky in range(4)]
        for r in range(first, 16):
            act(a * 16 + r, (group[(r // 4 + r % 4) % 4], member[r]))

    sixteen(0, 1)

    def loop(a, carry):
        sixteen(a, 0)
        return carry

    lax.fori_loop(1, 8, loop, 0)


def sigmoid(v):
    return 1.0 / (1.0 + jnp.exp(-v))


def exchange_kernel(
    own_ref, row_ref, len_ref, x_ref, lg_ref, table_hbm, w0_hbm, w1_hbm, w2_hbm, wt0_hbm, wt1_ref,
    ids_out, gmain_out, gextra_out, flat_out,
    table_v, ids_send, ids_recv, ids_smem, stage, send_main, send_extra, recv_main, recv_extra,
    hits, vals, bag_of, bag_extra, st, st_extra, pooled, pg, wt0_p, top_in, hid, dup,
    table_sem, smem_sem, ids_ssem, ids_rsem, row_ssem, row_esem, rowm_rsem, rowe_rsem,
    g_ssem, g_esem, gm_rsem, ge_rsem, flat, flat_half, own_sem, half_ssem, half_rsem,
    w0_ref, w1_ref, w2_ref, wt0_ref, w_sem,
):
    g, m = lax.axis_index("group"), lax.axis_index("member")
    me = g * N_MEMBER + m

    table_copy = pltpu.make_async_copy(table_hbm, table_v, table_sem)
    table_copy.start()
    barrier = pltpu.get_barrier_semaphore()
    weight_copies = [
        pltpu.make_async_copy(src, dst, w_sem.at[i])
        for i, (src, dst) in enumerate([(w0_hbm, w0_ref), (w1_hbm, w1_ref), (w2_hbm, w2_ref), (wt0_hbm, wt0_ref)])
    ]
    for copy in weight_copies:
        copy.start()

    each_peer(lambda k, to: pl.semaphore_signal(barrier, 1, device_id=to, device_id_type=MESH))

    upper = (iota((256, 384), 0) < iota((256, 384), 1)).astype(bf16)
    dev_of = iota((128, 256), 0)
    lane = iota((1, 128), 1)
    bag_lo = (jnp.concatenate([lane, lane], axis=1) + 128).astype(f32).astype(bf16)

    def place(j, count):
        t = j // 4
        h = (2 * j) % 8
        length = len_ref[pl.ds(t, 1), :]
        own = jnp.concatenate([own_ref[pl.ds(2 * j, 1), :], own_ref[pl.ds(2 * j + 1, 1), :]], axis=1)
        row = jnp.concatenate([row_ref[pl.ds(2 * j, 1), :], row_ref[pl.ds(2 * j + 1, 1), :]], axis=1)
        own = jnp.where(jnp.concatenate([h < length, h + 1 < length], axis=1), own, -1)
        hit = (own == dev_of).astype(f32)
        hit_b = hit.astype(bf16)
        ranks = dot(hit_b, upper, NN)
        before = ranks[:, 0:256] + jnp.concatenate([count, count], axis=1)
        pos = jnp.sum(before * hit, axis=0, keepdims=True).astype(i32)
        at = (pos == dev_of).astype(f32).astype(bf16)
        hits[j] = hit_b
        vals[j, 0:128, :] = at * (row // 32).astype(f32).astype(bf16)
        vals[j, 128:256, :] = at * (row % 32 * 8 + t).astype(f32).astype(bf16)
        vals[j, 256:384, :] = at * bag_lo
        return count + ranks[:, 256:384]

    count = lax.fori_loop(0, 32, place, jnp.zeros((128, 128), f32), unroll=4)
    acc = dot(vals[0], hits[0], NT_)
    for j in range(1, 32):
        acc = acc + dot(vals[j], hits[j], NT_)
    mixed = acc[128:256].astype(i32)
    ids = (acc[0:128] * 32.0 + (mixed // 8).astype(f32)).T
    ids = jnp.where(iota((128, 128), 1) == 127, count, ids).astype(i32)
    for d in range(N_DEV):
        ids_send[d] = ids[d : d + 1, :]
    sample = acc[256:384] - 128.0
    bag = jnp.where(sample >= 0.0, (mixed % 8).astype(f32) * 128.0 + sample, -1.0)
    pl.semaphore_wait(barrier, N_DEV - 1)

    def send_ids(k, to):
        pltpu.make_async_remote_copy(
            ids_send.at[to[0] * N_MEMBER + to[1]], ids_recv.at[k], ids_ssem, ids_rsem.at[k // SERVE],
            device_id=to, device_id_type=MESH,
        ).start()

    each_peer(send_ids)
    ids_recv[0] = ids_send[me]

    def take_ids(c, count):
        pltpu.make_async_copy(
            ids_send.at[pl.ds(0, count)], ids_recv.at[pl.ds(0, count)], ids_rsem.at[c]
        ).wait()
        at = pl.ds(c * SERVE, SERVE)
        ids_recv[at] = jnp.clip(ids_recv[at], 0, ROWS_DEV - 1)
        smem_copy(c).start()

    def smem_copy(c):
        at = pl.ds(c * SERVE, SERVE)
        return pltpu.make_async_copy(ids_recv.at[at], ids_smem.at[at], smem_sem.at[c])

    take_ids(0, SERVE - 1)
    table_copy.wait()

    def gather(slot):
        for i in range(MAIN):
            stage[i : i + 1, :] = table_v[pl.ds(ids_smem[slot, 0, i] & (ROWS_DEV - 1), 1), :]
        send_main[slot] = stage[...].astype(bf16)
        send_extra[slot] = table_v[pl.ds(ids_smem[slot, 0, MAIN] & (ROWS_DEV - 1), 1), :]

    def rows_copies(k):
        to = origin(k)
        return (
            pltpu.make_async_remote_copy(
                send_main.at[k], recv_main.at[k], row_ssem, rowm_rsem.at[k // GROUP],
                device_id=to, device_id_type=MESH,
            ),
            pltpu.make_async_remote_copy(
                send_extra.at[k], recv_extra.at[k], row_esem, rowe_rsem.at[k // GROUP],
                device_id=to, device_id_type=MESH,
            ),
        )

    def serve(k, c):
        gather(k)
        for copy in rows_copies(k):
            copy.start()
        return c

    def serve_chunk(c, carry):
        take_ids(c + 1, SERVE)
        smem_copy(c).wait()
        lax.fori_loop(jnp.maximum(c * SERVE, 1), c * SERVE + SERVE, serve, 0)
        return carry

    lax.fori_loop(0, N_DEV // SERVE - 1, serve_chunk, 0)
    smem_copy(N_DEV // SERVE - 1).wait()
    lax.fori_loop(N_DEV - SERVE, N_DEV, serve, 0)
    gather(0)
    recv_main[0] = send_main[0]
    recv_extra[0] = send_extra[0]

    bag_i = bag.astype(i32)
    for d in range(N_DEV):
        bag_of[d] = jnp.broadcast_to(bag_i[0:MAIN, d : d + 1], (MAIN, 128))
    bag_t = bag.T.astype(i32)
    bag_extra[...] = jnp.broadcast_to(bag_t[:, MAIN : MAIN + 1], (128, 128))

    for copy in weight_copies:
        copy.wait()

    top_in[...] = jnp.zeros_like(top_in)
    top_in[0:DENSE, :] = x_ref[...]
    x_pad = top_in[0:128, :]
    x_h = halves(x_pad)
    w0_t = jnp.concatenate([w0_ref[...], jnp.zeros((128 - DENSE, BOT1), f32)], axis=0).T
    w0_th = halves(w0_t)
    h1p = dot3(w0_th, x_h, NN)
    s1 = sigmoid(h1p)
    h1_h = halves(h1p * s1)
    d1 = s1 * (1.0 + h1p * (1.0 - s1))
    w1_h = halves(w1_ref[...])
    w1_th = halves(w1_ref[...].T)
    h2p = dot3(w1_th, h1_h, NN)
    s2 = sigmoid(h2p)
    h2_h = halves(h2p * s2)
    d2 = s2 * (1.0 + h2p * (1.0 - s2))
    w2_h = halves(w2_ref[...])
    w2_th = halves(w2_ref[...].T)
    bp = dot3(w2_th, h2_h, NN)
    s3 = sigmoid(bp)
    bottom = bp * s3
    d3 = s3 * (1.0 + bp * (1.0 - s3))
    top_in[0:128, :] = bottom
    wt0_p[...] = jnp.zeros_like(wt0_p)
    wt0_p[0:TOPIN, :] = wt0_ref[...]
    wt0_h = halves(wt0_p[...])
    wt0_th = halves(wt0_p[...].T)

    def one_hot(bags):
        return jnp.concatenate(
            [(bags == iota((1, 128), 1) + 128 * t).astype(f32).astype(bf16) for t in range(NT)], axis=1
        )

    def pool_main(q):
        for i in range(GROUP):
            from_g, from_m = peer(q * GROUP + i)
            st[pl.ds(i * MAIN, MAIN), :] = one_hot(bag_of[from_g * N_MEMBER + from_m])
            hid[pl.ds(from_g * N_MEMBER + from_m, 1), :] = recv_extra[q * GROUP + i]
        rows = recv_main[pl.ds(q * GROUP, GROUP)].reshape(GROUP * MAIN, E)
        pooled[...] += dot(rows, st[...], TN)

    def wait_rows(q, count):
        pltpu.make_async_copy(
            send_main.at[pl.ds(0, count)], recv_main.at[pl.ds(0, count)], rowm_rsem.at[q]
        ).wait()
        pltpu.make_async_copy(
            send_extra.at[pl.ds(0, count)], recv_extra.at[pl.ds(0, count)], rowe_rsem.at[q]
        ).wait()

    st_extra[...] = one_hot(bag_extra[...])
    pooled[...] = jnp.zeros_like(pooled)
    wait_rows(0, GROUP - 1)
    pool_main(0)

    def pool_step(q, c):
        wait_rows(q, GROUP)
        pool_main(q)
        return c

    lax.fori_loop(1, N_DEV // GROUP, pool_step, 0)
    pooled[...] += dot(hid[0:128, :].astype(bf16), st_extra[...], TN)

    z = [bottom] + [pooled[:, 128 * t : 128 * (t + 1)] for t in range(NT)]
    for n, (i, j) in enumerate(PAIRS):
        top_in[128 + n : 129 + n, :] = jnp.sum(z[i] * z[j], axis=0, keepdims=True)
    top_h = halves(top_in[...])
    up = dot3(wt0_th, top_h, NN)
    su = sigmoid(up)
    hid[...] = up * su
    lg = lg_ref[...]
    wt1_col = jnp.broadcast_to(wt1_ref[...], (128, TOPH)).T
    dup[...] = wt1_col * lg * (su * (1.0 + up * (1.0 - su)))
    dup_h = halves(dup[...])
    d_top = dot3(wt0_h, dup_h, NN)
    d_pair = {}
    for n, (i, j) in enumerate(PAIRS):
        d_pair[i, j] = d_pair[j, i] = d_top[128 + n : 129 + n, :]
    d_z = []
    for i in range(9):
        total = None
        for j in range(9):
            if j != i:
                term = d_pair[i, j] * z[j]
                total = term if total is None else total + term
        d_z.append(total)
        if i > 0:
            pg[128 * (i - 1) : 128 * i, :] = total.T.astype(bf16)

    pltpu.make_async_copy(send_main.at[pl.ds(0, 127)], recv_main.at[pl.ds(0, 127)], row_ssem).wait()
    pltpu.make_async_copy(send_extra.at[pl.ds(0, 127)], recv_extra.at[pl.ds(0, 127)], row_esem).wait()

    def main_copy(k):
        return pltpu.make_async_remote_copy(
            send_main.at[k], gmain_out.at[k], g_ssem, gm_rsem, device_id=peer(k), device_id_type=MESH
        )

    def send_grad_extra(k, to):
        pltpu.make_async_remote_copy(
            send_extra.at[to[0] * N_MEMBER + to[1]], gextra_out.at[k], g_esem, ge_rsem,
            device_id=to, device_id_type=MESH,
        ).start()

    def expand(q):
        for i in range(GROUP):
            to_g, to_m = peer(q * GROUP + i)
            st[pl.ds(i * MAIN, MAIN), :] = one_hot(bag_of[to_g * N_MEMBER + to_m])
        grads = dot(st[...], pg[...], NN).astype(bf16)
        send_main[pl.ds(q * GROUP, GROUP)] = grads.reshape(GROUP, MAIN, E)

    def start_grads(k, c):
        main_copy(k).start()
        return c

    expand(0)
    lax.fori_loop(1, GROUP, start_grads, 0)

    def expand_step(q, c):
        expand(q)
        lax.fori_loop(q * GROUP, q * GROUP + GROUP, start_grads, 0)
        return c

    lax.fori_loop(1, N_DEV // GROUP // 2, expand_step, 0)
    extra = dot(st_extra[...], pg[...], NN)
    for d in range(N_DEV):
        send_extra[d] = extra[d : d + 1, :]
    each_peer(send_grad_extra)
    lax.fori_loop(N_DEV // GROUP // 2, N_DEV // GROUP, expand_step, 0)
    own_copy = pltpu.make_async_copy(send_main.at[0], gmain_out.at[0], own_sem)
    own_copy.start()
    gextra_out[0] = send_extra[me]
    ids_out[...] = ids_recv[...]

    flat[...] = jnp.zeros_like(flat)
    g_t0 = dot3(top_h, dup_h, NT_)
    for c in range(8):
        flat[OFF_TOP0 + c * TOP0_ROWS : OFF_TOP0 + (c + 1) * TOP0_ROWS, :] = g_t0[
            0:TOP0_ROWS, 128 * c : 128 * (c + 1)
        ]
    lg_h = halves(jnp.broadcast_to(lg, (8, 128)))
    g_t1 = dot3(lg_h, halves(hid[...]), NT_)[0:1]
    g_t1 = jnp.concatenate([g_t1[:, 128 * c : 128 * (c + 1)] for c in range(8)], axis=0)
    flat[OFF_TOP1 : OFF_TOP1 + 16, :] = jnp.concatenate([g_t1, g_t1], axis=0)
    d_bp = halves((d_top[0:128] + d_z[0]) * d3)
    flat[OFF_BOT2 : OFF_BOT2 + BOT2, :] = dot3(h2_h, d_bp, NT_)
    d_h2p = halves(dot3(w2_h, d_bp, NN) * d2)
    g_b1 = dot3(h1_h, d_h2p, NT_)
    for c in range(2):
        flat[OFF_BOT1 + c * BOT1 : OFF_BOT1 + (c + 1) * BOT1, :] = g_b1[:, 128 * c : 128 * (c + 1)]
    d_h1p = halves(dot3(w1_h, d_h2p, NN) * d1)
    g_b0 = dot3(x_h, d_h1p, NT_)[0:16]
    for c in range(4):
        flat[OFF_BOT0 + c * 16 : OFF_BOT0 + (c + 1) * 16, :] = g_b0[:, 128 * c : 128 * (c + 1)]

    core = g % 2
    half_copy = pltpu.make_async_remote_copy(
        flat.at[pl.ds(pl.multiple_of((1 - core) * HALF, HALF), HALF)], flat_half, half_ssem, half_rsem,
        device_id=(g + 1 - 2 * core, m), device_id_type=MESH,
    )
    half_copy.start()
    half_copy.wait()
    own_half = flat[pl.ds(pl.multiple_of(core * HALF, HALF), HALF), :]
    flat_out[...] = (own_half + flat_half[...]).astype(bf16)

    own_copy.wait()
    pltpu.make_async_copy(ids_send.at[pl.ds(0, 127)], ids_recv.at[pl.ds(0, 127)], ids_ssem).wait()
    pltpu.make_async_copy(send_main.at[pl.ds(0, 127)], recv_main.at[pl.ds(0, 127)], g_ssem).wait()
    pltpu.make_async_copy(send_extra.at[pl.ds(0, 127)], recv_extra.at[pl.ds(0, 127)], g_esem).wait()
    pltpu.make_async_copy(send_main.at[pl.ds(1, 127)], gmain_out.at[pl.ds(1, 127)], gm_rsem).wait()
    pltpu.make_async_copy(send_extra.at[pl.ds(0, 127)], gextra_out.at[pl.ds(0, 127)], ge_rsem).wait()


WAYS = 4
BATCH = 32
CHUNK = 512


def scatter_kernel(ids_ref, gmain_hbm, gextra_ref, table_hbm, new_hbm, change_hbm,
                   sums, stage, gmain, table, change, gmain_sem, table_sem, new_sem, change_sem):
    def gmain_copy(q):
        at = pl.ds(q * SERVE, SERVE)
        return pltpu.make_async_copy(gmain_hbm.at[at], gmain.at[at], gmain_sem.at[q])

    for q in range(N_DEV // SERVE):
        gmain_copy(q).start()
    table_copy = pltpu.make_async_copy(table_hbm, table, table_sem)
    table_copy.start()
    sums[...] = jnp.zeros_like(sums)

    def convert(s, c):
        stage[s, 0:MAIN, :] = gmain[s].astype(f32)
        stage[s, MAIN : MAIN + 8, :] = jnp.where(iota((8, 128), 0) == 0, gextra_ref[s], 0.0)
        stage[s, MAIN + 8 : 128, :] = jnp.zeros((24, 128), f32)
        return c

    def source(s, c):
        count = ids_ref[s, 0, 127]

        def batch(b, c):
            first = pl.multiple_of(b * BATCH, BATCH)
            for h in range(0, BATCH, WAYS):
                rows = [ids_ref[s, 0, first + h + i] for i in range(WAYS)]
                total = [
                    sums[i, pl.ds(rows[i], 1), :] + stage[s, pl.ds(first + h + i, 1), :] for i in range(WAYS)
                ]
                for i in range(WAYS):
                    sums[i, pl.ds(rows[i], 1), :] = total[i]
            return c

        lax.fori_loop(0, (count + BATCH - 1) // BATCH, batch, 0)
        return c

    def chunk(q, c):
        gmain_copy(q).wait()
        lax.fori_loop(0, SERVE, lambda i, c: convert(q * SERVE + i, c), 0, unroll=4)
        lax.fori_loop(q * SERVE, q * SERVE + SERVE, source, 0)
        return c

    lax.fori_loop(0, N_DEV // SERVE, chunk, 0)
    table_copy.wait()

    def finish(b, c):
        start = pl.multiple_of(b * CHUNK, CHUNK)
        for r in range(0, CHUNK, 64):
            at = pl.ds(pl.multiple_of(start + r, 64), 64)
            total = sums[0, at, :]
            for i in range(1, WAYS):
                total = total + sums[i, at, :]
            total = -embed_rate * total
            table[at, :] = table[at, :] + total
            change[at, :] = total.astype(bf16)
        at = pl.ds(start, CHUNK)
        pltpu.make_async_copy(table.at[at], new_hbm.at[at], new_sem).start()
        pltpu.make_async_copy(change.at[at], change_hbm.at[at], change_sem).start()
        return c

    lax.fori_loop(0, ROWS_DEV // CHUNK, finish, 0)
    pltpu.make_async_copy(table, new_hbm, new_sem).wait()
    pltpu.make_async_copy(change, change_hbm, change_sem).wait()


def member_peer(k, sign):
    x, y = lax.axis_index("member") // 4, lax.axis_index("member") % 4
    kx = k % 4
    ky = (k // 4 + kx) % 4
    if sign < 0:
        kx, ky = (4 - kx) % 4, (4 - ky) % 4
    return ((x + kx) % 4) * 4 + (y + ky) % 4


CUT = (5, 9, 13)


def parity_kernel(
    change_ref, parity_ref, flat_ref,
    new_ref, all_z,
    pieces, part_z, sum_z, part_xy, sum_xy, all_xy,
    ch_ssem, ch_rsem, rz_ssem, rz_rsem, rx_ssem, rx_rsem, ax_ssem, ax_rsem, az_ssem, az_rsem, ac_ssem, ac_rsem, own_sem,
):
    g, m = lax.axis_index("group"), lax.axis_index("member")
    barrier = pltpu.get_barrier_semaphore()
    for j in range(1, N_GROUP):
        pl.semaphore_signal(barrier, 1, device_id=((g + j) % N_GROUP, m), device_id_type=MESH)
    for k in range(1, N_MEMBER):
        pl.semaphore_signal(barrier, 1, device_id=(g, member_peer(k, 1)), device_id_type=MESH)
    pl.semaphore_wait(barrier, N_GROUP - 1 + N_MEMBER - 1)

    def remote(src, dst, ssem, rsem, to):
        return pltpu.make_async_remote_copy(src, dst, ssem, rsem, device_id=to, device_id_type=MESH)

    rows = ROWS_DEV // N_MEMBER

    def change_copy(k):
        to = member_peer(k, 1)
        return remote(
            change_ref.at[pl.ds(pl.multiple_of(to * rows, rows), rows)], pieces.at[k], ch_ssem.at[k], ch_rsem.at[k],
            (g, to),
        )

    z, core = g // 2, g % 2

    def rz_copy(j):
        to = (z + j) % 4
        return remote(
            flat_ref.at[pl.ds(pl.multiple_of(to * PIECE, PIECE), PIECE)], part_z.at[j], rz_ssem.at[j], rz_rsem.at[j],
            (to * 2 + core, m),
        )

    def rx_copy(k):
        to = member_peer(k, 1)
        return remote(
            sum_z.at[pl.ds(pl.multiple_of(to * SMALL, SMALL), SMALL)], part_xy.at[k], rx_ssem.at[k], rx_rsem.at[k],
            (g, to),
        )

    def ax_copy(k):
        return remote(sum_xy, all_xy.at[m], ax_ssem.at[k], ax_rsem.at[k], (g, member_peer(k, 1)))

    place = core * 4 + z

    def az_copy(j):
        return remote(
            all_z.at[place], all_z.at[place], az_ssem.at[j], az_rsem.at[j], ((z + j) % 4 * 2 + core, m)
        )

    def across_copy(j):
        slot = core * 4 + (z + 4 - j) % 4
        return remote(
            all_z.at[slot], all_z.at[slot], ac_ssem.at[j], ac_rsem.at[j], (z * 2 + 1 - core, m)
        )

    own_copy = pltpu.make_async_copy(
        change_ref.at[pl.ds(pl.multiple_of(m * rows, rows), rows)], pieces.at[0], own_sem
    )
    own_copy.start()
    for j in range(1, 4):
        rz_copy(j).start()
    for k in range(1, CUT[0]):
        change_copy(k).start()
    total = flat_ref[pl.ds(pl.multiple_of(z * PIECE, PIECE), PIECE), :].astype(f32)
    for j in range(1, 4):
        rz_copy(j).wait()
        total = total + part_z[j].astype(f32)
    sum_z[...] = total
    for k in range(1, N_MEMBER):
        rx_copy(k).start()
    for k in range(CUT[0], CUT[1]):
        change_copy(k).start()
    total = sum_z[pl.ds(pl.multiple_of(m * SMALL, SMALL), SMALL), :]
    for k in range(1, N_MEMBER):
        rx_copy(k).wait()
        total = total + part_xy[k]
    sum_xy[...] = total
    for k in range(1, N_MEMBER):
        ax_copy(k).start()
    for k in range(CUT[1], CUT[2]):
        change_copy(k).start()
    all_xy[m] = total
    for k in range(1, N_MEMBER):
        ax_copy(k).wait()
    all_z[place] = all_xy[...].reshape(PIECE, E).astype(bf16)
    for j in range(1, 4):
        az_copy(j).start()
    across_copy(0).start()
    for k in range(CUT[2], N_MEMBER):
        change_copy(k).start()

    def weights(k):
        source = member_peer(k, -1).astype(f32) / N_MEMBER
        one = jnp.ones((1, 128), f32)
        return 1.0 / (one + source), 1.0 / (one * 2.0 + source)

    for j in range(1, 4):
        az_copy(j).wait_recv()
        across_copy(j).start()

    def add(k, part_of, base_of):
        first, second = weights(k)

        def step(b, c):
            at = pl.ds(pl.multiple_of(b * 64, 64), 64)
            part = part_of(b).astype(f32)
            new_ref[at, 0:128] = base_of[at, 0:128] + first * part
            new_ref[at, 128:256] = base_of[at, 128:256] + second * part
            return c

        lax.fori_loop(0, rows // 64, step, 0)

    own_copy.wait()
    add(0, lambda b: pieces[0, pl.ds(pl.multiple_of(b * 64, 64), 64), :], parity_ref)
    for k in range(1, N_MEMBER):
        change_copy(k).wait()
        add(k, lambda b: pieces[k, pl.ds(pl.multiple_of(b * 64, 64), 64), :], new_ref)

    for j in range(4):
        if j > 0:
            az_copy(j).wait_send()
        across_copy(j).wait()


def unpack_kernel(
    parity_hbm, all_z_hbm, new_hbm, g0_ref, g1_ref, g2_ref, gt0_ref, gt1_ref,
    all_z, parity, parity_sem, all_z_sem, new_sem,
):
    parity_copy = pltpu.make_async_copy(parity_hbm, parity, parity_sem)
    parity_copy.start()
    all_z_copy = pltpu.make_async_copy(all_z_hbm, all_z, all_z_sem)
    all_z_copy.start()
    parity_copy.wait()
    new_copy = pltpu.make_async_copy(parity, new_hbm, new_sem)
    new_copy.start()
    all_z_copy.wait()
    for c in range(8):
        gt0_ref[:, 128 * c : 128 * (c + 1)] = piece_rows(all_z, OFF_TOP0 + c * TOP0_ROWS, TOP0_ROWS)[0:TOPIN]
    for c in range(2):
        g1_ref[:, 128 * c : 128 * (c + 1)] = piece_rows(all_z, OFF_BOT1 + c * BOT1, BOT1)
    g2_ref[...] = piece_rows(all_z, OFF_BOT2, BOT2)
    for c in range(4):
        g0_ref[:, 128 * c : 128 * (c + 1)] = piece_rows(all_z, OFF_BOT0 + c * 16, 16)[0:DENSE]
    top1 = piece_rows(all_z, OFF_TOP1, 16)
    for c in range(8):
        gt1_ref[:, 128 * c : 128 * (c + 1)] = top1[c : c + 1, :]
    new_copy.wait()


def piece_rows(ref, start, count):
    out = []
    while count > 0:
        p, at = start // PIECE, start % PIECE
        n = min(count, PIECE - at)
        out.append(ref[p, at : at + n, :].astype(f32))
        start, count = start + n, count - n
    return out[0] if len(out) == 1 else jnp.concatenate(out, axis=0)


def body(
    dense_in, lookup_owner, lookup_row, bag_length, logit_grad, table, parity,
    w_bottom0, w_bottom1, w_bottom2, w_top0, w_top1,
):
    owner = lookup_owner.transpose(1, 2, 0).reshape(NT * HOT, 128)
    row = lookup_row.transpose(1, 2, 0).reshape(NT * HOT, 128)
    vmem = pl.BlockSpec(memory_space=VM)
    anyw = pl.BlockSpec(memory_space=pl.ANY)
    smem = pl.BlockSpec(memory_space=pltpu.SMEM)
    dma = pltpu.SemaphoreType.DMA
    sds = jax.ShapeDtypeStruct
    ids, gmain, gextra, flat = pl.pallas_call(
        exchange_kernel,
        out_shape=(
            sds((N_DEV, 1, 128), i32),
            sds((N_DEV, MAIN, E), bf16),
            sds((N_DEV, 1, E), f32),
            sds((HALF, E), bf16),
        ),
        in_specs=[vmem] * 5 + [anyw] * 5 + [vmem],
        out_specs=(vmem, anyw, vmem, vmem),
        scratch_shapes=[
            VM((ROWS_DEV, E), f32),
            VM((N_DEV, 1, 128), i32),
            VM((N_DEV, 1, 128), i32),
            pltpu.SMEM((N_DEV, 1, 128), i32),
            VM((MAIN, E), f32),
            VM((N_DEV, MAIN, E), bf16),
            VM((N_DEV, 1, E), f32),
            VM((N_DEV, MAIN, E), bf16),
            VM((N_DEV, 1, E), f32),
            VM((32, 128, 256), bf16),
            VM((32, 384, 256), bf16),
            VM((N_DEV, MAIN, 128), i32),
            VM((128, 128), i32),
            VM((GROUP * MAIN, BAGS), bf16),
            VM((N_DEV, BAGS), bf16),
            VM((E, BAGS), f32),
            VM((BAGS, E), bf16),
            VM((256, TOPH), f32),
            VM((256, 128), f32),
            VM((TOPH, 128), f32),
            VM((TOPH, 128), f32),
            dma, dma((N_DEV // SERVE,)), dma, dma((N_DEV // SERVE,)), dma, dma,
            dma((N_DEV // GROUP,)), dma((N_DEV // GROUP,)),
            dma, dma, dma, dma,
            VM((FLAT, E), f32),
            VM((HALF, E), f32),
            dma, dma, dma,
            VM((DENSE, BOT1), f32),
            VM((BOT1, BOT2), f32),
            VM((BOT2, E), f32),
            VM((TOPIN, TOPH), f32),
            dma((4,)),
        ],
        compiler_params=pltpu.CompilerParams(
            collective_id=0, has_side_effects=True, vmem_limit_bytes=56 << 20
        ),
    )(
        owner, row, bag_length.T, dense_in.T, logit_grad.reshape(1, 128), table,
        w_bottom0, w_bottom1, w_bottom2, w_top0, w_top1.reshape(1, TOPH),
    )
    new_table, change = pl.pallas_call(
        scatter_kernel,
        out_shape=(sds((ROWS_DEV, E), f32), sds((ROWS_DEV, E), bf16)),
        in_specs=[smem, anyw, vmem, anyw],
        out_specs=(anyw, anyw),
        scratch_shapes=[
            VM((WAYS, ROWS_DEV, E), f32),
            VM((N_DEV, 128, E), f32),
            VM((N_DEV, MAIN, E), bf16),
            VM((ROWS_DEV, E), f32),
            VM((ROWS_DEV, E), bf16),
            dma((N_DEV // SERVE,)), dma, dma, dma,
        ],
        compiler_params=pltpu.CompilerParams(vmem_limit_bytes=56 << 20),
    )(ids, gmain, gextra, table)
    parity_sum, all_z = pl.pallas_call(
        parity_kernel,
        out_shape=(sds(parity.shape, f32), sds((N_GROUP, PIECE, E), bf16)),
        in_specs=[anyw, vmem, vmem],
        out_specs=(vmem, vmem),
        scratch_shapes=[
            VM((N_MEMBER, ROWS_DEV // N_MEMBER, E), bf16),
            VM((4, PIECE, E), bf16),
            VM((PIECE, E), f32),
            VM((N_MEMBER, SMALL, E), f32),
            VM((SMALL, E), f32),
            VM((N_MEMBER, SMALL, E), f32),
            dma((N_MEMBER,)), dma((N_MEMBER,)), dma((4,)), dma((4,)),
            dma((N_MEMBER,)), dma((N_MEMBER,)), dma((N_MEMBER,)), dma((N_MEMBER,)),
            dma((4,)), dma((4,)), dma((4,)), dma((4,)), dma,
        ],
        compiler_params=pltpu.CompilerParams(
            collective_id=1, has_side_effects=True, vmem_limit_bytes=60 << 20
        ),
    )(change, parity, flat)
    new_parity, g0, g1, g2, gt0, gt1 = pl.pallas_call(
        unpack_kernel,
        out_shape=(
            sds(parity.shape, f32),
            sds((DENSE, BOT1), f32),
            sds((BOT1, BOT2), f32),
            sds((BOT2, E), f32),
            sds((TOPIN, TOPH), f32),
            sds((1, TOPH), f32),
        ),
        in_specs=[anyw] * 2,
        out_specs=(anyw,) + (vmem,) * 5,
        scratch_shapes=[VM((N_GROUP, PIECE, E), bf16), VM(parity.shape, f32), dma, dma, dma],
        compiler_params=pltpu.CompilerParams(vmem_limit_bytes=60 << 20),
    )(parity_sum, all_z)
    return new_table, new_parity, g0, g1, g2, gt0, gt1.reshape(TOPH)


def solution(mesh):
    rows = P(("group", "member"), None)
    cube = P(("group", "member"), None, None)
    in_specs = (rows, cube, cube, rows, P(("group", "member")), rows, rows, P(), P(), P(), P(), P())
    out_specs = (rows, rows, P(), P(), P(), P(), P())
    return jax.shard_map(body, mesh=mesh, in_specs=in_specs, out_specs=out_specs, check_vma=False)
```
